256 devices in a mesh: sample: 4 (over y), space: 64 (over z, x, core).
Axes of the slice: x: 4, y: 4, z: 8, core: 2. Of those that a mesh axis runs over, the one named last changes fastest.
Arguments:
- field: bfloat16 [4, 256, 512, 128], P('sample', 'space'), may hold values from -6 to 6
- send_rows: int32 [64, 5, 512], P('space'), may hold values from 0 to 2047, as said below
- send_count: int32 [64, 5], P('space'), may hold values from 0 to 512, as said below
- dep_slot: int32 [4, 256, 512], P(None, 'space'), may hold values from 0 to 2559, as said below
- dep_weight: float32 [4, 256, 512], P(None, 'space'), may hold values from 0 to 1, as said below
- helm_coef: float32 [128], replicated, may hold values from 0.5 to 4
- w_first: bfloat16 [128, 256], replicated, may hold values from -0.5 to 0.5
- b_first: float32 [256], replicated, may hold values from -3 to 3
- w_second: bfloat16 [256, 256], replicated, may hold values from -0.375 to 0.375
- b_second: float32 [256], replicated, may hold values from -3 to 3
- w_third: bfloat16 [256, 128], replicated, may hold values from -0.375 to 0.375
- cotangent: bfloat16 [4, 256, 512, 128], P('sample', 'space'), may hold values from -6 to 6
Outputs:
- next_state: bfloat16 [4, 256, 512, 128], P('sample', 'space')
- field_grad: float32 [4, 256, 512, 128], P('sample', 'space')
- grad_first: float32 [128, 256], replicated
- grad_bfirst: float32 [256], replicated
- grad_second: float32 [256, 256], replicated
- grad_bsecond: float32 [256], replicated
- grad_third: float32 [256, 128], replicated
The draws below stay inside these ranges and needn't reach their ends.
Inputs may be any that keep to these rules, and one draw needn't show every extreme that they name: `send_rows`: slots come in quads 4 q to 4 q + 3, the corners (row, lon), (row, lon + 1), (row + 1, lon), (row + 1, lon + 1) of one grid box of band s, longitude periodic. `send_count`: A multiple of 4; 0 where the target band s + e - 2 lies off the grid or farther from s than its reach (1 band, or 2 for the polar and jet bands); 512 for every live pair whose target is among the first or last max(1, 64 // 8) bands. `dep_slot`: tap k of a cell of band t reads slot e * 512 + 4 q + k of one live quad (4 q + 4 <= send_count[t - e + 2, e]), the same quad for all four taps; |e - 2| is at most the reach of band t. `dep_weight`: the four weights of a cell are bilinear and sum to 1.
All inputs are finite; a program needn't handle non-finite values.
Results may differ from the reference program's by a relative error of at most 0.017.
Values may be sent and summed in bfloat16 or wider, within the bound.
No kernel may reach another device: no remote copies, remote signals or barrier semaphores. Data moves between devices by JAX's collectives and lax.ppermute only.
A program may use at most 64 MiB of HBM per device.

```python
import math
import jax
import jax.numpy as jnp
from jax import lax

CH = 128
HID = 256
LON = 512
LATB = 4
CAP = 512
RMAX = 2
SWEEPS = 2
LAT = 256
BATCH = 4
N_SPACE = 64


def band_table():
    band = jnp.arange(N_SPACE)
    polar = max(1, N_SPACE // 8)
    edge = (band < polar) | (band >= N_SPACE - polar)
    wide = edge | (band == N_SPACE // 4) | (band == 3 * N_SPACE // 4)
    return (jnp.where(wide, RMAX, 1), edge)


def shared_counts(key):
    base = jax.random.fold_in(key, 7)
    span_bands, edge = band_table()
    offsets = jnp.arange(2 * RMAX + 1)
    target = jnp.arange(N_SPACE)[:, None] + offsets[None, :] - RMAX
    inside = (target >= 0) & (target < N_SPACE)
    clipped = jnp.clip(target, 0, N_SPACE - 1)
    near = jnp.abs(offsets - RMAX)[None, :] <= span_bands[clipped]
    quads = jax.random.randint(base, (N_SPACE, 2 * RMAX + 1), max(1, CAP // 8), CAP // 4 + 1)
    quads = jnp.where(edge[clipped], CAP // 4, quads)
    return jnp.where(inside & near, 4 * quads, 0).astype(jnp.int32)


def draw_send_count(key, part):
    counts = shared_counts(key)
    return counts


def draw_send_rows(key, part):
    counts = shared_counts(key)
    key = jax.random.fold_in(key, 3)
    row_key, lon_key = jax.random.split(key)
    quad_shape = (N_SPACE, 2 * RMAX + 1, CAP // 4)
    nquads = jnp.maximum(counts // 4, 1)[:, :, None]
    quad = jnp.arange(CAP // 4)[None, None, :]
    start = quad * LON // nquads
    spread = jnp.maximum(LON // nquads, 1)
    row = jax.random.randint(row_key, quad_shape, 0, LATB - 1)
    jitter = jax.random.randint(lon_key, quad_shape, 0, spread)
    lon = (start + jitter) % LON
    corner = jnp.arange(4)
    cells = (row[..., None] + corner // 2) * LON + (lon[..., None] + corner % 2) % LON
    return cells.reshape(N_SPACE, 2 * RMAX + 1, CAP).astype(jnp.int32)


def draw_dep_slot(key, part):
    counts = shared_counts(key)
    key = jax.random.fold_in(key, 5)
    step_key, wind_key = jax.random.split(key)
    span_bands, edge = band_table()
    band = jnp.arange(LAT) // LATB
    limit = span_bands[band][:, None]
    step = jax.random.randint(step_key, (LAT, LON), 0, 2 * limit + 1) - limit
    target = band[:, None]
    source = target + step
    source = jnp.where((source < 0) | (source >= N_SPACE), target - step, source)
    offset = target - source + RMAX
    nquads = counts[source, offset] // 4
    wind = jax.random.randint(wind_key, (N_SPACE,), -3, 4)[band][:, None]
    quad = (jnp.arange(LON)[None, :] - wind) % LON * nquads // LON
    base = offset * CAP + 4 * quad
    return (base[None] + jnp.arange(4)[:, None, None]).astype(jnp.int32)


def draw_dep_weight(key, part):
    key = jax.random.fold_in(key, 11)
    lat_key, lon_key = jax.random.split(key)
    low, high = (0.02, 0.98)
    along = jax.random.uniform(lat_key, (LAT, LON), jnp.float32, low, high)
    across = jax.random.uniform(lon_key, (LAT, LON), jnp.float32, low, high)
    weights = jnp.stack([(1.0 - along) * (1.0 - across), (1.0 - along) * across, along * (1.0 - across), along * across])
    return weights.astype(jnp.float32)


def shard_levels(stream_key, shape, cuts, least, largest):
    def one(axis_at, shards_of):
        draws = jax.random.uniform(jax.random.fold_in(jax.random.fold_in(stream_key, 6), axis_at), (shards_of,), jnp.float32, least / len(cuts), largest / len(cuts))
        return jnp.repeat(jnp.exp(draws), shape[axis_at] // shards_of).reshape((-1,) + (1,) * (len(shape) - axis_at - 1))

    loudness = one(*cuts[0])
    for cut in cuts[1:]:
        loudness = loudness * one(*cut)
    return loudness


def noise(stream_key, extent, scale, bound, shards=(), held_as=jnp.bfloat16):
    result = scale * jax.random.normal(stream_key, extent, jnp.float32)
    if shards:
        result = result * shard_levels(stream_key, extent, shards, -0.22, 0.18)
    return jnp.clip(result, -bound, bound).astype(held_as)


def setup_inputs(seed: int = 0) -> dict:
    keys = jax.random.split(jax.random.key(seed), 13)
    field = noise(keys[0], (BATCH, LAT, LON, CH), 1.0, 6.0, ((0, 4), (1, 64)))
    send_rows = draw_send_rows(jax.random.fold_in(keys[12], 71), 0)
    send_count = draw_send_count(jax.random.fold_in(keys[12], 71), 0)
    dep_slot = draw_dep_slot(jax.random.fold_in(keys[12], 71), 0)
    dep_weight = draw_dep_weight(jax.random.fold_in(keys[12], 71), 0)
    helm_coef = jnp.clip(jnp.exp(jax.random.uniform(keys[5], (CH,), jnp.float32, math.log(0.5), math.log(4.0))), 0.5, 4.0)
    w_first = noise(keys[6], (CH, HID), CH ** -0.5, 0.5)
    b_first = noise(keys[7], (HID,), 0.5, 3.0, (), jnp.float32)
    w_second = noise(keys[8], (HID, HID), HID ** -0.5, 0.375)
    b_second = noise(keys[9], (HID,), 0.5, 3.0, (), jnp.float32)
    w_third = noise(keys[10], (HID, CH), HID ** -0.5, 0.375)
    cotangent = noise(keys[11], (BATCH, LAT, LON, CH), 1.0, 6.0, ((0, 4), (1, 64)))
    return {"field": field, "send_rows": send_rows, "send_count": send_count, "dep_slot": dep_slot, "dep_weight": dep_weight, "helm_coef": helm_coef, "w_first": w_first, "b_first": b_first, "w_second": w_second, "b_second": b_second, "w_third": w_third, "cotangent": cotangent}


def neighbours(state):
    padded = jnp.pad(state, ((1, 1), (0, 0), (0, 0)))
    return padded[:-2] + padded[2:] + jnp.roll(state, 1, axis=1) + jnp.roll(state, -1, axis=1)

def helmholtz(departure, helm_coef):
    smooth = departure
    denom = 1.0 + 4.0 * helm_coef
    for sweep in range(SWEEPS):
        smooth = (departure + helm_coef * neighbours(smooth)) / denom
    return smooth

def departures(sample_field, send_rows, send_count, dep_slot, dep_weight):
    tiles = sample_field.reshape(N_SPACE, LATB * LON, CH)
    offsets = jnp.arange(2 * RMAX + 1, dtype=jnp.int32)
    slot_iota = jnp.arange(CAP, dtype=jnp.int32)

    def one_band(target):
        source = target - offsets + RMAX
        inside = (source >= 0) & (source < N_SPACE)
        clipped = jnp.clip(source, 0, N_SPACE - 1).astype(jnp.int32)
        rows_here = send_rows[clipped, offsets]
        picked = tiles[clipped[:, None], rows_here]
        counts = jnp.where(inside, send_count[clipped, offsets], 0)
        live = slot_iota[None, :] < counts[:, None]
        received = jnp.where(live[:, :, None], picked, jnp.zeros((), picked.dtype)).reshape(-1, CH)
        slots = lax.dynamic_slice_in_dim(dep_slot, (target * LATB).astype(jnp.int32), LATB, 1)
        weights = lax.dynamic_slice_in_dim(dep_weight, (target * LATB).astype(jnp.int32), LATB, 1)
        taps = received[slots]
        return lax.optimization_barrier(jnp.sum(weights[..., None] * taps, axis=0))
    bands = lax.map(one_band, jnp.arange(N_SPACE, dtype=jnp.int32))
    return bands.reshape(LAT, LON, CH)

def reference(field, send_rows, send_count, dep_slot, dep_weight, helm_coef, w_first, b_first, w_second, b_second, w_third, cotangent):

    def per_sample(totals, inputs):
        sample_field, sample_cot = inputs

        def forward(field_value):
            return helmholtz(departures(field_value, send_rows, send_count, dep_slot, dep_weight), helm_coef)
        smooth, pullback = jax.vjp(forward, sample_field.astype(jnp.float32))
        smoothed = smooth.astype(jnp.bfloat16).reshape(-1, CH)
        pre_first = jnp.dot(smoothed, w_first, preferred_element_type=jnp.float32) + b_first
        act_value, first_back = jax.vjp(jax.nn.gelu, pre_first)
        act_first = act_value.astype(jnp.bfloat16)
        pre_second = jnp.dot(act_first, w_second, preferred_element_type=jnp.float32) + b_second
        act_value, second_back = jax.vjp(jax.nn.gelu, pre_second)
        act_second = act_value.astype(jnp.bfloat16)
        next_rows = smoothed.astype(jnp.float32) + jnp.dot(act_second, w_third, preferred_element_type=jnp.float32)
        cot_rows = sample_cot.reshape(-1, CH)
        grad_third = jnp.dot(act_second.T, cot_rows, preferred_element_type=jnp.float32)
        gact_second = jnp.dot(cot_rows, w_third.T, preferred_element_type=jnp.float32)
        gpre_second = second_back(gact_second)[0].astype(jnp.bfloat16)
        grad_second = jnp.dot(act_first.T, gpre_second, preferred_element_type=jnp.float32)
        grad_bsecond = lax.optimization_barrier(jnp.sum(gpre_second.astype(jnp.float32), axis=0))
        gact_first = jnp.dot(gpre_second, w_second.T, preferred_element_type=jnp.float32)
        gpre_first = first_back(gact_first)[0].astype(jnp.bfloat16)
        grad_first = jnp.dot(smoothed.T, gpre_first, preferred_element_type=jnp.float32)
        grad_bfirst = lax.optimization_barrier(jnp.sum(gpre_first.astype(jnp.float32), axis=0))
        gsmooth = cot_rows.astype(jnp.float32) + jnp.dot(gpre_first, w_first.T, preferred_element_type=jnp.float32)
        field_grad = pullback(gsmooth.reshape(LAT, LON, CH))[0]
        totals = (totals[0] + grad_first, totals[1] + grad_bfirst, totals[2] + grad_second, totals[3] + grad_bsecond, totals[4] + grad_third)
        return (totals, (next_rows.astype(jnp.bfloat16).reshape(LAT, LON, CH), field_grad))
    zeros = (jnp.zeros((CH, HID), jnp.float32), jnp.zeros((HID,), jnp.float32), jnp.zeros((HID, HID), jnp.float32), jnp.zeros((HID,), jnp.float32), jnp.zeros((HID, CH), jnp.float32))
    totals, (next_state, field_grad) = lax.scan(per_sample, zeros, (field, cotangent))
    return (next_state, field_grad, totals[0], totals[1], totals[2], totals[3], totals[4])
```

```python
import functools
import math

import jax
import jax.numpy as jnp
from jax import lax
from jax.experimental import pallas as pl
from jax.experimental.pallas import tpu as pltpu
from jax.sharding import Mesh
from jax.sharding import PartitionSpec as P

F32 = jnp.float32
BF16 = jnp.bfloat16
SPACE = ("z", "x", "core")
GELU_SCALE = math.sqrt(2.0 / math.pi)
GELU_CUBE = 0.044715
PART_ROWS = 40

VMEM = pl.BlockSpec(memory_space=pltpu.VMEM)
SMEM = pl.BlockSpec(memory_space=pltpu.SMEM)


def dot(left, right, left_dim=1, right_dim=0):
    return lax.dot_general(
        left,
        right,
        (((left_dim,), (right_dim,)), ((), ())),
        preferred_element_type=F32,
    )


def call(kernel, outs, ins, scratch=(), flops=0, name=None):
    nbytes = sum(math.prod(o.shape) * o.dtype.itemsize for o in outs)
    return pl.pallas_call(
        kernel,
        out_shape=outs,
        in_specs=ins,
        out_specs=[VMEM] * len(outs),
        scratch_shapes=list(scratch),
        compiler_params=pltpu.CompilerParams(vmem_limit_bytes=40 * 1024 * 1024),
        cost_estimate=pl.CostEstimate(
            flops=flops, bytes_accessed=2 * nbytes, transcendentals=0
        ),
        name=name,
    )


def quad_boxes(rows_ref, count_ref, offsets, slots):
    quads = slots // 4
    rows = rows_ref[...]
    pick = (
        lax.broadcasted_iota(jnp.int32, (slots, quads), 0)
        == 4 * lax.broadcasted_iota(jnp.int32, (slots, quads), 1)
    ).astype(F32).astype(BF16)
    high = (rows >> 3).astype(F32).astype(BF16)
    low = (rows & 7).astype(F32).astype(BF16)
    cells = (dot(high, pick) * 8.0 + dot(low, pick)).astype(jnp.int32)
    offset_at = lax.broadcasted_iota(jnp.int32, cells.shape, 0)
    live = jnp.zeros(cells.shape, jnp.int32)
    for offset in range(offsets):
        live = jnp.where(offset_at == offset, count_ref[0, offset], live)
    slot_at = 4 * lax.broadcasted_iota(jnp.int32, cells.shape, 1)
    return jnp.where(slot_at < live, cells, -1)


def pack_kernel(offsets, field_ref, rows_ref, count_ref, *refs):
    outs, (pair, select) = refs[:offsets], refs[offsets:]
    band_rows, lon, ch = field_ref.shape
    slots = rows_ref.shape[1]
    quads = slots // 4
    boxes = (band_rows - 1) * lon
    cells = quad_boxes(rows_ref, count_ref, offsets, slots)
    columns = cells.astype(F32).T.astype(jnp.int32)
    box_at = lax.broadcasted_iota(jnp.int32, (quads, boxes), 1)
    for offset in range(offsets):
        select[offset * quads : (offset + 1) * quads] = (
            (box_at == columns[:, offset : offset + 1]).astype(F32).astype(BF16)
        )
    for row in range(band_rows):
        line = field_ref[row]
        pair[row * lon : (row + 1) * lon, :ch] = line
        pair[row * lon : (row + 1) * lon, ch:] = pltpu.roll(
            line.astype(F32), lon - 1, 0
        ).astype(BF16)
    for part in range(2):
        picked = dot(select[...], pair[part * lon : part * lon + boxes]).astype(BF16)
        for offset in range(offsets):
            outs[offset][:, part * 2 * ch : (part + 1) * 2 * ch] = picked[
                offset * quads : (offset + 1) * quads
            ]


def tap_columns(weight_ref, stack):
    taps, band_rows, _ = weight_ref.shape
    for tap in range(taps):
        stack[tap * band_rows : (tap + 1) * band_rows] = weight_ref[tap]
    return stack[...].T


def interp_kernel(offsets, *refs):
    blocks = refs[:offsets]
    slot_ref, weight_ref, dep_ref, up_ref, down_ref, table, stack, slot_stack = refs[offsets:]
    taps, band_rows, lon = weight_ref.shape
    quads, wide = blocks[0].shape
    ch = wide // taps
    weights = tap_columns(weight_ref, stack)
    slot_stack[...] = jnp.zeros_like(slot_stack)
    slot_stack[:band_rows] = (slot_ref[0] >> 2).astype(F32)
    quad_columns = slot_stack[...].T.astype(jnp.int32)
    for offset in range(offsets):
        table[offset * quads : (offset + 1) * quads] = blocks[offset][...]
    quad_at = lax.broadcasted_iota(jnp.int32, (lon, offsets * quads), 1)
    for row in range(band_rows):
        hit = (quad_at == quad_columns[:, row : row + 1]).astype(F32).astype(BF16)
        tapped = dot(hit, table[...])
        line = jnp.zeros((lon, ch), F32)
        for tap in range(taps):
            at = tap * band_rows + row
            line = line + weights[:, at : at + 1] * tapped[:, tap * ch : (tap + 1) * ch]
        dep_ref[row] = line
        if row < 2:
            up_ref[row] = line.astype(BF16)
        if row >= band_rows - 2:
            down_ref[row - band_rows + 2] = line.astype(BF16)


def lon_sum(line):
    lon = line.shape[0]
    return pltpu.roll(line, 1, 0) + pltpu.roll(line, lon - 1, 0)


def gelu_parts(pre):
    square = pre * pre
    curve = jnp.tanh(pre * (GELU_SCALE + (GELU_SCALE * GELU_CUBE) * square))
    half = 0.5 + 0.5 * curve
    slope = half + (0.5 * pre) * (1.0 - curve * curve) * (
        GELU_SCALE + (3.0 * GELU_SCALE * GELU_CUBE) * square
    )
    return pre * half, slope


def mlp_kernel(
    dep_ref,
    before_ref,
    after_ref,
    cot_ref,
    place_ref,
    helm_ref,
    w1_ref,
    b1_ref,
    w2_ref,
    b2_ref,
    w3_ref,
    next_ref,
    scaled_ref,
    up_ref,
    down_ref,
    keep_ref,
    give_ref,
    once,
    smooth,
    g1,
    gb1,
    g2,
    gb2,
    g3,
):
    band_rows, lon, ch = dep_ref.shape
    helm = helm_ref[...]
    inverse = 1.0 / (1.0 + 4.0 * helm)

    def departure(row):
        if row < 0:
            return before_ref[row + 2].astype(F32)
        if row >= band_rows:
            return after_ref[row - band_rows].astype(F32)
        return dep_ref[row]

    first = jnp.where(place_ref[0] == 0, 0.0, 1.0)
    last = jnp.where(place_ref[0] == place_ref[1] - 1, 0.0, 1.0)
    ahead = departure(-2), departure(-1)
    if True:
        ahead = ahead[0] * first, ahead[1] * first
    behind = departure(band_rows) * last, departure(band_rows + 1) * last
    lines = {-2: ahead[0], -1: ahead[1], band_rows: behind[0], band_rows + 1: behind[1]}
    for row in range(-1, band_rows + 1):
        mid, above, below = (
            lines[r] if r in lines else departure(r) for r in (row, row - 1, row + 1)
        )
        value = (mid + helm * (above + below + lon_sum(mid))) * inverse
        if row < 0:
            value = value * first
        if row >= band_rows:
            value = value * last
        once[row + 1] = value
    for row in range(band_rows):
        value = (
            dep_ref[row] + helm * (once[row] + once[row + 2] + lon_sum(once[row + 1]))
        ) * inverse
        smooth[row] = value.astype(BF16)
    for total in (g1, gb1, g2, gb2, g3):
        total[...] = jnp.zeros_like(total)

    def one_row(row, carry):
        rows = smooth[row]
        cot = cot_ref[row]
        act, slope_first = gelu_parts(dot(rows, w1_ref[...]) + b1_ref[...])
        act_first = act.astype(BF16)
        act, slope_second = gelu_parts(dot(act_first, w2_ref[...]) + b2_ref[...])
        act_second = act.astype(BF16)
        next_ref[row] = (rows.astype(F32) + dot(act_second, w3_ref[...])).astype(BF16)
        g3[...] += dot(act_second, cot, 0, 0)
        gpre = dot(cot, w3_ref[...], 1, 1) * slope_second
        gpre_second = gpre.astype(BF16)
        gb2[...] += jnp.sum(gpre_second.astype(F32), axis=0, keepdims=True)
        g2[...] += dot(act_first, gpre_second, 0, 0)
        gpre = dot(gpre_second, w2_ref[...], 1, 1) * slope_first
        gpre_first = gpre.astype(BF16)
        gb1[...] += jnp.sum(gpre_first.astype(F32), axis=0, keepdims=True)
        g1[...] += dot(rows, gpre_first, 0, 0)
        gsmooth = cot.astype(F32) + dot(gpre_first, w1_ref[...], 1, 1)
        scaled_ref[row] = gsmooth * inverse
        return carry

    lax.fori_loop(0, band_rows, one_row, 0)
    for row in range(2):
        up_ref[row] = scaled_ref[row].astype(BF16)
        down_ref[row] = scaled_ref[band_rows - 2 + row].astype(BF16)
    half = keep_ref.shape[0]
    low = place_ref[2] == 0
    hid = g1.shape[1]

    def place(at, zero, one):
        rows = zero.shape[0]
        keep_ref[at : at + rows] = jnp.where(low, zero, one).astype(BF16)
        give_ref[at : at + rows] = jnp.where(low, one, zero).astype(BF16)

    place(0, g1[:, :ch], g2[:ch, :ch])
    place(ch, g1[:, ch:], g2[ch:, :ch])
    place(2 * ch, g3[:ch], g2[:ch, ch:])
    place(3 * ch, g3[ch:], g2[ch:, ch:])
    row_at = lax.broadcasted_iota(jnp.int32, (half - 4 * ch, ch), 0)

    def bias(ref):
        return jnp.where(
            row_at == 0, ref[:, :ch], jnp.where(row_at == 1, ref[:, ch:], 0.0)
        )

    place(4 * ch, bias(gb1), bias(gb2))


def adjoint_kernel(
    offsets,
    scaled_ref,
    before_ref,
    after_ref,
    place_ref,
    helm_ref,
    slot_ref,
    weight_ref,
    *refs,
):
    outs, (once, spread, hit, stack) = refs[:offsets], refs[offsets:]
    band_rows, lon, ch = scaled_ref.shape
    taps = weight_ref.shape[0]
    quads = outs[0].shape[0]
    helm = helm_ref[...]
    inverse = 1.0 / (1.0 + 4.0 * helm)
    first = jnp.where(place_ref[0] == 0, 0.0, 1.0)
    last = jnp.where(place_ref[0] == place_ref[1] - 1, 0.0, 1.0)
    weights = tap_columns(weight_ref, stack)
    quad_lanes = slot_ref[0] >> 2
    quad_at = lax.broadcasted_iota(jnp.int32, (offsets * quads, lon), 0)
    for row in range(band_rows):
        hit[:, row * lon : (row + 1) * lon] = (
            (quad_at == quad_lanes[row : row + 1]).astype(F32).astype(BF16)
        )

    def scaled(row):
        if row < 0:
            return before_ref[row + 2].astype(F32) * first
        if row >= band_rows:
            return after_ref[row - band_rows].astype(F32) * last
        return scaled_ref[row]

    for row in range(-1, band_rows + 1):
        value = (helm * inverse) * (scaled(row - 1) + scaled(row + 1) + lon_sum(scaled(row)))
        if row < 0:
            value = value * first
        if row >= band_rows:
            value = value * last
        once[row + 1] = value
    for row in range(band_rows):
        value = (
            scaled_ref[row]
            + once[row + 1]
            + helm * (once[row] + once[row + 2] + lon_sum(once[row + 1]))
        )
        for tap in range(taps):
            at = tap * band_rows + row
            spread[row * lon : (row + 1) * lon, tap * ch : (tap + 1) * ch] = (
                weights[:, at : at + 1] * value
            ).astype(BF16)
    slot_grads = dot(hit[...], spread[...]).astype(BF16)
    for offset in range(offsets):
        outs[offset][...] = slot_grads[offset * quads : (offset + 1) * quads]


def scatter_kernel(offsets, rows_ref, count_ref, *refs):
    blocks = refs[:offsets]
    out_ref, table, hit = refs[offsets:]
    band_rows, lon, ch = out_ref.shape
    slots = rows_ref.shape[1]
    quads = slots // 4
    boxes = (band_rows - 1) * lon
    cells = quad_boxes(rows_ref, count_ref, offsets, slots)
    box_at = lax.broadcasted_iota(jnp.int32, (boxes, quads), 0)
    for offset in range(offsets):
        table[offset * quads : (offset + 1) * quads] = blocks[offset][...]
        hit[:, offset * quads : (offset + 1) * quads] = (
            (box_at == cells[offset : offset + 1]).astype(F32).astype(BF16)
        )
    for row in range(band_rows):
        here = jnp.zeros((lon, ch), F32)
        right = jnp.zeros((lon, ch), F32)
        if row < band_rows - 1:
            both = dot(hit[row * lon : (row + 1) * lon], table[:, : 2 * ch])
            here = here + both[:, :ch]
            right = right + both[:, ch:]
        if row > 0:
            both = dot(hit[(row - 1) * lon : row * lon], table[:, 2 * ch :])
            here = here + both[:, :ch]
            right = right + both[:, ch:]
        out_ref[row] = here + pltpu.roll(right, 1, 0)


def add_kernel(left_ref, right_ref, out_ref):
    out_ref[...] = (left_ref[...].astype(F32) + right_ref[...].astype(F32)).astype(BF16)


def sum_kernel(copies, parts_ref, out_ref):
    total = parts_ref[0].astype(F32)
    for part in range(1, parts_ref.shape[0]):
        total = total + parts_ref[part].astype(F32)
    total = total.astype(BF16)
    for copy in range(copies):
        out_ref[copy] = total


def unpack_kernel(mine_ref, other_ref, place_ref, g1, gb1, g2, gb2, g3):
    ch, hid = g1.shape
    low = place_ref[2] == 0

    def halves(at, rows):
        mine = mine_ref[at : at + rows].astype(F32)
        other = other_ref[at : at + rows].astype(F32)
        return jnp.where(low, mine, other), jnp.where(low, other, mine)

    zero, one = halves(0, ch)
    g1[:, :ch], g2[:ch, :ch] = zero, one
    zero, one = halves(ch, ch)
    g1[:, ch:], g2[ch:, :ch] = zero, one
    zero, one = halves(2 * ch, ch)
    g3[:ch], g2[:ch, ch:] = zero, one
    zero, one = halves(3 * ch, ch)
    g3[ch:], g2[ch:, ch:] = zero, one
    zero, one = halves(4 * ch, 8)
    gb1[:, :ch], gb1[:, ch:] = zero[:1], zero[1:2]
    gb2[:, :ch], gb2[:, ch:] = one[:1], one[1:2]


def shifted(block, by, count):
    return lax.ppermute(block, SPACE, [(i, (i + by) % count) for i in range(count)])


def body(
    field,
    send_rows,
    send_count,
    dep_slot,
    dep_weight,
    helm_coef,
    w_first,
    b_first,
    w_second,
    b_second,
    w_third,
    cotangent,
):
    _, band_rows, lon, ch = field.shape
    hid = w_first.shape[1]
    offsets, slots = send_rows.shape[1:]
    taps = dep_slot.shape[0]
    reach = (offsets - 1) // 2
    quads = slots // 4
    bands = lax.axis_size(SPACE)
    shape = jax.ShapeDtypeStruct
    core = lax.axis_index("core").astype(jnp.int32)
    place = jnp.stack(
        [lax.axis_index(SPACE).astype(jnp.int32), jnp.int32(bands), core]
    )
    rows8 = jnp.pad(send_rows[0], ((0, 8 - offsets), (0, 0)))
    helm = helm_coef.reshape(1, ch)
    block = shape((quads, taps * ch), BF16)
    edge = shape((2, lon, ch), BF16)

    packed = call(
        functools.partial(pack_kernel, offsets),
        [block] * offsets,
        [VMEM, VMEM, SMEM],
        [
            pltpu.VMEM((band_rows * lon, 2 * ch), BF16),
            pltpu.VMEM((offsets * quads, (band_rows - 1) * lon), BF16),
        ],
        name="pack",
    )(field[0], rows8, send_count)
    received = [
        packed[e] if e == reach else shifted(packed[e], e - reach, bands)
        for e in range(offsets)
    ]
    departure, up, down = call(
        functools.partial(interp_kernel, offsets),
        [shape((band_rows, lon, ch), F32), edge, edge],
        [VMEM] * (offsets + 2),
        [
            pltpu.VMEM((offsets * quads, taps * ch), BF16),
            pltpu.VMEM((taps * band_rows, lon), F32),
            pltpu.VMEM((8, lon), F32),
        ],
        name="interp",
    )(*received, dep_slot, dep_weight)
    before = shifted(down, 1, bands)
    after = shifted(up, -1, bands)
    half = shape((16 * PART_ROWS, ch), BF16)
    next_state, scaled, up, down, keep, give = call(
        mlp_kernel,
        [
            shape((band_rows, lon, ch), BF16),
            shape((band_rows, lon, ch), F32),
            edge,
            edge,
            half,
            half,
        ],
        [VMEM] * 4 + [SMEM] + [VMEM] * 6,
        [
            pltpu.VMEM((band_rows + 2, lon, ch), F32),
            pltpu.VMEM((band_rows, lon, ch), BF16),
            pltpu.VMEM((ch, hid), F32),
            pltpu.VMEM((1, hid), F32),
            pltpu.VMEM((hid, hid), F32),
            pltpu.VMEM((1, hid), F32),
            pltpu.VMEM((hid, ch), F32),
        ],
        name="smooth_mlp",
    )(
        departure,
        before,
        after,
        cotangent[0],
        place,
        helm,
        w_first,
        b_first.reshape(1, hid),
        w_second,
        b_second.reshape(1, hid),
        w_third,
    )
    before = shifted(down, 1, bands)
    after = shifted(up, -1, bands)

    swap = [(0, 1), (1, 0)]
    groups = ("y", "x")
    group = lax.axis_size(groups)
    depth = lax.axis_size("z")
    gained = lax.ppermute(give, "core", swap)
    (half_sum,) = call(add_kernel, [half], [VMEM] * 2, name="half_sum")(keep, gained)
    parts = lax.all_to_all(half_sum.reshape(group, PART_ROWS, ch), groups, 0, 0)
    (part_sum,) = call(
        functools.partial(sum_kernel, depth),
        [shape((depth, PART_ROWS, ch), BF16)],
        [VMEM],
        name="part_sum",
    )(parts)
    parts = lax.all_to_all(part_sum, "z", 0, 0)
    (part_sum,) = call(
        functools.partial(sum_kernel, group),
        [shape((group, PART_ROWS, ch), BF16)],
        [VMEM],
        name="whole_sum",
    )(parts)
    mine = lax.all_to_all(part_sum, groups, 0, 0).reshape(16 * PART_ROWS, ch)
    other = lax.ppermute(mine, "core", swap)

    slot_grads = call(
        functools.partial(adjoint_kernel, offsets),
        [block] * offsets,
        [VMEM] * 3 + [SMEM] + [VMEM] * 3,
        [
            pltpu.VMEM((band_rows + 2, lon, ch), F32),
            pltpu.VMEM((band_rows * lon, taps * ch), BF16),
            pltpu.VMEM((offsets * quads, band_rows * lon), BF16),
            pltpu.VMEM((taps * band_rows, lon), F32),
        ],
        name="adjoint",
    )(scaled, before, after, place, helm, dep_slot, dep_weight)
    back = [
        slot_grads[e] if e == reach else shifted(slot_grads[e], reach - e, bands)
        for e in range(offsets)
    ]
    (field_grad,) = call(
        functools.partial(scatter_kernel, offsets),
        [shape((band_rows, lon, ch), F32)],
        [VMEM, SMEM] + [VMEM] * offsets,
        [
            pltpu.VMEM((offsets * quads, taps * ch), BF16),
            pltpu.VMEM(((band_rows - 1) * lon, offsets * quads), BF16),
        ],
        name="scatter",
    )(rows8, send_count, *back)
    grads = call(
        unpack_kernel,
        [
            shape((ch, hid), F32),
            shape((1, hid), F32),
            shape((hid, hid), F32),
            shape((1, hid), F32),
            shape((hid, ch), F32),
        ],
        [VMEM, VMEM, SMEM],
        name="unpack",
    )(mine, other, place)
    return (
        next_state[None],
        field_grad[None],
        grads[0],
        grads[1].reshape(hid),
        grads[2],
        grads[3].reshape(hid),
        grads[4],
    )


def solution(mesh):
    fine = Mesh(mesh.devices.reshape(4, 8, 4, 2), ("y",) + SPACE)
    state = P("y", SPACE, None, None)
    return jax.shard_map(
        body,
        mesh=fine,
        in_specs=(
            state,
            P(SPACE, None, None),
            P(SPACE, None),
            P(None, SPACE, None),
            P(None, SPACE, None),
            P(),
            P(),
            P(),
            P(),
            P(),
            P(),
            state,
        ),
        out_specs=(state, state, P(), P(), P(), P(), P()),
        check_vma=False,
    )
```

```python
import functools
import math

import jax
import jax.numpy as jnp
from jax import lax
from jax.experimental import pallas as pl
from jax.experimental.pallas import tpu as pltpu
from jax.sharding import Mesh
from jax.sharding import PartitionSpec as P

F32 = jnp.float32
BF16 = jnp.bfloat16
SPACE = ("z", "x", "core")
GELU_SCALE = math.sqrt(2.0 / math.pi)
GELU_CUBE = 0.044715
PART_ROWS = 40

VMEM = pl.BlockSpec(memory_space=pltpu.VMEM)
ANY = pl.BlockSpec(memory_space=pl.ANY)
SMEM = pl.BlockSpec(memory_space=pltpu.SMEM)


def dot(left, right, left_dim=1, right_dim=0):
    return lax.dot_general(
        left,
        right,
        (((left_dim,), (right_dim,)), ((), ())),
        preferred_element_type=F32,
    )


def call(kernel, outs, ins, scratch=(), flops=0, name=None):
    nbytes = sum(math.prod(o.shape) * o.dtype.itemsize for o in outs)
    return pl.pallas_call(
        kernel,
        out_shape=outs,
        in_specs=ins,
        out_specs=[VMEM] * len(outs),
        scratch_shapes=list(scratch),
        compiler_params=pltpu.CompilerParams(vmem_limit_bytes=40 * 1024 * 1024),
        cost_estimate=pl.CostEstimate(
            flops=flops, bytes_accessed=2 * nbytes, transcendentals=0
        ),
        name=name,
    )


def quad_boxes(rows_ref, count_ref, offsets, slots):
    quads = slots // 4
    rows = rows_ref[...]
    pick = (
        lax.broadcasted_iota(jnp.int32, (slots, quads), 0)
        == 4 * lax.broadcasted_iota(jnp.int32, (slots, quads), 1)
    ).astype(F32).astype(BF16)
    high = (rows >> 3).astype(F32).astype(BF16)
    low = (rows & 7).astype(F32).astype(BF16)
    cells = (dot(high, pick) * 8.0 + dot(low, pick)).astype(jnp.int32)
    offset_at = lax.broadcasted_iota(jnp.int32, cells.shape, 0)
    live = jnp.zeros(cells.shape, jnp.int32)
    for offset in range(offsets):
        live = jnp.where(offset_at == offset, count_ref[0, offset], live)
    slot_at = 4 * lax.broadcasted_iota(jnp.int32, cells.shape, 1)
    return jnp.where(slot_at < live, cells, -1)


def pack_kernel(offsets, field_ref, rows_ref, count_ref, *refs):
    outs, (pair, select) = refs[:offsets], refs[offsets:]
    band_rows, lon, ch = field_ref.shape
    slots = rows_ref.shape[1]
    quads = slots // 4
    boxes = (band_rows - 1) * lon
    cells = quad_boxes(rows_ref, count_ref, offsets, slots)
    columns = cells.astype(F32).T.astype(jnp.int32)
    box_at = lax.broadcasted_iota(jnp.int32, (quads, boxes), 1)
    for offset in range(offsets):
        select[offset * quads : (offset + 1) * quads] = (
            (box_at == columns[:, offset : offset + 1]).astype(F32).astype(BF16)
        )
    for row in range(band_rows):
        line = field_ref[row]
        pair[row * lon : (row + 1) * lon, :ch] = line
        pair[row * lon : (row + 1) * lon, ch:] = pltpu.roll(
            line.astype(F32), lon - 1, 0
        ).astype(BF16)
    for part in range(2):
        picked = dot(select[...], pair[part * lon : part * lon + boxes]).astype(BF16)
        for offset in range(offsets):
            outs[offset][:, part * 2 * ch : (part + 1) * 2 * ch] = picked[
                offset * quads : (offset + 1) * quads
            ]


def tap_columns(weight_ref, stack):
    taps, band_rows, _ = weight_ref.shape
    for tap in range(taps):
        stack[tap * band_rows : (tap + 1) * band_rows] = weight_ref[tap]
    return stack[...].T


def interp_kernel(offsets, *refs):
    blocks = refs[:offsets]
    slot_ref, weight_ref, dep_ref, up_ref, down_ref, table, stack, slot_stack = refs[offsets:]
    taps, band_rows, lon = weight_ref.shape
    quads, wide = blocks[0].shape
    ch = wide // taps
    weights = tap_columns(weight_ref, stack)
    slot_stack[...] = jnp.zeros_like(slot_stack)
    slot_stack[:band_rows] = (slot_ref[0] >> 2).astype(F32)
    quad_columns = slot_stack[...].T.astype(jnp.int32)
    for offset in range(offsets):
        table[offset * quads : (offset + 1) * quads] = blocks[offset][...]
    quad_at = lax.broadcasted_iota(jnp.int32, (lon, offsets * quads), 1)
    for row in range(band_rows):
        hit = (quad_at == quad_columns[:, row : row + 1]).astype(F32).astype(BF16)
        tapped = dot(hit, table[...])
        line = jnp.zeros((lon, ch), F32)
        for tap in range(taps):
            at = tap * band_rows + row
            line = line + weights[:, at : at + 1] * tapped[:, tap * ch : (tap + 1) * ch]
        dep_ref[row] = line
        if row < 2:
            up_ref[row] = line.astype(BF16)
        if row >= band_rows - 2:
            down_ref[row - band_rows + 2] = line.astype(BF16)


def lon_sum(line):
    lon = line.shape[0]
    return pltpu.roll(line, 1, 0) + pltpu.roll(line, lon - 1, 0)


def gelu_parts(pre):
    square = pre * pre
    curve = jnp.tanh(pre * (GELU_SCALE + (GELU_SCALE * GELU_CUBE) * square))
    half = 0.5 + 0.5 * curve
    slope = half + (0.5 * pre) * (1.0 - curve * curve) * (
        GELU_SCALE + (3.0 * GELU_SCALE * GELU_CUBE) * square
    )
    return pre * half, slope


def mlp_kernel(
    dep_ref,
    before_ref,
    after_ref,
    cot_ref,
    place_ref,
    helm_ref,
    w1_ref,
    b1_ref,
    w2_ref,
    b2_ref,
    w3_ref,
    next_ref,
    scaled_ref,
    up_ref,
    down_ref,
    keep_ref,
    give_ref,
    once,
    smooth,
    g1,
    gb1,
    g2,
    gb2,
    g3,
):
    band_rows, lon, ch = dep_ref.shape
    helm = helm_ref[...]
    inverse = 1.0 / (1.0 + 4.0 * helm)

    def departure(row):
        if row < 0:
            return before_ref[row + 2].astype(F32)
        if row >= band_rows:
            return after_ref[row - band_rows].astype(F32)
        return dep_ref[row]

    first = jnp.where(place_ref[0] == 0, 0.0, 1.0)
    last = jnp.where(place_ref[0] == place_ref[1] - 1, 0.0, 1.0)
    ahead = departure(-2), departure(-1)
    if True:
        ahead = ahead[0] * first, ahead[1] * first
    behind = departure(band_rows) * last, departure(band_rows + 1) * last
    lines = {-2: ahead[0], -1: ahead[1], band_rows: behind[0], band_rows + 1: behind[1]}
    for row in range(-1, band_rows + 1):
        mid, above, below = (
            lines[r] if r in lines else departure(r) for r in (row, row - 1, row + 1)
        )
        value = (mid + helm * (above + below + lon_sum(mid))) * inverse
        if row < 0:
            value = value * first
        if row >= band_rows:
            value = value * last
        once[row + 1] = value
    for row in range(band_rows):
        value = (
            dep_ref[row] + helm * (once[row] + once[row + 2] + lon_sum(once[row + 1]))
        ) * inverse
        smooth[row] = value.astype(BF16)
    for total in (g1, gb1, g2, gb2, g3):
        total[...] = jnp.zeros_like(total)

    def one_row(row, carry):
        rows = smooth[row]
        cot = cot_ref[row]
        act, slope_first = gelu_parts(dot(rows, w1_ref[...]) + b1_ref[...])
        act_first = act.astype(BF16)
        act, slope_second = gelu_parts(dot(act_first, w2_ref[...]) + b2_ref[...])
        act_second = act.astype(BF16)
        next_ref[row] = (rows.astype(F32) + dot(act_second, w3_ref[...])).astype(BF16)
        g3[...] += dot(act_second, cot, 0, 0)
        gpre = dot(cot, w3_ref[...], 1, 1) * slope_second
        gpre_second = gpre.astype(BF16)
        gb2[...] += jnp.sum(gpre_second.astype(F32), axis=0, keepdims=True)
        g2[...] += dot(act_first, gpre_second, 0, 0)
        gpre = dot(gpre_second, w2_ref[...], 1, 1) * slope_first
        gpre_first = gpre.astype(BF16)
        gb1[...] += jnp.sum(gpre_first.astype(F32), axis=0, keepdims=True)
        g1[...] += dot(rows, gpre_first, 0, 0)
        gsmooth = cot.astype(F32) + dot(gpre_first, w1_ref[...], 1, 1)
        scaled_ref[row] = gsmooth * inverse
        return carry

    lax.fori_loop(0, band_rows, one_row, 0)
    for row in range(2):
        up_ref[row] = scaled_ref[row].astype(BF16)
        down_ref[row] = scaled_ref[band_rows - 2 + row].astype(BF16)
    half = keep_ref.shape[0]
    low = place_ref[2] == 0
    hid = g1.shape[1]

    def place(at, zero, one):
        rows = zero.shape[0]
        keep_ref[at : at + rows] = jnp.where(low, zero, one).astype(BF16)
        give_ref[at : at + rows] = jnp.where(low, one, zero).astype(BF16)

    place(0, g1[:, :ch], g2[:ch, :ch])
    place(ch, g1[:, ch:], g2[ch:, :ch])
    place(2 * ch, g3[:ch], g2[:ch, ch:])
    place(3 * ch, g3[ch:], g2[ch:, ch:])
    row_at = lax.broadcasted_iota(jnp.int32, (half - 4 * ch, ch), 0)

    def bias(ref):
        return jnp.where(
            row_at == 0, ref[:, :ch], jnp.where(row_at == 1, ref[:, ch:], 0.0)
        )

    place(4 * ch, bias(gb1), bias(gb2))


def adjoint_kernel(
    offsets,
    scaled_ref,
    before_ref,
    after_ref,
    place_ref,
    helm_ref,
    slot_ref,
    weight_ref,
    *refs,
):
    outs, (once, spread, hit, stack) = refs[:offsets], refs[offsets:]
    band_rows, lon, ch = scaled_ref.shape
    taps = weight_ref.shape[0]
    quads = outs[0].shape[0]
    helm = helm_ref[...]
    inverse = 1.0 / (1.0 + 4.0 * helm)
    first = jnp.where(place_ref[0] == 0, 0.0, 1.0)
    last = jnp.where(place_ref[0] == place_ref[1] - 1, 0.0, 1.0)
    weights = tap_columns(weight_ref, stack)
    quad_lanes = slot_ref[0] >> 2
    quad_at = lax.broadcasted_iota(jnp.int32, (offsets * quads, lon), 0)
    for row in range(band_rows):
        hit[:, row * lon : (row + 1) * lon] = (
            (quad_at == quad_lanes[row : row + 1]).astype(F32).astype(BF16)
        )

    def scaled(row):
        if row < 0:
            return before_ref[row + 2].astype(F32) * first
        if row >= band_rows:
            return after_ref[row - band_rows].astype(F32) * last
        return scaled_ref[row]

    for row in range(-1, band_rows + 1):
        value = (helm * inverse) * (scaled(row - 1) + scaled(row + 1) + lon_sum(scaled(row)))
        if row < 0:
            value = value * first
        if row >= band_rows:
            value = value * last
        once[row + 1] = value
    for row in range(band_rows):
        value = (
            scaled_ref[row]
            + once[row + 1]
            + helm * (once[row] + once[row + 2] + lon_sum(once[row + 1]))
        )
        for tap in range(taps):
            at = tap * band_rows + row
            spread[row * lon : (row + 1) * lon, tap * ch : (tap + 1) * ch] = (
                weights[:, at : at + 1] * value
            ).astype(BF16)
    slot_grads = dot(hit[...], spread[...]).astype(BF16)
    for offset in range(offsets):
        outs[offset][...] = slot_grads[offset * quads : (offset + 1) * quads]


def scatter_kernel(offsets, rows_ref, count_ref, *refs):
    blocks = refs[:offsets]
    out_ref, done_ref, table, hit = refs[offsets:]
    done_ref[...] = jnp.zeros_like(done_ref)
    band_rows, lon, ch = out_ref.shape
    slots = rows_ref.shape[1]
    quads = slots // 4
    boxes = (band_rows - 1) * lon
    cells = quad_boxes(rows_ref, count_ref, offsets, slots)
    box_at = lax.broadcasted_iota(jnp.int32, (boxes, quads), 0)
    for offset in range(offsets):
        table[offset * quads : (offset + 1) * quads] = blocks[offset][...]
        hit[:, offset * quads : (offset + 1) * quads] = (
            (box_at == cells[offset : offset + 1]).astype(F32).astype(BF16)
        )
    for row in range(band_rows):
        here = jnp.zeros((lon, ch), F32)
        right = jnp.zeros((lon, ch), F32)
        if row < band_rows - 1:
            both = dot(hit[row * lon : (row + 1) * lon], table[:, : 2 * ch])
            here = here + both[:, :ch]
            right = right + both[:, ch:]
        if row > 0:
            both = dot(hit[(row - 1) * lon : row * lon], table[:, 2 * ch :])
            here = here + both[:, :ch]
            right = right + both[:, ch:]
        out_ref[row] = here + pltpu.roll(right, 1, 0)


def add_kernel(left_ref, right_ref, out_ref):
    out_ref[...] = (left_ref[...].astype(F32) + right_ref[...].astype(F32)).astype(BF16)


def sum_kernel(copies, parts_ref, ahead_ref, out_ref):
    total = parts_ref[0].astype(F32)
    for part in range(1, parts_ref.shape[0]):
        total = total + parts_ref[part].astype(F32)
    total = total.astype(BF16)
    for copy in range(copies):
        out_ref[copy] = total


def unpack_kernel(mine_ref, other_ref, place_ref, g1, gb1, g2, gb2, g3):
    ch, hid = g1.shape
    low = place_ref[2] == 0

    def halves(at, rows):
        mine = mine_ref[at : at + rows].astype(F32)
        other = other_ref[at : at + rows].astype(F32)
        return jnp.where(low, mine, other), jnp.where(low, other, mine)

    zero, one = halves(0, ch)
    g1[:, :ch], g2[:ch, :ch] = zero, one
    zero, one = halves(ch, ch)
    g1[:, ch:], g2[ch:, :ch] = zero, one
    zero, one = halves(2 * ch, ch)
    g3[:ch], g2[:ch, ch:] = zero, one
    zero, one = halves(3 * ch, ch)
    g3[ch:], g2[ch:, ch:] = zero, one
    zero, one = halves(4 * ch, 8)
    gb1[:, :ch], gb1[:, ch:] = zero[:1], zero[1:2]
    gb2[:, :ch], gb2[:, ch:] = one[:1], one[1:2]


def shifted(block, by, count):
    return lax.ppermute(block, SPACE, [(i, (i + by) % count) for i in range(count)])


def body(
    field,
    send_rows,
    send_count,
    dep_slot,
    dep_weight,
    helm_coef,
    w_first,
    b_first,
    w_second,
    b_second,
    w_third,
    cotangent,
):
    _, band_rows, lon, ch = field.shape
    hid = w_first.shape[1]
    offsets, slots = send_rows.shape[1:]
    taps = dep_slot.shape[0]
    reach = (offsets - 1) // 2
    quads = slots // 4
    bands = lax.axis_size(SPACE)
    shape = jax.ShapeDtypeStruct
    core = lax.axis_index("core").astype(jnp.int32)
    place = jnp.stack(
        [lax.axis_index(SPACE).astype(jnp.int32), jnp.int32(bands), core]
    )
    rows8 = jnp.pad(send_rows[0], ((0, 8 - offsets), (0, 0)))
    helm = helm_coef.reshape(1, ch)
    block = shape((quads, taps * ch), BF16)
    edge = shape((2, lon, ch), BF16)

    packed = call(
        functools.partial(pack_kernel, offsets),
        [block] * offsets,
        [VMEM, VMEM, SMEM],
        [
            pltpu.VMEM((band_rows * lon, 2 * ch), BF16),
            pltpu.VMEM((offsets * quads, (band_rows - 1) * lon), BF16),
        ],
        name="pack",
    )(field[0], rows8, send_count)
    received = [
        packed[e] if e == reach else shifted(packed[e], e - reach, bands)
        for e in range(offsets)
    ]
    departure, up, down = call(
        functools.partial(interp_kernel, offsets),
        [shape((band_rows, lon, ch), F32), edge, edge],
        [VMEM] * (offsets + 2),
        [
            pltpu.VMEM((offsets * quads, taps * ch), BF16),
            pltpu.VMEM((taps * band_rows, lon), F32),
            pltpu.VMEM((8, lon), F32),
        ],
        name="interp",
    )(*received, dep_slot, dep_weight)
    before = shifted(down, 1, bands)
    after = shifted(up, -1, bands)
    half = shape((16 * PART_ROWS, ch), BF16)
    next_state, scaled, up, down, keep, give = call(
        mlp_kernel,
        [
            shape((band_rows, lon, ch), BF16),
            shape((band_rows, lon, ch), F32),
            edge,
            edge,
            half,
            half,
        ],
        [VMEM] * 4 + [SMEM] + [VMEM] * 6,
        [
            pltpu.VMEM((band_rows + 2, lon, ch), F32),
            pltpu.VMEM((band_rows, lon, ch), BF16),
            pltpu.VMEM((ch, hid), F32),
            pltpu.VMEM((1, hid), F32),
            pltpu.VMEM((hid, hid), F32),
            pltpu.VMEM((1, hid), F32),
            pltpu.VMEM((hid, ch), F32),
        ],
        name="smooth_mlp",
    )(
        departure,
        before,
        after,
        cotangent[0],
        place,
        helm,
        w_first,
        b_first.reshape(1, hid),
        w_second,
        b_second.reshape(1, hid),
        w_third,
    )
    before = shifted(down, 1, bands)
    after = shifted(up, -1, bands)

    swap = [(0, 1), (1, 0)]
    groups = ("y", "x")
    group = lax.axis_size(groups)
    depth = lax.axis_size("z")
    gained = lax.ppermute(give, "core", swap)
    (half_sum,) = call(add_kernel, [half], [VMEM] * 2, name="half_sum")(keep, gained)
    parts = lax.all_to_all(half_sum.reshape(group, PART_ROWS, ch), groups, 0, 0)
    slot_grads = call(
        functools.partial(adjoint_kernel, offsets),
        [block] * offsets,
        [VMEM] * 3 + [SMEM] + [VMEM] * 3,
        [
            pltpu.VMEM((band_rows + 2, lon, ch), F32),
            pltpu.VMEM((band_rows * lon, taps * ch), BF16),
            pltpu.VMEM((offsets * quads, band_rows * lon), BF16),
            pltpu.VMEM((taps * band_rows, lon), F32),
        ],
        name="adjoint",
    )(scaled, before, after, place, helm, dep_slot, dep_weight)
    (part_sum,) = call(
        functools.partial(sum_kernel, depth),
        [shape((depth, PART_ROWS, ch), BF16)],
        [VMEM, ANY],
        name="part_sum",
    )(parts, slot_grads[reach])
    parts = lax.all_to_all(part_sum, "z", 0, 0)
    back = [
        slot_grads[e] if e == reach else shifted(slot_grads[e], reach - e, bands)
        for e in range(offsets)
    ]
    field_grad, done = call(
        functools.partial(scatter_kernel, offsets),
        [shape((band_rows, lon, ch), F32), shape((8, ch), F32)],
        [VMEM, SMEM] + [VMEM] * offsets,
        [
            pltpu.VMEM((offsets * quads, taps * ch), BF16),
            pltpu.VMEM(((band_rows - 1) * lon, offsets * quads), BF16),
        ],
        name="scatter",
    )(rows8, send_count, *back)
    (part_sum,) = call(
        functools.partial(sum_kernel, group),
        [shape((group, PART_ROWS, ch), BF16)],
        [VMEM, ANY],
        name="whole_sum",
    )(parts, done)
    mine = lax.all_to_all(part_sum, groups, 0, 0).reshape(16 * PART_ROWS, ch)
    other = lax.ppermute(mine, "core", swap)

    grads = call(
        unpack_kernel,
        [
            shape((ch, hid), F32),
            shape((1, hid), F32),
            shape((hid, hid), F32),
            shape((1, hid), F32),
            shape((hid, ch), F32),
        ],
        [VMEM, VMEM, SMEM],
        name="unpack",
    )(mine, other, place)
    return (
        next_state[None],
        field_grad[None],
        grads[0],
        grads[1].reshape(hid),
        grads[2],
        grads[3].reshape(hid),
        grads[4],
    )


def solution(mesh):
    fine = Mesh(mesh.devices.reshape(4, 8, 4, 2), ("y",) + SPACE)
    state = P("y", SPACE, None, None)
    return jax.shard_map(
        body,
        mesh=fine,
        in_specs=(
            state,
            P(SPACE, None, None),
            P(SPACE, None),
            P(None, SPACE, None),
            P(None, SPACE, None),
            P(),
            P(),
            P(),
            P(),
            P(),
            P(),
            state,
        ),
        out_specs=(state, state, P(), P(), P(), P(), P()),
        check_vma=False,
    )
```

```python
import functools
import math

import jax
import jax.numpy as jnp
from jax import lax
from jax.experimental import pallas as pl
from jax.experimental.pallas import tpu as pltpu
from jax.sharding import Mesh
from jax.sharding import PartitionSpec as P

F32 = jnp.float32
BF16 = jnp.bfloat16
SPACE = ("z", "x", "core")
GELU_SCALE = math.sqrt(2.0 / math.pi)
GELU_CUBE = 0.044715
PART_ROWS = 40
TABLE_AT = 16
PREPARE_COST = 10**9
GATHER_COST = 10**10
PART_COST = 10**10
ADJOINT_COST = 10**11
SCATTER_COST = 10**11
CHOOSE_COST = 2 * 10**9

VMEM = pl.BlockSpec(memory_space=pltpu.VMEM)
ANY = pl.BlockSpec(memory_space=pl.ANY)
SMEM = pl.BlockSpec(memory_space=pltpu.SMEM)


def dot(left, right, left_dim=1, right_dim=0):
    return lax.dot_general(
        left,
        right,
        (((left_dim,), (right_dim,)), ((), ())),
        preferred_element_type=F32,
    )


def call(kernel, outs, ins, scratch=(), flops=0, name=None):
    nbytes = sum(math.prod(o.shape) * o.dtype.itemsize for o in outs)
    return pl.pallas_call(
        kernel,
        out_shape=outs,
        in_specs=ins,
        out_specs=[VMEM] * len(outs),
        scratch_shapes=list(scratch),
        compiler_params=pltpu.CompilerParams(vmem_limit_bytes=32 * 1024 * 1024),
        cost_estimate=pl.CostEstimate(
            flops=flops, bytes_accessed=2 * nbytes, transcendentals=0
        ),
        name=name,
    )


def quad_boxes(rows, counts, offsets, quads):
    lines = rows.shape[0]
    parts = lines // offsets
    share = quads // parts
    line_at = lax.broadcasted_iota(jnp.int32, rows.shape, 0)
    from_lane = lax.broadcasted_iota(jnp.int32, (quads, quads), 0)
    to_lane = lax.broadcasted_iota(jnp.int32, (quads, quads), 1)
    high = jnp.zeros(rows.shape, F32)
    low = jnp.zeros(rows.shape, F32)
    for part in range(parts):
        pick = (from_lane == 4 * (to_lane - part * share)).astype(F32).astype(BF16)
        here = jnp.where(line_at % parts == part, rows, 0)
        high = high + dot((here >> 3).astype(F32).astype(BF16), pick)
        low = low + dot((here & 7).astype(F32).astype(BF16), pick)
    gather = (
        lax.broadcasted_iota(jnp.int32, (8, lines), 1) // parts
        == lax.broadcasted_iota(jnp.int32, (8, lines), 0)
    ).astype(F32).astype(BF16)
    cells = dot(gather, high.astype(BF16)) * 8.0 + dot(gather, low.astype(BF16))
    cells = cells.astype(jnp.int32)
    offset_at = lax.broadcasted_iota(jnp.int32, cells.shape, 0)
    live = jnp.zeros(cells.shape, jnp.int32)
    for offset in range(offsets):
        live = jnp.where(offset_at == offset, counts[:, offset : offset + 1], live)
    slot_at = 4 * lax.broadcasted_iota(jnp.int32, cells.shape, 1)
    return jnp.where(slot_at < live, cells, -1)


def one_hot(mask):
    return mask.astype(F32).astype(BF16)


def choose_kernel(offsets, rows_ref, count_ref, cells_ref, select_ref):
    quads = cells_ref.shape[1]
    cells = quad_boxes(rows_ref[...], count_ref[...], offsets, quads)
    cells_ref[...] = cells
    columns = cells.astype(F32).T.astype(jnp.int32)
    box_at = lax.broadcasted_iota(jnp.int32, (quads, select_ref.shape[1]), 1)
    for offset in range(offsets):
        select_ref[offset * quads : (offset + 1) * quads] = one_hot(
            box_at == columns[:, offset : offset + 1]
        )


def pack_kernel(offsets, field_ref, select_ref, *refs):
    outs, pair = refs[:offsets], refs[offsets]
    band_rows, lon, ch = field_ref.shape
    quads = outs[0].shape[0]
    boxes = (band_rows - 1) * lon
    for row in range(band_rows):
        line = field_ref[row]
        pair[row * lon : (row + 1) * lon, :ch] = line
        pair[row * lon : (row + 1) * lon, ch:] = pltpu.roll(
            line.astype(F32), lon - 1, 0
        ).astype(BF16)
    for part in range(2):
        picked = dot(select_ref[...], pair[part * lon : part * lon + boxes]).astype(BF16)
        for offset in range(offsets):
            outs[offset][:, part * 2 * ch : (part + 1) * 2 * ch] = picked[
                offset * quads : (offset + 1) * quads
            ]


def prepare_kernel(slot_ref, weight_ref, helm_ref, b1_ref, b2_ref, table_ref):
    taps, band_rows, lon = weight_ref.shape
    ch = helm_ref.shape[1]
    hid = b1_ref.shape[1]
    table_ref[...] = jnp.zeros_like(table_ref)
    for tap in range(taps):
        table_ref[tap * band_rows : (tap + 1) * band_rows] = weight_ref[tap]
    at = taps * band_rows
    table_ref[at : at + band_rows] = (slot_ref[0] >> 2).astype(F32)
    helm = helm_ref[...]
    table_ref[at + 8 : at + 9, :ch] = helm
    table_ref[at + 8 : at + 9, ch : 2 * ch] = 1.0 / (1.0 + 4.0 * helm)
    table_ref[at + 9 : at + 10, :hid] = b1_ref[...]
    table_ref[at + 10 : at + 11, :hid] = b2_ref[...]


def coefficients(table_ref, at, ch):
    return table_ref[at + 8 : at + 9, :ch], table_ref[at + 8 : at + 9, ch : 2 * ch]


def interp_kernel(offsets, *refs):
    blocks = refs[:offsets]
    table_ref, dep_ref, up_ref, down_ref, table = refs[offsets:]
    band_rows, lon, ch = dep_ref.shape
    quads, wide = blocks[0].shape
    taps = wide // ch
    weights = table_ref[: taps * band_rows + 8].T
    columns = weights[:, taps * band_rows :].astype(jnp.int32)
    quad_at = lax.broadcasted_iota(jnp.int32, (lon, offsets * quads), 1)
    for offset in range(offsets):
        table[offset * quads : (offset + 1) * quads] = blocks[offset][...]
    for row in range(band_rows):
        tapped = dot(one_hot(quad_at == columns[:, row : row + 1]), table[...])
        line = jnp.zeros((lon, ch), F32)
        for tap in range(taps):
            at = tap * band_rows + row
            line = line + weights[:, at : at + 1] * tapped[:, tap * ch : (tap + 1) * ch]
        dep_ref[row] = line
        if row < 2:
            up_ref[row] = line.astype(BF16)
        if row >= band_rows - 2:
            down_ref[row - band_rows + 2] = line.astype(BF16)


def lon_sum(line):
    lon = line.shape[0]
    return pltpu.roll(line, 1, 0) + pltpu.roll(line, lon - 1, 0)


def gelu_parts(pre):
    square = pre * pre
    curve = jnp.tanh(pre * (GELU_SCALE + (GELU_SCALE * GELU_CUBE) * square))
    share = 0.5 + 0.5 * curve
    act = pre * share
    slope = share + (act - act * share) * (
        2.0 * GELU_SCALE + (6.0 * GELU_SCALE * GELU_CUBE) * square
    )
    return act, slope


def mlp_kernel(
    dep_ref,
    before_ref,
    after_ref,
    cot_ref,
    place_ref,
    table_ref,
    w1_ref,
    w2_ref,
    w3_ref,
    next_ref,
    scaled_ref,
    up_ref,
    down_ref,
    g1,
    gb1,
    g2,
    gb2,
    g3,
    once,
    smooth,
):
    band_rows, lon, ch = dep_ref.shape
    hid = w1_ref.shape[1]
    helm, inverse = coefficients(table_ref, TABLE_AT, ch)
    b1 = table_ref[TABLE_AT + 9 : TABLE_AT + 10, :hid]
    b2 = table_ref[TABLE_AT + 10 : TABLE_AT + 11, :hid]

    def departure(row):
        if row < 0:
            return before_ref[row + 2].astype(F32)
        if row >= band_rows:
            return after_ref[row - band_rows].astype(F32)
        return dep_ref[row]

    first = jnp.where(place_ref[0] == 0, 0.0, 1.0)
    last = jnp.where(place_ref[0] == place_ref[1] - 1, 0.0, 1.0)
    ahead = departure(-2) * first, departure(-1) * first
    behind = departure(band_rows) * last, departure(band_rows + 1) * last
    lines = {-2: ahead[0], -1: ahead[1], band_rows: behind[0], band_rows + 1: behind[1]}
    for row in range(-1, band_rows + 1):
        mid, above, below = (
            lines[r] if r in lines else departure(r) for r in (row, row - 1, row + 1)
        )
        value = (mid + helm * (above + below + lon_sum(mid))) * inverse
        if row < 0:
            value = value * first
        if row >= band_rows:
            value = value * last
        once[row + 1] = value
    for row in range(band_rows):
        value = (
            dep_ref[row] + helm * (once[row] + once[row + 2] + lon_sum(once[row + 1]))
        ) * inverse
        smooth[row] = value.astype(BF16)
    for total in (g1, gb1, g2, gb2, g3):
        total[...] = jnp.zeros_like(total)

    def one_row(row, carry):
        rows = smooth[row]
        cot = cot_ref[row]
        act, slope_first = gelu_parts(dot(rows, w1_ref[...]) + b1)
        act_first = act.astype(BF16)
        act, slope_second = gelu_parts(dot(act_first, w2_ref[...]) + b2)
        act_second = act.astype(BF16)
        next_ref[row] = (rows.astype(F32) + dot(act_second, w3_ref[...])).astype(BF16)
        g3[...] += dot(act_second, cot, 0, 0)
        gpre = dot(cot, w3_ref[...], 1, 1) * slope_second
        gpre_second = gpre.astype(BF16)
        gb2[...] += jnp.sum(gpre_second.astype(F32), axis=0, keepdims=True)
        g2[...] += dot(act_first, gpre_second, 0, 0)
        gpre = dot(gpre_second, w2_ref[...], 1, 1) * slope_first
        gpre_first = gpre.astype(BF16)
        gb1[...] += jnp.sum(gpre_first.astype(F32), axis=0, keepdims=True)
        g1[...] += dot(rows, gpre_first, 0, 0)
        gsmooth = cot.astype(F32) + dot(gpre_first, w1_ref[...], 1, 1)
        scaled_ref[row] = gsmooth * inverse
        return carry

    lax.fori_loop(0, band_rows, one_row, 0)
    for row in range(2):
        up_ref[row] = scaled_ref[row].astype(BF16)
        down_ref[row] = scaled_ref[band_rows - 2 + row].astype(BF16)


def gather_kernel(g1, gb1, g2, gb2, g3, grads_ref):
    ch = g1.shape[0]
    grads_ref[:ch] = g1[:, :ch].astype(BF16)
    grads_ref[ch : 2 * ch] = g1[:, ch:].astype(BF16)
    grads_ref[2 * ch : 4 * ch] = g2[:, :ch].astype(BF16)
    grads_ref[4 * ch : 6 * ch] = g2[:, ch:].astype(BF16)
    grads_ref[6 * ch : 8 * ch] = g3[...].astype(BF16)
    rest = grads_ref.shape[0] - 8 * ch
    row_at = lax.broadcasted_iota(jnp.int32, (rest, ch), 0)
    tail = jnp.zeros((rest, ch), F32)
    for index, line in enumerate((gb1[:, :ch], gb1[:, ch:], gb2[:, :ch], gb2[:, ch:])):
        tail = jnp.where(row_at == index, line, tail)
    grads_ref[8 * ch :] = tail.astype(BF16)


def adjoint_kernel(
    offsets,
    scaled_ref,
    before_ref,
    after_ref,
    place_ref,
    table_ref,
    *refs,
):
    outs, (once, spread, hit) = refs[:offsets], refs[offsets:]
    band_rows, lon, ch = scaled_ref.shape
    quads, wide = outs[0].shape
    taps = wide // ch
    helm, inverse = coefficients(table_ref, TABLE_AT, ch)
    first = jnp.where(place_ref[0] == 0, 0.0, 1.0)
    last = jnp.where(place_ref[0] == place_ref[1] - 1, 0.0, 1.0)
    weights = table_ref[:TABLE_AT].T
    quad_lanes = table_ref[TABLE_AT : TABLE_AT + 8].astype(jnp.int32)
    quad_at = lax.broadcasted_iota(jnp.int32, (offsets * quads, lon), 0)
    for row in range(band_rows):
        hit[:, row * lon : (row + 1) * lon] = one_hot(quad_at == quad_lanes[row : row + 1])

    def scaled(row):
        if row < 0:
            return before_ref[row + 2].astype(F32) * first
        if row >= band_rows:
            return after_ref[row - band_rows].astype(F32) * last
        return scaled_ref[row]

    for row in range(-1, band_rows + 1):
        value = (helm * inverse) * (scaled(row - 1) + scaled(row + 1) + lon_sum(scaled(row)))
        if row < 0:
            value = value * first
        if row >= band_rows:
            value = value * last
        once[row + 1] = value
    for row in range(band_rows):
        value = (
            scaled_ref[row]
            + once[row + 1]
            + helm * (once[row] + once[row + 2] + lon_sum(once[row + 1]))
        )
        for tap in range(taps):
            at = tap * band_rows + row
            spread[row * lon : (row + 1) * lon, tap * ch : (tap + 1) * ch] = (
                weights[:, at : at + 1] * value
            ).astype(BF16)
    slot_grads = dot(hit[...], spread[...]).astype(BF16)
    for offset in range(offsets):
        outs[offset][...] = slot_grads[offset * quads : (offset + 1) * quads]


def scatter_kernel(offsets, cells_ref, *refs):
    blocks = refs[:offsets]
    out_ref, done_ref, table, hit = refs[offsets:]
    done_ref[...] = jnp.zeros_like(done_ref)
    band_rows, lon, ch = out_ref.shape
    quads = blocks[0].shape[0]
    box_at = lax.broadcasted_iota(jnp.int32, ((band_rows - 1) * lon, quads), 0)
    for offset in range(offsets):
        table[offset * quads : (offset + 1) * quads] = blocks[offset][...]
        hit[:, offset * quads : (offset + 1) * quads] = one_hot(
            box_at == cells_ref[offset : offset + 1]
        )
    for row in range(band_rows):
        here = jnp.zeros((lon, ch), F32)
        right = jnp.zeros((lon, ch), F32)
        if row < band_rows - 1:
            both = dot(hit[row * lon : (row + 1) * lon], table[:, : 2 * ch])
            here = here + both[:, :ch]
            right = right + both[:, ch:]
        if row > 0:
            both = dot(hit[(row - 1) * lon : row * lon], table[:, 2 * ch :])
            here = here + both[:, :ch]
            right = right + both[:, ch:]
        out_ref[row] = here + pltpu.roll(right, 1, 0)


def sum_kernel(copies, parts_ref, ahead_ref, out_ref):
    total = parts_ref[0].astype(F32)
    for part in range(1, parts_ref.shape[0]):
        total = total + parts_ref[part].astype(F32)
    total = total.astype(BF16)
    for copy in range(copies):
        out_ref[copy] = total


def unpack_kernel(sums_ref, g1, gb1, g2, gb2, g3):
    ch, hid = g1.shape
    g1[:, :ch] = sums_ref[:ch].astype(F32)
    g1[:, ch:] = sums_ref[ch : 2 * ch].astype(F32)
    g2[:, :ch] = sums_ref[2 * ch : 4 * ch].astype(F32)
    g2[:, ch:] = sums_ref[4 * ch : 6 * ch].astype(F32)
    g3[...] = sums_ref[6 * ch : 8 * ch].astype(F32)
    tail = sums_ref[8 * ch : 8 * ch + 8].astype(F32)
    gb1[:, :ch], gb1[:, ch:] = tail[0:1], tail[1:2]
    gb2[:, :ch], gb2[:, ch:] = tail[2:3], tail[3:4]


def shifted(block, by, count):
    return lax.ppermute(block, SPACE, [(i, (i + by) % count) for i in range(count)])


def body(
    field,
    send_rows,
    send_count,
    dep_slot,
    dep_weight,
    helm_coef,
    w_first,
    b_first,
    w_second,
    b_second,
    w_third,
    cotangent,
):
    _, band_rows, lon, ch = field.shape
    hid = w_first.shape[1]
    offsets, slots = send_rows.shape[1:]
    taps = dep_slot.shape[0]
    reach = (offsets - 1) // 2
    quads = slots // 4
    bands = lax.axis_size(SPACE)
    shape = jax.ShapeDtypeStruct
    place = jnp.stack([lax.axis_index(SPACE).astype(jnp.int32), jnp.int32(bands)])
    block = shape((quads, taps * ch), BF16)
    edge = shape((2, lon, ch), BF16)
    lines = send_rows.reshape(offsets * slots // quads, quads)

    cells, select = call(
        functools.partial(choose_kernel, offsets),
        [
            shape((8, quads), jnp.int32),
            shape((offsets * quads, (band_rows - 1) * lon), BF16),
        ],
        [VMEM] * 2,
        flops=CHOOSE_COST,
        name="choose",
    )(lines, send_count)
    packed = call(
        functools.partial(pack_kernel, offsets),
        [block] * offsets,
        [VMEM] * 2,
        [pltpu.VMEM((band_rows * lon, 2 * ch), BF16)],
        name="pack",
    )(field[0], select)
    received = [
        packed[e] if e == reach else shifted(packed[e], e - reach, bands)
        for e in range(offsets)
    ]
    (table,) = call(
        prepare_kernel,
        [shape((TABLE_AT + 16, lon), F32)],
        [VMEM] * 5,
        flops=PREPARE_COST,
        name="prepare",
    )(
        dep_slot,
        dep_weight,
        helm_coef.reshape(1, ch),
        b_first.reshape(1, hid),
        b_second.reshape(1, hid),
    )
    departure, up, down = call(
        functools.partial(interp_kernel, offsets),
        [shape((band_rows, lon, ch), F32), edge, edge],
        [VMEM] * (offsets + 1),
        [pltpu.VMEM((offsets * quads, taps * ch), BF16)],
        name="interp",
    )(*received, table)
    before = shifted(down, 1, bands)
    after = shifted(up, -1, bands)
    groups = ("y", "x", "core")
    group = lax.axis_size(groups)
    depth = lax.axis_size("z")
    grad_shapes = [
        shape((ch, hid), F32),
        shape((1, hid), F32),
        shape((hid, hid), F32),
        shape((1, hid), F32),
        shape((hid, ch), F32),
    ]
    next_state, scaled, up, down, *grads = call(
        mlp_kernel,
        [shape((band_rows, lon, ch), BF16), shape((band_rows, lon, ch), F32), edge, edge]
        + grad_shapes,
        [VMEM] * 4 + [SMEM] + [VMEM] * 4,
        [
            pltpu.VMEM((band_rows + 2, lon, ch), F32),
            pltpu.VMEM((band_rows, lon, ch), BF16),
        ],
        name="smooth_mlp",
    )(departure, before, after, cotangent[0], place, table, w_first, w_second, w_third)
    before = shifted(down, 1, bands)
    after = shifted(up, -1, bands)

    (grads,) = call(
        gather_kernel,
        [shape((group * PART_ROWS, ch), BF16)],
        [VMEM] * 5,
        flops=GATHER_COST,
        name="gather",
    )(*grads)
    parts = lax.all_to_all(grads.reshape(group, PART_ROWS, ch), groups, 0, 0)
    slot_grads = call(
        functools.partial(adjoint_kernel, offsets),
        [block] * offsets,
        [VMEM] * 3 + [SMEM, VMEM],
        [
            pltpu.VMEM((band_rows + 2, lon, ch), F32),
            pltpu.VMEM((band_rows * lon, taps * ch), BF16),
            pltpu.VMEM((offsets * quads, band_rows * lon), BF16),
        ],
        flops=ADJOINT_COST,
        name="adjoint",
    )(scaled, before, after, place, table)
    (part_sum,) = call(
        functools.partial(sum_kernel, depth),
        [shape((depth, PART_ROWS, ch), BF16)],
        [VMEM, ANY],
        flops=PART_COST,
        name="part_sum",
    )(parts, slot_grads[reach])
    parts = lax.all_to_all(part_sum, "z", 0, 0)
    back = [
        slot_grads[e] if e == reach else shifted(slot_grads[e], reach - e, bands)
        for e in range(offsets)
    ]
    field_grad, done = call(
        functools.partial(scatter_kernel, offsets),
        [shape((band_rows, lon, ch), F32), shape((8, ch), F32)],
        [VMEM] * (offsets + 1),
        [
            pltpu.VMEM((offsets * quads, taps * ch), BF16),
            pltpu.VMEM(((band_rows - 1) * lon, offsets * quads), BF16),
        ],
        flops=SCATTER_COST,
        name="scatter",
    )(cells, *back)
    (whole_sum,) = call(
        functools.partial(sum_kernel, group),
        [shape((group, PART_ROWS, ch), BF16)],
        [VMEM, ANY],
        name="whole_sum",
    )(parts, done)
    sums = lax.all_to_all(whole_sum, groups, 0, 0).reshape(group * PART_ROWS, ch)
    grads = call(
        unpack_kernel,
        grad_shapes,
        [VMEM],
        name="unpack",
    )(sums)
    return (
        next_state[None],
        field_grad[None],
        grads[0],
        grads[1].reshape(hid),
        grads[2],
        grads[3].reshape(hid),
        grads[4],
    )


def solution(mesh):
    fine = Mesh(mesh.devices.reshape(4, 8, 4, 2), ("y",) + SPACE)
    state = P("y", SPACE, None, None)
    return jax.shard_map(
        body,
        mesh=fine,
        in_specs=(
            state,
            P(SPACE, None, None),
            P(SPACE, None),
            P(None, SPACE, None),
            P(None, SPACE, None),
            P(),
            P(),
            P(),
            P(),
            P(),
            P(),
            state,
        ),
        out_specs=(state, state, P(), P(), P(), P(), P()),
        check_vma=False,
    )
```

```python
import functools
import math

import jax
import jax.numpy as jnp
from jax import lax
from jax.experimental import pallas as pl
from jax.experimental.pallas import tpu as pltpu
from jax.sharding import Mesh
from jax.sharding import PartitionSpec as P

F32 = jnp.float32
BF16 = jnp.bfloat16
SPACE = ("z", "x", "core")
GELU_SCALE = math.sqrt(2.0 / math.pi)
GELU_CUBE = 0.044715
PART_ROWS = 40
TABLE_AT = 16
PREPARE_COST = 10**9
GATHER_COST = 10**10
PART_COST = 0
ADJOINT_COST = 10**11
SCATTER_COST = 10**11
CHOOSE_COST = 2 * 10**9

VMEM = pl.BlockSpec(memory_space=pltpu.VMEM)
ANY = pl.BlockSpec(memory_space=pl.ANY)
SMEM = pl.BlockSpec(memory_space=pltpu.SMEM)


def dot(left, right, left_dim=1, right_dim=0):
    return lax.dot_general(
        left,
        right,
        (((left_dim,), (right_dim,)), ((), ())),
        preferred_element_type=F32,
    )


def call(kernel, outs, ins, scratch=(), flops=0, name=None):
    nbytes = sum(math.prod(o.shape) * o.dtype.itemsize for o in outs)
    return pl.pallas_call(
        kernel,
        out_shape=outs,
        in_specs=ins,
        out_specs=[VMEM] * len(outs),
        scratch_shapes=list(scratch),
        compiler_params=pltpu.CompilerParams(vmem_limit_bytes=32 * 1024 * 1024),
        cost_estimate=pl.CostEstimate(
            flops=flops, bytes_accessed=2 * nbytes, transcendentals=0
        ),
        name=name,
    )


def quad_boxes(index_ref, offsets, quads):
    index = index_ref[...]
    pick = one_hot(
        lax.broadcasted_iota(jnp.int32, (4 * quads, quads), 0)
        == 4 * lax.broadcasted_iota(jnp.int32, (4 * quads, quads), 1)
    )
    high = (index >> 3).astype(F32).astype(BF16)
    low = (index & 7).astype(F32).astype(BF16)
    cells = (dot(high, pick) * 8.0 + dot(low, pick)).astype(jnp.int32)
    offset_at = lax.broadcasted_iota(jnp.int32, cells.shape, 0)
    live = jnp.zeros(cells.shape, jnp.int32)
    for offset in range(offsets):
        count = index[offsets : offsets + 1, offset : offset + 1]
        live = jnp.where(offset_at == offset, count, live)
    slot_at = 4 * lax.broadcasted_iota(jnp.int32, cells.shape, 1)
    return jnp.where(slot_at < live, cells, -1)


def one_hot(mask):
    return mask.astype(F32).astype(BF16)


def choose_kernel(offsets, index_ref, cells_ref, select_ref):
    quads = cells_ref.shape[1]
    cells = quad_boxes(index_ref, offsets, quads)
    cells_ref[...] = cells
    columns = cells.astype(F32).T.astype(jnp.int32)
    box_at = lax.broadcasted_iota(jnp.int32, (quads, select_ref.shape[1]), 1)
    for offset in range(offsets):
        select_ref[offset * quads : (offset + 1) * quads] = one_hot(
            box_at == columns[:, offset : offset + 1]
        )


def pack_kernel(offsets, field_ref, select_ref, *refs):
    outs, pair = refs[:offsets], refs[offsets]
    band_rows, lon, ch = field_ref.shape
    quads = outs[0].shape[0]
    boxes = (band_rows - 1) * lon
    for row in range(band_rows):
        line = field_ref[row]
        pair[row * lon : (row + 1) * lon, :ch] = line
        pair[row * lon : (row + 1) * lon, ch:] = pltpu.roll(
            line.astype(F32), lon - 1, 0
        ).astype(BF16)
    for part in range(2):
        picked = dot(select_ref[...], pair[part * lon : part * lon + boxes]).astype(BF16)
        for offset in range(offsets):
            outs[offset][:, part * 2 * ch : (part + 1) * 2 * ch] = picked[
                offset * quads : (offset + 1) * quads
            ]


def prepare_kernel(slot_ref, weight_ref, helm_ref, b1_ref, b2_ref, table_ref):
    taps, band_rows, lon = weight_ref.shape
    ch = helm_ref.shape[1]
    hid = b1_ref.shape[1]
    table_ref[...] = jnp.zeros_like(table_ref)
    for tap in range(taps):
        table_ref[tap * band_rows : (tap + 1) * band_rows] = weight_ref[tap]
    at = taps * band_rows
    table_ref[at : at + band_rows] = (slot_ref[0] >> 2).astype(F32)
    helm = helm_ref[...]
    table_ref[at + 8 : at + 9, :ch] = helm
    table_ref[at + 8 : at + 9, ch : 2 * ch] = 1.0 / (1.0 + 4.0 * helm)
    table_ref[at + 9 : at + 10, :hid] = b1_ref[...]
    table_ref[at + 10 : at + 11, :hid] = b2_ref[...]


def coefficients(table_ref, at, ch):
    return table_ref[at + 8 : at + 9, :ch], table_ref[at + 8 : at + 9, ch : 2 * ch]


def interp_kernel(offsets, *refs):
    blocks = refs[:offsets]
    table_ref, dep_ref, up_ref, down_ref, table = refs[offsets:]
    band_rows, lon, ch = dep_ref.shape
    quads, wide = blocks[0].shape
    taps = wide // ch
    weights = table_ref[: taps * band_rows + 8].T
    columns = weights[:, taps * band_rows :].astype(jnp.int32)
    quad_at = lax.broadcasted_iota(jnp.int32, (lon, offsets * quads), 1)
    for offset in range(offsets):
        table[offset * quads : (offset + 1) * quads] = blocks[offset][...]
    for row in range(band_rows):
        tapped = dot(one_hot(quad_at == columns[:, row : row + 1]), table[...])
        line = jnp.zeros((lon, ch), F32)
        for tap in range(taps):
            at = tap * band_rows + row
            line = line + weights[:, at : at + 1] * tapped[:, tap * ch : (tap + 1) * ch]
        dep_ref[row] = line
        if row < 2:
            up_ref[row] = line.astype(BF16)
        if row >= band_rows - 2:
            down_ref[row - band_rows + 2] = line.astype(BF16)


def lon_sum(line):
    lon = line.shape[0]
    return pltpu.roll(line, 1, 0) + pltpu.roll(line, lon - 1, 0)


def gelu_parts(pre):
    square = pre * pre
    curve = jnp.tanh(pre * (GELU_SCALE + (GELU_SCALE * GELU_CUBE) * square))
    share = 0.5 + 0.5 * curve
    act = pre * share
    slope = share + (act - act * share) * (
        2.0 * GELU_SCALE + (6.0 * GELU_SCALE * GELU_CUBE) * square
    )
    return act, slope


def mlp_kernel(
    dep_ref,
    before_ref,
    after_ref,
    cot_ref,
    place_ref,
    table_ref,
    w1_ref,
    w2_ref,
    w3_ref,
    next_ref,
    scaled_ref,
    up_ref,
    down_ref,
    g1,
    gb1,
    g2,
    gb2,
    g3,
    once,
    smooth,
    a1,
    a2,
    p1,
    p2,
):
    band_rows, lon, ch = dep_ref.shape
    hid = w1_ref.shape[1]
    helm, inverse = coefficients(table_ref, TABLE_AT, ch)
    b1 = table_ref[TABLE_AT + 9 : TABLE_AT + 10, :hid]
    b2 = table_ref[TABLE_AT + 10 : TABLE_AT + 11, :hid]

    def departure(row):
        if row < 0:
            return before_ref[row + 2].astype(F32)
        if row >= band_rows:
            return after_ref[row - band_rows].astype(F32)
        return dep_ref[row]

    first = jnp.where(place_ref[0] == 0, 0.0, 1.0)
    last = jnp.where(place_ref[0] == place_ref[1] - 1, 0.0, 1.0)
    ahead = departure(-2) * first, departure(-1) * first
    behind = departure(band_rows) * last, departure(band_rows + 1) * last
    lines = {-2: ahead[0], -1: ahead[1], band_rows: behind[0], band_rows + 1: behind[1]}
    for row in range(-1, band_rows + 1):
        mid, above, below = (
            lines[r] if r in lines else departure(r) for r in (row, row - 1, row + 1)
        )
        value = (mid + helm * (above + below + lon_sum(mid))) * inverse
        if row < 0:
            value = value * first
        if row >= band_rows:
            value = value * last
        once[row + 1] = value
    for row in range(band_rows):
        value = (
            dep_ref[row] + helm * (once[row] + once[row + 2] + lon_sum(once[row + 1]))
        ) * inverse
        smooth[row] = value.astype(BF16)
    gb1[...] = jnp.zeros_like(gb1)
    gb2[...] = jnp.zeros_like(gb2)

    for row in range(band_rows):
        rows = smooth[row]
        cot = cot_ref[row]
        act, slope_first = gelu_parts(dot(rows, w1_ref[...]) + b1)
        act_first = act.astype(BF16)
        act, slope_second = gelu_parts(dot(act_first, w2_ref[...]) + b2)
        act_second = act.astype(BF16)
        next_ref[row] = (rows.astype(F32) + dot(act_second, w3_ref[...])).astype(BF16)
        gpre = dot(cot, w3_ref[...], 1, 1) * slope_second
        gpre_second = gpre.astype(BF16)
        gb2[...] += jnp.sum(gpre_second.astype(F32), axis=0, keepdims=True)
        gpre = dot(gpre_second, w2_ref[...], 1, 1) * slope_first
        gpre_first = gpre.astype(BF16)
        gb1[...] += jnp.sum(gpre_first.astype(F32), axis=0, keepdims=True)
        a1[row], a2[row], p1[row], p2[row] = act_first, act_second, gpre_first, gpre_second
        gsmooth = cot.astype(F32) + dot(gpre_first, w1_ref[...], 1, 1)
        scaled_ref[row] = gsmooth * inverse
    flat = band_rows * lon

    def whole(ref):
        return ref[...].reshape(flat, ref.shape[2])

    g3[...] = dot(whole(a2), whole(cot_ref), 0, 0)
    g2[...] = dot(whole(a1), whole(p2), 0, 0)
    g1[...] = dot(whole(smooth), whole(p1), 0, 0)
    for row in range(2):
        up_ref[row] = scaled_ref[row].astype(BF16)
        down_ref[row] = scaled_ref[band_rows - 2 + row].astype(BF16)


def gather_kernel(g1, gb1, g2, gb2, g3, grads_ref):
    ch = g1.shape[0]
    grads_ref[:ch] = g1[:, :ch].astype(BF16)
    grads_ref[ch : 2 * ch] = g1[:, ch:].astype(BF16)
    grads_ref[2 * ch : 4 * ch] = g2[:, :ch].astype(BF16)
    grads_ref[4 * ch : 6 * ch] = g2[:, ch:].astype(BF16)
    grads_ref[6 * ch : 8 * ch] = g3[...].astype(BF16)
    rest = grads_ref.shape[0] - 8 * ch
    row_at = lax.broadcasted_iota(jnp.int32, (rest, ch), 0)
    tail = jnp.zeros((rest, ch), F32)
    for index, line in enumerate((gb1[:, :ch], gb1[:, ch:], gb2[:, :ch], gb2[:, ch:])):
        tail = jnp.where(row_at == index, line, tail)
    grads_ref[8 * ch :] = tail.astype(BF16)


def adjoint_kernel(
    offsets,
    scaled_ref,
    before_ref,
    after_ref,
    place_ref,
    table_ref,
    *refs,
):
    outs, (once, spread, hit) = refs[:offsets], refs[offsets:]
    band_rows, lon, ch = scaled_ref.shape
    quads, wide = outs[0].shape
    taps = wide // ch
    helm, inverse = coefficients(table_ref, TABLE_AT, ch)
    first = jnp.where(place_ref[0] == 0, 0.0, 1.0)
    last = jnp.where(place_ref[0] == place_ref[1] - 1, 0.0, 1.0)
    weights = table_ref[:TABLE_AT].T
    quad_lanes = table_ref[TABLE_AT : TABLE_AT + 8].astype(jnp.int32)
    quad_at = lax.broadcasted_iota(jnp.int32, (offsets * quads, lon), 0)
    for row in range(band_rows):
        hit[:, row * lon : (row + 1) * lon] = one_hot(quad_at == quad_lanes[row : row + 1])

    def scaled(row):
        if row < 0:
            return before_ref[row + 2].astype(F32) * first
        if row >= band_rows:
            return after_ref[row - band_rows].astype(F32) * last
        return scaled_ref[row]

    for row in range(-1, band_rows + 1):
        value = (helm * inverse) * (scaled(row - 1) + scaled(row + 1) + lon_sum(scaled(row)))
        if row < 0:
            value = value * first
        if row >= band_rows:
            value = value * last
        once[row + 1] = value
    for row in range(band_rows):
        value = (
            scaled_ref[row]
            + once[row + 1]
            + helm * (once[row] + once[row + 2] + lon_sum(once[row + 1]))
        )
        for tap in range(taps):
            at = tap * band_rows + row
            spread[row * lon : (row + 1) * lon, tap * ch : (tap + 1) * ch] = (
                weights[:, at : at + 1] * value
            ).astype(BF16)
    slot_grads = dot(hit[...], spread[...]).astype(BF16)
    for offset in range(offsets):
        outs[offset][...] = slot_grads[offset * quads : (offset + 1) * quads]


def scatter_kernel(offsets, cells_ref, *refs):
    blocks = refs[:offsets]
    out_ref, done_ref, table, hit = refs[offsets:]
    done_ref[...] = jnp.zeros_like(done_ref)
    band_rows, lon, ch = out_ref.shape
    quads = blocks[0].shape[0]
    box_at = lax.broadcasted_iota(jnp.int32, ((band_rows - 1) * lon, quads), 0)
    for offset in range(offsets):
        table[offset * quads : (offset + 1) * quads] = blocks[offset][...]
        hit[:, offset * quads : (offset + 1) * quads] = one_hot(
            box_at == cells_ref[offset : offset + 1]
        )
    for row in range(band_rows):
        here = jnp.zeros((lon, ch), F32)
        right = jnp.zeros((lon, ch), F32)
        if row < band_rows - 1:
            both = dot(hit[row * lon : (row + 1) * lon], table[:, : 2 * ch])
            here = here + both[:, :ch]
            right = right + both[:, ch:]
        if row > 0:
            both = dot(hit[(row - 1) * lon : row * lon], table[:, 2 * ch :])
            here = here + both[:, :ch]
            right = right + both[:, ch:]
        out_ref[row] = here + pltpu.roll(right, 1, 0)


def sum_kernel(copies, parts_ref, ahead_ref, out_ref):
    total = parts_ref[0].astype(F32)
    for part in range(1, parts_ref.shape[0]):
        total = total + parts_ref[part].astype(F32)
    total = total.astype(BF16)
    for copy in range(copies):
        out_ref[copy] = total


def unpack_kernel(sums_ref, ahead_ref, g1, gb1, g2, gb2, g3):
    ch, hid = g1.shape
    g1[:, :ch] = sums_ref[:ch].astype(F32)
    g1[:, ch:] = sums_ref[ch : 2 * ch].astype(F32)
    g2[:, :ch] = sums_ref[2 * ch : 4 * ch].astype(F32)
    g2[:, ch:] = sums_ref[4 * ch : 6 * ch].astype(F32)
    g3[...] = sums_ref[6 * ch : 8 * ch].astype(F32)
    tail = sums_ref[8 * ch : 8 * ch + 8].astype(F32)
    gb1[:, :ch], gb1[:, ch:] = tail[0:1], tail[1:2]
    gb2[:, :ch], gb2[:, ch:] = tail[2:3], tail[3:4]


def shifted(block, by, count):
    return lax.ppermute(block, SPACE, [(i, (i + by) % count) for i in range(count)])


def body(
    field,
    send_rows,
    send_count,
    dep_slot,
    dep_weight,
    helm_coef,
    w_first,
    b_first,
    w_second,
    b_second,
    w_third,
    cotangent,
):
    _, band_rows, lon, ch = field.shape
    hid = w_first.shape[1]
    offsets, slots = send_rows.shape[1:]
    taps = dep_slot.shape[0]
    reach = (offsets - 1) // 2
    quads = slots // 4
    bands = lax.axis_size(SPACE)
    shape = jax.ShapeDtypeStruct
    place = jnp.stack([lax.axis_index(SPACE).astype(jnp.int32), jnp.int32(bands)])
    block = shape((quads, taps * ch), BF16)
    edge = shape((2, lon, ch), BF16)
    index = jnp.pad(send_rows[0], ((0, 8 - offsets), (0, 0))) + jnp.pad(
        send_count, ((offsets, 7 - offsets), (0, slots - offsets))
    )

    cells, select = call(
        functools.partial(choose_kernel, offsets),
        [
            shape((8, quads), jnp.int32),
            shape((offsets * quads, (band_rows - 1) * lon), BF16),
        ],
        [VMEM],
        flops=CHOOSE_COST,
        name="choose",
    )(index)
    packed = call(
        functools.partial(pack_kernel, offsets),
        [block] * offsets,
        [VMEM] * 2,
        [pltpu.VMEM((band_rows * lon, 2 * ch), BF16)],
        name="pack",
    )(field[0], select)
    received = [
        packed[e] if e == reach else shifted(packed[e], e - reach, bands)
        for e in range(offsets)
    ]
    (table,) = call(
        prepare_kernel,
        [shape((TABLE_AT + 16, lon), F32)],
        [VMEM] * 5,
        flops=PREPARE_COST,
        name="prepare",
    )(
        dep_slot,
        dep_weight,
        helm_coef.reshape(1, ch),
        b_first.reshape(1, hid),
        b_second.reshape(1, hid),
    )
    departure, up, down = call(
        functools.partial(interp_kernel, offsets),
        [shape((band_rows, lon, ch), F32), edge, edge],
        [VMEM] * (offsets + 1),
        [pltpu.VMEM((offsets * quads, taps * ch), BF16)],
        name="interp",
    )(*received, table)
    before = shifted(down, 1, bands)
    after = shifted(up, -1, bands)
    groups = ("y", "x", "core")
    group = lax.axis_size(groups)
    depth = lax.axis_size("z")
    grad_shapes = [
        shape((ch, hid), F32),
        shape((1, hid), F32),
        shape((hid, hid), F32),
        shape((1, hid), F32),
        shape((hid, ch), F32),
    ]
    next_state, scaled, up, down, *grads = call(
        mlp_kernel,
        [shape((band_rows, lon, ch), BF16), shape((band_rows, lon, ch), F32), edge, edge]
        + grad_shapes,
        [VMEM] * 4 + [SMEM] + [VMEM] * 4,
        [
            pltpu.VMEM((band_rows + 2, lon, ch), F32),
            pltpu.VMEM((band_rows, lon, ch), BF16),
        ]
        + [pltpu.VMEM((band_rows, lon, hid), BF16)] * 4,
        name="smooth_mlp",
    )(departure, before, after, cotangent[0], place, table, w_first, w_second, w_third)
    before = shifted(down, 1, bands)
    after = shifted(up, -1, bands)

    (grads,) = call(
        gather_kernel,
        [shape((group * PART_ROWS, ch), BF16)],
        [VMEM] * 5,
        flops=GATHER_COST,
        name="gather",
    )(*grads)
    parts = lax.all_to_all(grads.reshape(group, PART_ROWS, ch), groups, 0, 0)
    slot_grads = call(
        functools.partial(adjoint_kernel, offsets),
        [block] * offsets,
        [VMEM] * 3 + [SMEM, VMEM],
        [
            pltpu.VMEM((band_rows + 2, lon, ch), F32),
            pltpu.VMEM((band_rows * lon, taps * ch), BF16),
            pltpu.VMEM((offsets * quads, band_rows * lon), BF16),
        ],
        flops=ADJOINT_COST,
        name="adjoint",
    )(scaled, before, after, place, table)
    (part_sum,) = call(
        functools.partial(sum_kernel, depth),
        [shape((depth, PART_ROWS, ch), BF16)],
        [VMEM, ANY],
        flops=PART_COST,
        name="part_sum",
    )(parts, slot_grads[reach])
    parts = lax.all_to_all(part_sum, "z", 0, 0)
    back = [
        slot_grads[e] if e == reach else shifted(slot_grads[e], reach - e, bands)
        for e in range(offsets)
    ]
    field_grad, done = call(
        functools.partial(scatter_kernel, offsets),
        [shape((band_rows, lon, ch), F32), shape((8, ch), F32)],
        [VMEM] * (offsets + 1),
        [
            pltpu.VMEM((offsets * quads, taps * ch), BF16),
            pltpu.VMEM(((band_rows - 1) * lon, offsets * quads), BF16),
        ],
        flops=SCATTER_COST,
        name="scatter",
    )(cells, *back)
    (whole_sum,) = call(
        functools.partial(sum_kernel, group),
        [shape((group, PART_ROWS, ch), BF16)],
        [VMEM, ANY],
        name="whole_sum",
    )(parts, slot_grads[reach])
    sums = lax.all_to_all(whole_sum, groups, 0, 0).reshape(group * PART_ROWS, ch)
    grads = call(
        unpack_kernel,
        grad_shapes,
        [VMEM, ANY],
        name="unpack",
    )(sums, done)
    return (
        next_state[None],
        field_grad[None],
        grads[0],
        grads[1].reshape(hid),
        grads[2],
        grads[3].reshape(hid),
        grads[4],
    )


def solution(mesh):
    fine = Mesh(mesh.devices.reshape(4, 8, 4, 2), ("y",) + SPACE)
    state = P("y", SPACE, None, None)
    return jax.shard_map(
        body,
        mesh=fine,
        in_specs=(
            state,
            P(SPACE, None, None),
            P(SPACE, None),
            P(None, SPACE, None),
            P(None, SPACE, None),
            P(),
            P(),
            P(),
            P(),
            P(),
            P(),
            state,
        ),
        out_specs=(state, state, P(), P(), P(), P(), P()),
        check_vma=False,
    )
```

```python
import functools
import math

import jax
import jax.numpy as jnp
from jax import lax
from jax.experimental import pallas as pl
from jax.experimental.pallas import tpu as pltpu
from jax.sharding import Mesh
from jax.sharding import PartitionSpec as P

F32 = jnp.float32
BF16 = jnp.bfloat16
SPACE = ("z", "x", "core")
GELU_SCALE = math.sqrt(2.0 / math.pi)
GELU_CUBE = 0.044715
PART_ROWS = 40
TABLE_AT = 16
PREPARE_COST = 10**9
PART_COST = 0
ADJOINT_COST = 10**11
SCATTER_COST = 10**11
CHOOSE_COST = 2 * 10**9

VMEM = pl.BlockSpec(memory_space=pltpu.VMEM)
ANY = pl.BlockSpec(memory_space=pl.ANY)
SMEM = pl.BlockSpec(memory_space=pltpu.SMEM)


def dot(left, right, left_dim=1, right_dim=0):
    return lax.dot_general(
        left,
        right,
        (((left_dim,), (right_dim,)), ((), ())),
        preferred_element_type=F32,
    )


def call(kernel, outs, ins, scratch=(), flops=0, name=None):
    nbytes = sum(math.prod(o.shape) * o.dtype.itemsize for o in outs)
    return pl.pallas_call(
        kernel,
        out_shape=outs,
        in_specs=ins,
        out_specs=[VMEM] * len(outs),
        scratch_shapes=list(scratch),
        compiler_params=pltpu.CompilerParams(vmem_limit_bytes=32 * 1024 * 1024),
        cost_estimate=pl.CostEstimate(
            flops=flops, bytes_accessed=2 * nbytes, transcendentals=0
        ),
        name=name,
    )


def quad_boxes(index, quads):
    pick = one_hot(
        lax.broadcasted_iota(jnp.int32, (4 * quads, quads), 0)
        == 4 * lax.broadcasted_iota(jnp.int32, (4 * quads, quads), 1)
    )
    high = (index >> 3).astype(F32).astype(BF16)
    low = (index & 7).astype(F32).astype(BF16)
    return (dot(high, pick) * 8.0 + dot(low, pick)).astype(jnp.int32)


def live_quads(count_ref, offset, quads):
    slot_at = 4 * lax.broadcasted_iota(jnp.int32, (quads, 1), 0)
    return slot_at < count_ref[:, offset : offset + 1]


def one_hot(mask):
    return mask.astype(F32).astype(BF16)


def choose_kernel(rows_ref, cells_ref, select_ref, index):
    quads = cells_ref.shape[1]
    offsets = rows_ref.shape[0]
    index[...] = jnp.zeros_like(index)
    for offset in range(offsets):
        index[offset : offset + 1] = rows_ref[offset]
    cells = quad_boxes(index[...], quads)
    cells_ref[...] = cells
    columns = cells.astype(F32).T.astype(jnp.int32)
    box_at = lax.broadcasted_iota(jnp.int32, (quads, select_ref.shape[1]), 1)
    for offset in range(offsets):
        select_ref[offset * quads : (offset + 1) * quads] = one_hot(
            box_at == columns[:, offset : offset + 1]
        )


def pack_kernel(offsets, field_ref, select_ref, count_ref, *refs):
    outs, pair = refs[:offsets], refs[offsets]
    band_rows, lon, ch = field_ref.shape
    quads = outs[0].shape[0]
    boxes = (band_rows - 1) * lon
    for row in range(band_rows):
        line = field_ref[row]
        pair[row * lon : (row + 1) * lon, :ch] = line
        pair[row * lon : (row + 1) * lon, ch:] = pltpu.roll(
            line.astype(F32), lon - 1, 0
        ).astype(BF16)
    for part in range(2):
        picked = dot(select_ref[...], pair[part * lon : part * lon + boxes])
        for offset in range(offsets):
            outs[offset][:, part * 2 * ch : (part + 1) * 2 * ch] = jnp.where(
                live_quads(count_ref, offset, quads),
                picked[offset * quads : (offset + 1) * quads],
                0.0,
            ).astype(BF16)


def prepare_kernel(slot_ref, weight_ref, helm_ref, b1_ref, b2_ref, table_ref):
    taps, band_rows, lon = weight_ref.shape
    ch = helm_ref.shape[1]
    hid = b1_ref.shape[1]
    table_ref[...] = jnp.zeros_like(table_ref)
    for tap in range(taps):
        table_ref[tap * band_rows : (tap + 1) * band_rows] = weight_ref[tap]
    at = taps * band_rows
    table_ref[at : at + band_rows] = (slot_ref[0] >> 2).astype(F32)
    helm = helm_ref[...]
    table_ref[at + 8 : at + 9, :ch] = helm
    table_ref[at + 8 : at + 9, ch : 2 * ch] = 1.0 / (1.0 + 4.0 * helm)
    table_ref[at + 9 : at + 10, :hid] = b1_ref[...]
    table_ref[at + 10 : at + 11, :hid] = b2_ref[...]


def coefficients(table_ref, at, ch):
    return table_ref[at + 8 : at + 9, :ch], table_ref[at + 8 : at + 9, ch : 2 * ch]


def interp_kernel(offsets, order, *refs):
    blocks = dict(zip(order, refs[:offsets]))
    table_ref, dep_ref, up_ref, down_ref, table = refs[offsets:]
    band_rows, lon, ch = dep_ref.shape
    quads, wide = refs[0].shape
    taps = wide // ch
    weights = table_ref[: taps * band_rows + 8].T
    columns = weights[:, taps * band_rows :].astype(jnp.int32)
    quad_at = lax.broadcasted_iota(jnp.int32, (lon, offsets * quads), 1)
    for offset in range(offsets):
        table[offset * quads : (offset + 1) * quads] = blocks[offset][...]
    for row in range(band_rows):
        tapped = dot(one_hot(quad_at == columns[:, row : row + 1]), table[...])
        line = jnp.zeros((lon, ch), F32)
        for tap in range(taps):
            at = tap * band_rows + row
            line = line + weights[:, at : at + 1] * tapped[:, tap * ch : (tap + 1) * ch]
        dep_ref[row] = line
        if row < 2:
            up_ref[row] = line.astype(BF16)
        if row >= band_rows - 2:
            down_ref[row - band_rows + 2] = line.astype(BF16)


def lon_sum(line):
    lon = line.shape[0]
    return pltpu.roll(line, 1, 0) + pltpu.roll(line, lon - 1, 0)


def gelu_parts(pre):
    square = pre * pre
    curve = jnp.tanh(pre * (GELU_SCALE + (GELU_SCALE * GELU_CUBE) * square))
    share = 0.5 + 0.5 * curve
    act = pre * share
    slope = share + (act - act * share) * (
        2.0 * GELU_SCALE + (6.0 * GELU_SCALE * GELU_CUBE) * square
    )
    return act, slope


def mlp_kernel(
    dep_ref,
    after_ref,
    before_ref,
    cot_ref,
    place_ref,
    table_ref,
    w1_ref,
    w2_ref,
    w3_ref,
    next_ref,
    scaled_ref,
    up_ref,
    down_ref,
    grads_ref,
    gb1,
    gb2,
    once,
    smooth,
    a1,
    a2,
    p1,
    p2,
):
    band_rows, lon, ch = dep_ref.shape
    hid = w1_ref.shape[1]
    helm, inverse = coefficients(table_ref, TABLE_AT, ch)
    b1 = table_ref[TABLE_AT + 9 : TABLE_AT + 10, :hid]
    b2 = table_ref[TABLE_AT + 10 : TABLE_AT + 11, :hid]

    def departure(row):
        if row < 0:
            return before_ref[row + 2].astype(F32)
        if row >= band_rows:
            return after_ref[row - band_rows].astype(F32)
        return dep_ref[row]

    first = jnp.where(place_ref[0] == 0, 0.0, 1.0)
    last = jnp.where(place_ref[0] == place_ref[1] - 1, 0.0, 1.0)
    ahead = departure(-2) * first, departure(-1) * first
    behind = departure(band_rows) * last, departure(band_rows + 1) * last
    lines = {-2: ahead[0], -1: ahead[1], band_rows: behind[0], band_rows + 1: behind[1]}
    for row in range(-1, band_rows + 1):
        mid, above, below = (
            lines[r] if r in lines else departure(r) for r in (row, row - 1, row + 1)
        )
        value = (mid + helm * (above + below + lon_sum(mid))) * inverse
        if row < 0:
            value = value * first
        if row >= band_rows:
            value = value * last
        once[row + 1] = value
    for row in range(band_rows):
        value = (
            dep_ref[row] + helm * (once[row] + once[row + 2] + lon_sum(once[row + 1]))
        ) * inverse
        smooth[row] = value.astype(BF16)
    gb1[...] = jnp.zeros_like(gb1)
    gb2[...] = jnp.zeros_like(gb2)

    for row in range(band_rows):
        rows = smooth[row]
        cot = cot_ref[row]
        act, slope_first = gelu_parts(dot(rows, w1_ref[...]) + b1)
        act_first = act.astype(BF16)
        act, slope_second = gelu_parts(dot(act_first, w2_ref[...]) + b2)
        act_second = act.astype(BF16)
        next_ref[row] = (rows.astype(F32) + dot(act_second, w3_ref[...])).astype(BF16)
        gpre = dot(cot, w3_ref[...], 1, 1) * slope_second
        gpre_second = gpre.astype(BF16)
        gb2[...] += jnp.sum(gpre_second.astype(F32), axis=0, keepdims=True)
        gpre = dot(gpre_second, w2_ref[...], 1, 1) * slope_first
        gpre_first = gpre.astype(BF16)
        gb1[...] += jnp.sum(gpre_first.astype(F32), axis=0, keepdims=True)
        a1[row], a2[row], p1[row], p2[row] = act_first, act_second, gpre_first, gpre_second
        gsmooth = cot.astype(F32) + dot(gpre_first, w1_ref[...], 1, 1)
        scaled_ref[row] = gsmooth * inverse
    flat = band_rows * lon

    def whole(ref):
        return ref[...].reshape(flat, ref.shape[2])

    g3 = dot(whole(a2), whole(cot_ref), 0, 0).astype(BF16)
    g2 = dot(whole(a1), whole(p2), 0, 0).astype(BF16)
    g1 = dot(whole(smooth), whole(p1), 0, 0).astype(BF16)
    for row in range(2):
        up_ref[row] = scaled_ref[row].astype(BF16)
        down_ref[row] = scaled_ref[band_rows - 2 + row].astype(BF16)
    grads_ref[:ch] = g1[:, :ch]
    grads_ref[ch : 2 * ch] = g1[:, ch:]
    grads_ref[2 * ch : 4 * ch] = g2[:, :ch]
    grads_ref[4 * ch : 6 * ch] = g2[:, ch:]
    grads_ref[6 * ch : 8 * ch] = g3
    rest = grads_ref.shape[0] - 8 * ch
    row_at = lax.broadcasted_iota(jnp.int32, (rest, ch), 0)
    tail = jnp.zeros((rest, ch), F32)
    for index, line in enumerate((gb1[:, :ch], gb1[:, ch:], gb2[:, :ch], gb2[:, ch:])):
        tail = jnp.where(row_at == index, line, tail)
    grads_ref[8 * ch :] = tail.astype(BF16)


def adjoint_kernel(
    offsets,
    scaled_ref,
    before_ref,
    after_ref,
    place_ref,
    table_ref,
    *refs,
):
    outs, (once, spread, hit) = refs[:offsets], refs[offsets:]
    band_rows, lon, ch = scaled_ref.shape
    quads, wide = outs[0].shape
    taps = wide // ch
    helm, inverse = coefficients(table_ref, TABLE_AT, ch)
    first = jnp.where(place_ref[0] == 0, 0.0, 1.0)
    last = jnp.where(place_ref[0] == place_ref[1] - 1, 0.0, 1.0)
    weights = table_ref[:TABLE_AT].T
    quad_lanes = table_ref[TABLE_AT : TABLE_AT + 8].astype(jnp.int32)
    quad_at = lax.broadcasted_iota(jnp.int32, (offsets * quads, lon), 0)
    for row in range(band_rows):
        hit[:, row * lon : (row + 1) * lon] = one_hot(quad_at == quad_lanes[row : row + 1])

    def scaled(row):
        if row < 0:
            return before_ref[row + 2].astype(F32) * first
        if row >= band_rows:
            return after_ref[row - band_rows].astype(F32) * last
        return scaled_ref[row]

    for row in range(-1, band_rows + 1):
        value = (helm * inverse) * (scaled(row - 1) + scaled(row + 1) + lon_sum(scaled(row)))
        if row < 0:
            value = value * first
        if row >= band_rows:
            value = value * last
        once[row + 1] = value
    for row in range(band_rows):
        value = (
            scaled_ref[row]
            + once[row + 1]
            + helm * (once[row] + once[row + 2] + lon_sum(once[row + 1]))
        )
        for tap in range(taps):
            at = tap * band_rows + row
            spread[row * lon : (row + 1) * lon, tap * ch : (tap + 1) * ch] = (
                weights[:, at : at + 1] * value
            ).astype(BF16)
    slot_grads = dot(hit[...], spread[...]).astype(BF16)
    for offset in range(offsets):
        outs[offset][...] = slot_grads[offset * quads : (offset + 1) * quads]


def scatter_kernel(offsets, cells_ref, count_ref, *refs):
    blocks = refs[:offsets]
    out_ref, done_ref, table, hit = refs[offsets:]
    done_ref[...] = jnp.zeros_like(done_ref)
    band_rows, lon, ch = out_ref.shape
    quads = blocks[0].shape[0]
    box_at = lax.broadcasted_iota(jnp.int32, ((band_rows - 1) * lon, quads), 0)
    for offset in range(offsets):
        table[offset * quads : (offset + 1) * quads] = jnp.where(
            live_quads(count_ref, offset, quads), blocks[offset][...].astype(F32), 0.0
        ).astype(BF16)
        hit[:, offset * quads : (offset + 1) * quads] = one_hot(
            box_at == cells_ref[offset : offset + 1]
        )
    for row in range(band_rows):
        here = jnp.zeros((lon, ch), F32)
        right = jnp.zeros((lon, ch), F32)
        if row < band_rows - 1:
            both = dot(hit[row * lon : (row + 1) * lon], table[:, : 2 * ch])
            here = here + both[:, :ch]
            right = right + both[:, ch:]
        if row > 0:
            both = dot(hit[(row - 1) * lon : row * lon], table[:, 2 * ch :])
            here = here + both[:, :ch]
            right = right + both[:, ch:]
        out_ref[row] = here + pltpu.roll(right, 1, 0)


def sum_kernel(copies, parts_ref, ahead_ref, out_ref):
    total = parts_ref[0].astype(F32)
    for part in range(1, parts_ref.shape[0]):
        total = total + parts_ref[part].astype(F32)
    total = total.astype(BF16)
    for copy in range(copies):
        out_ref[copy] = total


def unpack_kernel(sums_ref, ahead_ref, g1, gb1, g2, gb2, g3):
    ch, hid = g1.shape
    g1[:, :ch] = sums_ref[:ch].astype(F32)
    g1[:, ch:] = sums_ref[ch : 2 * ch].astype(F32)
    g2[:, :ch] = sums_ref[2 * ch : 4 * ch].astype(F32)
    g2[:, ch:] = sums_ref[4 * ch : 6 * ch].astype(F32)
    g3[...] = sums_ref[6 * ch : 8 * ch].astype(F32)
    tail = sums_ref[8 * ch : 8 * ch + 8].astype(F32)
    gb1[:, :ch], gb1[:, ch:] = tail[0:1], tail[1:2]
    gb2[:, :ch], gb2[:, ch:] = tail[2:3], tail[3:4]


def shifted(block, by, count):
    return lax.ppermute(block, SPACE, [(i, (i + by) % count) for i in range(count)])


def body(
    field,
    send_rows,
    send_count,
    dep_slot,
    dep_weight,
    helm_coef,
    w_first,
    b_first,
    w_second,
    b_second,
    w_third,
    cotangent,
):
    _, band_rows, lon, ch = field.shape
    hid = w_first.shape[1]
    offsets, slots = send_rows.shape[1:]
    taps = dep_slot.shape[0]
    reach = (offsets - 1) // 2
    quads = slots // 4
    bands = lax.axis_size(SPACE)
    shape = jax.ShapeDtypeStruct
    place = jnp.stack([lax.axis_index(SPACE).astype(jnp.int32), jnp.int32(bands)])
    block = shape((quads, taps * ch), BF16)
    edge = shape((2, lon, ch), BF16)

    cells, select = call(
        choose_kernel,
        [
            shape((8, quads), jnp.int32),
            shape((offsets * quads, (band_rows - 1) * lon), BF16),
        ],
        [VMEM],
        [pltpu.VMEM((8, slots), jnp.int32)],
        flops=CHOOSE_COST,
        name="choose",
    )(jnp.transpose(send_rows, (1, 0, 2)))
    packed = call(
        functools.partial(pack_kernel, offsets),
        [block] * offsets,
        [VMEM] * 3,
        [pltpu.VMEM((band_rows * lon, 2 * ch), BF16)],
        name="pack",
    )(field[0], select, send_count)
    received = [
        packed[e] if e == reach else shifted(packed[e], e - reach, bands)
        for e in range(offsets)
    ]
    order = sorted(range(offsets), key=lambda e: -abs(e - reach))
    (table,) = call(
        prepare_kernel,
        [shape((TABLE_AT + 16, lon), F32)],
        [VMEM] * 5,
        flops=PREPARE_COST,
        name="prepare",
    )(
        dep_slot,
        dep_weight,
        helm_coef.reshape(1, ch),
        b_first.reshape(1, hid),
        b_second.reshape(1, hid),
    )
    departure, up, down = call(
        functools.partial(interp_kernel, offsets, order),
        [shape((band_rows, lon, ch), F32), edge, edge],
        [VMEM] * (offsets + 1),
        [pltpu.VMEM((offsets * quads, taps * ch), BF16)],
        name="interp",
    )(*(received[e] for e in order), table)
    after = shifted(up, -1, bands)
    before = shifted(down, 1, bands)
    groups = ("y", "x", "core")
    group = lax.axis_size(groups)
    depth = lax.axis_size("z")
    next_state, scaled, up, down, grads = call(
        mlp_kernel,
        [
            shape((band_rows, lon, ch), BF16),
            shape((band_rows, lon, ch), F32),
            edge,
            edge,
            shape((group * PART_ROWS, ch), BF16),
        ],
        [VMEM] * 4 + [SMEM] + [VMEM] * 4,
        [
            pltpu.VMEM((1, hid), F32),
            pltpu.VMEM((1, hid), F32),
            pltpu.VMEM((band_rows + 2, lon, ch), F32),
            pltpu.VMEM((band_rows, lon, ch), BF16),
        ]
        + [pltpu.VMEM((band_rows, lon, hid), BF16)] * 4,
        name="smooth_mlp",
    )(departure, after, before, cotangent[0], place, table, w_first, w_second, w_third)
    after = shifted(up, -1, bands)
    before = shifted(down, 1, bands)

    parts = lax.all_to_all(grads.reshape(group, PART_ROWS, ch), groups, 0, 0)
    slot_grads = call(
        functools.partial(adjoint_kernel, offsets),
        [block] * offsets,
        [VMEM] * 3 + [SMEM, VMEM],
        [
            pltpu.VMEM((band_rows + 2, lon, ch), F32),
            pltpu.VMEM((band_rows * lon, taps * ch), BF16),
            pltpu.VMEM((offsets * quads, band_rows * lon), BF16),
        ],
        flops=ADJOINT_COST,
        name="adjoint",
    )(scaled, before, after, place, table)
    (part_sum,) = call(
        functools.partial(sum_kernel, depth),
        [shape((depth, PART_ROWS, ch), BF16)],
        [VMEM, ANY],
        flops=PART_COST,
        name="part_sum",
    )(parts, slot_grads[reach])
    parts = lax.all_to_all(part_sum, "z", 0, 0)
    back = [
        slot_grads[e] if e == reach else shifted(slot_grads[e], reach - e, bands)
        for e in range(offsets)
    ]
    field_grad, done = call(
        functools.partial(scatter_kernel, offsets),
        [shape((band_rows, lon, ch), F32), shape((8, ch), F32)],
        [VMEM] * (offsets + 2),
        [
            pltpu.VMEM((offsets * quads, taps * ch), BF16),
            pltpu.VMEM(((band_rows - 1) * lon, offsets * quads), BF16),
        ],
        flops=SCATTER_COST,
        name="scatter",
    )(cells, send_count, *back)
    (whole_sum,) = call(
        functools.partial(sum_kernel, group),
        [shape((group, PART_ROWS, ch), BF16)],
        [VMEM, ANY],
        name="whole_sum",
    )(parts, slot_grads[reach])
    sums = lax.all_to_all(whole_sum, groups, 0, 0).reshape(group * PART_ROWS, ch)
    grad_shapes = [
        shape((ch, hid), F32),
        shape((1, hid), F32),
        shape((hid, hid), F32),
        shape((1, hid), F32),
        shape((hid, ch), F32),
    ]
    grads = call(
        unpack_kernel,
        grad_shapes,
        [VMEM, ANY],
        name="unpack",
    )(sums, done)
    return (
        next_state[None],
        field_grad[None],
        grads[0],
        grads[1].reshape(hid),
        grads[2],
        grads[3].reshape(hid),
        grads[4],
    )


def solution(mesh):
    fine = Mesh(mesh.devices.reshape(4, 8, 4, 2), ("y",) + SPACE)
    state = P("y", SPACE, None, None)
    return jax.shard_map(
        body,
        mesh=fine,
        in_specs=(
            state,
            P(SPACE, None, None),
            P(SPACE, None),
            P(None, SPACE, None),
            P(None, SPACE, None),
            P(),
            P(),
            P(),
            P(),
            P(),
            P(),
            state,
        ),
        out_specs=(state, state, P(), P(), P(), P(), P()),
        check_vma=False,
    )
```

```python
import functools
import math

import jax
import jax.numpy as jnp
from jax import lax
from jax.experimental import pallas as pl
from jax.experimental.pallas import tpu as pltpu
from jax.sharding import Mesh
from jax.sharding import PartitionSpec as P

F32 = jnp.float32
BF16 = jnp.bfloat16
SPACE = ("z", "x", "core")
GELU_SCALE = math.sqrt(2.0 / math.pi)
GELU_CUBE = 0.044715
PART_ROWS = 40
TABLE_AT = 16
PREPARE_COST = 10**9
PART_COST = 0
ADJOINT_COST = 10**11
SCATTER_COST = 10**11
CHOOSE_COST = 2 * 10**9

VMEM = pl.BlockSpec(memory_space=pltpu.VMEM)
ANY = pl.BlockSpec(memory_space=pl.ANY)
SMEM = pl.BlockSpec(memory_space=pltpu.SMEM)


def dot(left, right, left_dim=1, right_dim=0):
    return lax.dot_general(
        left,
        right,
        (((left_dim,), (right_dim,)), ((), ())),
        preferred_element_type=F32,
    )


def call(kernel, outs, ins, scratch=(), flops=0, name=None):
    nbytes = sum(math.prod(o.shape) * o.dtype.itemsize for o in outs)
    return pl.pallas_call(
        kernel,
        out_shape=outs,
        in_specs=ins,
        out_specs=[VMEM] * len(outs),
        scratch_shapes=list(scratch),
        compiler_params=pltpu.CompilerParams(vmem_limit_bytes=32 * 1024 * 1024),
        cost_estimate=pl.CostEstimate(
            flops=flops, bytes_accessed=2 * nbytes, transcendentals=0
        ),
        name=name,
    )


def quad_boxes(index, quads):
    pick = one_hot(
        lax.broadcasted_iota(jnp.int32, (4 * quads, quads), 0)
        == 4 * lax.broadcasted_iota(jnp.int32, (4 * quads, quads), 1)
    )
    high = (index >> 3).astype(F32).astype(BF16)
    low = (index & 7).astype(F32).astype(BF16)
    return (dot(high, pick) * 8.0 + dot(low, pick)).astype(jnp.int32)


def live_quads(count_ref, offset, quads):
    slot_at = 4 * lax.broadcasted_iota(jnp.int32, (quads, 1), 0)
    return slot_at < count_ref[:, offset : offset + 1]


def one_hot(mask):
    return mask.astype(F32).astype(BF16)


def choose_kernel(rows_ref, cells_ref, select_ref, index):
    quads = cells_ref.shape[1]
    offsets = rows_ref.shape[0]
    index[...] = jnp.zeros_like(index)
    for offset in range(offsets):
        index[offset : offset + 1] = rows_ref[offset]
    cells = quad_boxes(index[...], quads)
    cells_ref[...] = cells
    columns = cells.astype(F32).T.astype(jnp.int32)
    box_at = lax.broadcasted_iota(jnp.int32, (quads, select_ref.shape[1]), 1)
    for offset in range(offsets):
        select_ref[offset * quads : (offset + 1) * quads] = one_hot(
            box_at == columns[:, offset : offset + 1]
        )


def pack_kernel(offsets, field_ref, select_ref, count_ref, *refs):
    outs, pair = refs[:offsets], refs[offsets]
    band_rows, lon, ch = field_ref.shape
    quads = outs[0].shape[0]
    boxes = (band_rows - 1) * lon
    for row in range(band_rows):
        line = field_ref[row]
        pair[row * lon : (row + 1) * lon, :ch] = line
        pair[row * lon : (row + 1) * lon, ch:] = pltpu.roll(
            line.astype(F32), lon - 1, 0
        ).astype(BF16)
    for part in range(2):
        picked = dot(select_ref[...], pair[part * lon : part * lon + boxes])
        for offset in range(offsets):
            outs[offset][:, part * 2 * ch : (part + 1) * 2 * ch] = jnp.where(
                live_quads(count_ref, offset, quads),
                picked[offset * quads : (offset + 1) * quads],
                0.0,
            ).astype(BF16)


def prepare_kernel(slot_ref, weight_ref, helm_ref, b1_ref, b2_ref, table_ref):
    taps, band_rows, lon = weight_ref.shape
    ch = helm_ref.shape[1]
    hid = b1_ref.shape[1]
    table_ref[...] = jnp.zeros_like(table_ref)
    for tap in range(taps):
        table_ref[tap * band_rows : (tap + 1) * band_rows] = weight_ref[tap]
    at = taps * band_rows
    table_ref[at : at + band_rows] = (slot_ref[0] >> 2).astype(F32)
    helm = helm_ref[...]
    table_ref[at + 8 : at + 9, :ch] = helm
    table_ref[at + 8 : at + 9, ch : 2 * ch] = 1.0 / (1.0 + 4.0 * helm)
    table_ref[at + 9 : at + 10, :hid] = b1_ref[...]
    table_ref[at + 10 : at + 11, :hid] = b2_ref[...]


def coefficients(table_ref, at, ch):
    return table_ref[at + 8 : at + 9, :ch], table_ref[at + 8 : at + 9, ch : 2 * ch]


def interp_kernel(offsets, order, *refs):
    blocks = dict(zip(order, refs[:offsets]))
    table_ref, dep_ref, up_ref, down_ref, table = refs[offsets:]
    band_rows, lon, ch = dep_ref.shape
    quads, wide = refs[0].shape
    taps = wide // ch
    weights = table_ref[: taps * band_rows + 8].T
    columns = weights[:, taps * band_rows :].astype(jnp.int32)
    quad_at = lax.broadcasted_iota(jnp.int32, (lon, offsets * quads), 1)
    for offset in range(offsets):
        table[offset * quads : (offset + 1) * quads] = blocks[offset][...]
    for row in range(band_rows):
        tapped = dot(one_hot(quad_at == columns[:, row : row + 1]), table[...])
        line = jnp.zeros((lon, ch), F32)
        for tap in range(taps):
            at = tap * band_rows + row
            line = line + weights[:, at : at + 1] * tapped[:, tap * ch : (tap + 1) * ch]
        dep_ref[row] = line
        if row < 2:
            up_ref[row] = line.astype(BF16)
        if row >= band_rows - 2:
            down_ref[row - band_rows + 2] = line.astype(BF16)


def lon_sum(line):
    lon = line.shape[0]
    return pltpu.roll(line, 1, 0) + pltpu.roll(line, lon - 1, 0)


def gelu_parts(pre):
    square = pre * pre
    curve = jnp.tanh(pre * (GELU_SCALE + (GELU_SCALE * GELU_CUBE) * square))
    share = 0.5 + 0.5 * curve
    act = pre * share
    slope = share + (act - act * share) * (
        2.0 * GELU_SCALE + (6.0 * GELU_SCALE * GELU_CUBE) * square
    )
    return act, slope


def mlp_kernel(
    dep_ref,
    after_ref,
    before_ref,
    cot_ref,
    place_ref,
    table_ref,
    w1_ref,
    w2_ref,
    w3_ref,
    next_ref,
    scaled_ref,
    grads_ref,
    gb1,
    gb2,
    once,
    smooth,
    a1,
    a2,
    p1,
    p2,
):
    band_rows, lon, ch = dep_ref.shape
    hid = w1_ref.shape[1]
    helm, inverse = coefficients(table_ref, TABLE_AT, ch)
    b1 = table_ref[TABLE_AT + 9 : TABLE_AT + 10, :hid]
    b2 = table_ref[TABLE_AT + 10 : TABLE_AT + 11, :hid]

    def departure(row):
        if row < 0:
            return before_ref[row + 2].astype(F32)
        if row >= band_rows:
            return after_ref[row - band_rows].astype(F32)
        return dep_ref[row]

    first = jnp.where(place_ref[0] == 0, 0.0, 1.0)
    last = jnp.where(place_ref[0] == place_ref[1] - 1, 0.0, 1.0)
    ahead = departure(-2) * first, departure(-1) * first
    behind = departure(band_rows) * last, departure(band_rows + 1) * last
    lines = {-2: ahead[0], -1: ahead[1], band_rows: behind[0], band_rows + 1: behind[1]}
    for row in range(-1, band_rows + 1):
        mid, above, below = (
            lines[r] if r in lines else departure(r) for r in (row, row - 1, row + 1)
        )
        value = (mid + helm * (above + below + lon_sum(mid))) * inverse
        if row < 0:
            value = value * first
        if row >= band_rows:
            value = value * last
        once[row + 1] = value
    for row in range(band_rows):
        value = (
            dep_ref[row] + helm * (once[row] + once[row + 2] + lon_sum(once[row + 1]))
        ) * inverse
        smooth[row] = value.astype(BF16)
    gb1[...] = jnp.zeros_like(gb1)
    gb2[...] = jnp.zeros_like(gb2)

    for row in range(band_rows):
        rows = smooth[row]
        cot = cot_ref[row]
        act, slope_first = gelu_parts(dot(rows, w1_ref[...]) + b1)
        act_first = act.astype(BF16)
        act, slope_second = gelu_parts(dot(act_first, w2_ref[...]) + b2)
        act_second = act.astype(BF16)
        next_ref[row] = (rows.astype(F32) + dot(act_second, w3_ref[...])).astype(BF16)
        gpre = dot(cot, w3_ref[...], 1, 1) * slope_second
        gpre_second = gpre.astype(BF16)
        gb2[...] += jnp.sum(gpre_second.astype(F32), axis=0, keepdims=True)
        gpre = dot(gpre_second, w2_ref[...], 1, 1) * slope_first
        gpre_first = gpre.astype(BF16)
        gb1[...] += jnp.sum(gpre_first.astype(F32), axis=0, keepdims=True)
        a1[row], a2[row], p1[row], p2[row] = act_first, act_second, gpre_first, gpre_second
        gsmooth = cot.astype(F32) + dot(gpre_first, w1_ref[...], 1, 1)
        scaled_ref[row] = gsmooth * inverse
    flat = band_rows * lon

    def whole(ref):
        return ref[...].reshape(flat, ref.shape[2])

    g3 = dot(whole(a2), whole(cot_ref), 0, 0).astype(BF16)
    g2 = dot(whole(a1), whole(p2), 0, 0).astype(BF16)
    g1 = dot(whole(smooth), whole(p1), 0, 0).astype(BF16)
    grads_ref[:ch] = g1[:, :ch]
    grads_ref[ch : 2 * ch] = g1[:, ch:]
    grads_ref[2 * ch : 4 * ch] = g2[:, :ch]
    grads_ref[4 * ch : 6 * ch] = g2[:, ch:]
    grads_ref[6 * ch : 8 * ch] = g3
    rest = grads_ref.shape[0] - 8 * ch
    row_at = lax.broadcasted_iota(jnp.int32, (rest, ch), 0)
    tail = jnp.zeros((rest, ch), F32)
    for index, line in enumerate((gb1[:, :ch], gb1[:, ch:], gb2[:, :ch], gb2[:, ch:])):
        tail = jnp.where(row_at == index, line, tail)
    grads_ref[8 * ch :] = tail.astype(BF16)


def edges_kernel(scaled_ref, up_ref, down_ref):
    up_ref[...] = scaled_ref[:2].astype(BF16)
    down_ref[...] = scaled_ref[scaled_ref.shape[0] - 2 :].astype(BF16)


def adjoint_kernel(
    offsets,
    scaled_ref,
    before_ref,
    after_ref,
    place_ref,
    table_ref,
    *refs,
):
    outs, (once, spread, hit) = refs[:offsets], refs[offsets:]
    band_rows, lon, ch = scaled_ref.shape
    quads, wide = outs[0].shape
    taps = wide // ch
    helm, inverse = coefficients(table_ref, TABLE_AT, ch)
    first = jnp.where(place_ref[0] == 0, 0.0, 1.0)
    last = jnp.where(place_ref[0] == place_ref[1] - 1, 0.0, 1.0)
    weights = table_ref[:TABLE_AT].T
    quad_lanes = table_ref[TABLE_AT : TABLE_AT + 8].astype(jnp.int32)
    quad_at = lax.broadcasted_iota(jnp.int32, (offsets * quads, lon), 0)
    for row in range(band_rows):
        hit[:, row * lon : (row + 1) * lon] = one_hot(quad_at == quad_lanes[row : row + 1])

    def scaled(row):
        if row < 0:
            return before_ref[row + 2].astype(F32) * first
        if row >= band_rows:
            return after_ref[row - band_rows].astype(F32) * last
        return scaled_ref[row]

    for row in range(-1, band_rows + 1):
        value = (helm * inverse) * (scaled(row - 1) + scaled(row + 1) + lon_sum(scaled(row)))
        if row < 0:
            value = value * first
        if row >= band_rows:
            value = value * last
        once[row + 1] = value
    for row in range(band_rows):
        value = (
            scaled_ref[row]
            + once[row + 1]
            + helm * (once[row] + once[row + 2] + lon_sum(once[row + 1]))
        )
        for tap in range(taps):
            at = tap * band_rows + row
            spread[row * lon : (row + 1) * lon, tap * ch : (tap + 1) * ch] = (
                weights[:, at : at + 1] * value
            ).astype(BF16)
    slot_grads = dot(hit[...], spread[...]).astype(BF16)
    for offset in range(offsets):
        outs[offset][...] = slot_grads[offset * quads : (offset + 1) * quads]


def scatter_kernel(offsets, cells_ref, count_ref, *refs):
    blocks = refs[:offsets]
    out_ref, done_ref, table, hit = refs[offsets:]
    done_ref[...] = jnp.zeros_like(done_ref)
    band_rows, lon, ch = out_ref.shape
    quads = blocks[0].shape[0]
    box_at = lax.broadcasted_iota(jnp.int32, ((band_rows - 1) * lon, quads), 0)
    for offset in range(offsets):
        table[offset * quads : (offset + 1) * quads] = jnp.where(
            live_quads(count_ref, offset, quads), blocks[offset][...].astype(F32), 0.0
        ).astype(BF16)
        hit[:, offset * quads : (offset + 1) * quads] = one_hot(
            box_at == cells_ref[offset : offset + 1]
        )
    for row in range(band_rows):
        here = jnp.zeros((lon, ch), F32)
        right = jnp.zeros((lon, ch), F32)
        if row < band_rows - 1:
            both = dot(hit[row * lon : (row + 1) * lon], table[:, : 2 * ch])
            here = here + both[:, :ch]
            right = right + both[:, ch:]
        if row > 0:
            both = dot(hit[(row - 1) * lon : row * lon], table[:, 2 * ch :])
            here = here + both[:, :ch]
            right = right + both[:, ch:]
        out_ref[row] = here + pltpu.roll(right, 1, 0)


def sum_kernel(copies, parts_ref, *refs):
    out_ref = refs[-1]
    total = parts_ref[0].astype(F32)
    for part in range(1, parts_ref.shape[0]):
        total = total + parts_ref[part].astype(F32)
    total = total.astype(BF16)
    for copy in range(copies):
        out_ref[copy] = total


def unpack_kernel(sums_ref, ahead_ref, g1, gb1, g2, gb2, g3):
    ch, hid = g1.shape
    g1[:, :ch] = sums_ref[:ch].astype(F32)
    g1[:, ch:] = sums_ref[ch : 2 * ch].astype(F32)
    g2[:, :ch] = sums_ref[2 * ch : 4 * ch].astype(F32)
    g2[:, ch:] = sums_ref[4 * ch : 6 * ch].astype(F32)
    g3[...] = sums_ref[6 * ch : 8 * ch].astype(F32)
    tail = sums_ref[8 * ch : 8 * ch + 8].astype(F32)
    gb1[:, :ch], gb1[:, ch:] = tail[0:1], tail[1:2]
    gb2[:, :ch], gb2[:, ch:] = tail[2:3], tail[3:4]


def shifted(block, by, count):
    return lax.ppermute(block, SPACE, [(i, (i + by) % count) for i in range(count)])


def body(
    field,
    send_rows,
    send_count,
    dep_slot,
    dep_weight,
    helm_coef,
    w_first,
    b_first,
    w_second,
    b_second,
    w_third,
    cotangent,
):
    _, band_rows, lon, ch = field.shape
    hid = w_first.shape[1]
    offsets, slots = send_rows.shape[1:]
    taps = dep_slot.shape[0]
    reach = (offsets - 1) // 2
    quads = slots // 4
    bands = lax.axis_size(SPACE)
    shape = jax.ShapeDtypeStruct
    place = jnp.stack([lax.axis_index(SPACE).astype(jnp.int32), jnp.int32(bands)])
    block = shape((quads, taps * ch), BF16)
    edge = shape((2, lon, ch), BF16)

    cells, select = call(
        choose_kernel,
        [
            shape((8, quads), jnp.int32),
            shape((offsets * quads, (band_rows - 1) * lon), BF16),
        ],
        [VMEM],
        [pltpu.VMEM((8, slots), jnp.int32)],
        flops=CHOOSE_COST,
        name="choose",
    )(jnp.transpose(send_rows, (1, 0, 2)))
    packed = call(
        functools.partial(pack_kernel, offsets),
        [block] * offsets,
        [VMEM] * 3,
        [pltpu.VMEM((band_rows * lon, 2 * ch), BF16)],
        name="pack",
    )(field[0], select, send_count)
    received = [
        packed[e] if e == reach else shifted(packed[e], e - reach, bands)
        for e in range(offsets)
    ]
    order = sorted(range(offsets), key=lambda e: -abs(e - reach))
    (table,) = call(
        prepare_kernel,
        [shape((TABLE_AT + 16, lon), F32)],
        [VMEM] * 5,
        flops=PREPARE_COST,
        name="prepare",
    )(
        dep_slot,
        dep_weight,
        helm_coef.reshape(1, ch),
        b_first.reshape(1, hid),
        b_second.reshape(1, hid),
    )
    departure, up, down = call(
        functools.partial(interp_kernel, offsets, order),
        [shape((band_rows, lon, ch), F32), edge, edge],
        [VMEM] * (offsets + 1),
        [pltpu.VMEM((offsets * quads, taps * ch), BF16)],
        name="interp",
    )(*(received[e] for e in order), table)
    after = shifted(up, -1, bands)
    before = shifted(down, 1, bands)
    groups = ("y", "x", "core")
    group = lax.axis_size(groups)
    depth = lax.axis_size("z")
    next_state, scaled, grads = call(
        mlp_kernel,
        [
            shape((band_rows, lon, ch), BF16),
            shape((band_rows, lon, ch), F32),
            shape((group * PART_ROWS, ch), BF16),
        ],
        [VMEM] * 4 + [SMEM] + [VMEM] * 4,
        [
            pltpu.VMEM((1, hid), F32),
            pltpu.VMEM((1, hid), F32),
            pltpu.VMEM((band_rows + 2, lon, ch), F32),
            pltpu.VMEM((band_rows, lon, ch), BF16),
        ]
        + [pltpu.VMEM((band_rows, lon, hid), BF16)] * 4,
        name="smooth_mlp",
    )(departure, after, before, cotangent[0], place, table, w_first, w_second, w_third)
    up, down = call(edges_kernel, [edge, edge], [VMEM], name="edges")(scaled)
    after = shifted(up, -1, bands)
    before = shifted(down, 1, bands)

    parts = lax.all_to_all(grads.reshape(group, PART_ROWS, ch), groups, 0, 0)
    slot_grads = call(
        functools.partial(adjoint_kernel, offsets),
        [block] * offsets,
        [VMEM] * 3 + [SMEM, VMEM],
        [
            pltpu.VMEM((band_rows + 2, lon, ch), F32),
            pltpu.VMEM((band_rows * lon, taps * ch), BF16),
            pltpu.VMEM((offsets * quads, band_rows * lon), BF16),
        ],
        flops=ADJOINT_COST,
        name="adjoint",
    )(scaled, before, after, place, table)
    (part_sum,) = call(
        functools.partial(sum_kernel, depth),
        [shape((depth, PART_ROWS, ch), BF16)],
        [VMEM],
        flops=PART_COST,
        name="part_sum",
    )(parts)
    parts = lax.all_to_all(part_sum, "z", 0, 0)
    back = [
        slot_grads[e] if e == reach else shifted(slot_grads[e], reach - e, bands)
        for e in range(offsets)
    ]
    field_grad, done = call(
        functools.partial(scatter_kernel, offsets),
        [shape((band_rows, lon, ch), F32), shape((8, ch), F32)],
        [VMEM] * (offsets + 2),
        [
            pltpu.VMEM((offsets * quads, taps * ch), BF16),
            pltpu.VMEM(((band_rows - 1) * lon, offsets * quads), BF16),
        ],
        flops=SCATTER_COST,
        name="scatter",
    )(cells, send_count, *back)
    (whole_sum,) = call(
        functools.partial(sum_kernel, group),
        [shape((group, PART_ROWS, ch), BF16)],
        [VMEM, ANY],
        name="whole_sum",
    )(parts, slot_grads[reach])
    sums = lax.all_to_all(whole_sum, groups, 0, 0).reshape(group * PART_ROWS, ch)
    grad_shapes = [
        shape((ch, hid), F32),
        shape((1, hid), F32),
        shape((hid, hid), F32),
        shape((1, hid), F32),
        shape((hid, ch), F32),
    ]
    grads = call(
        unpack_kernel,
        grad_shapes,
        [VMEM, ANY],
        name="unpack",
    )(sums, done)
    return (
        next_state[None],
        field_grad[None],
        grads[0],
        grads[1].reshape(hid),
        grads[2],
        grads[3].reshape(hid),
        grads[4],
    )


def solution(mesh):
    fine = Mesh(mesh.devices.reshape(4, 8, 4, 2), ("y",) + SPACE)
    state = P("y", SPACE, None, None)
    return jax.shard_map(
        body,
        mesh=fine,
        in_specs=(
            state,
            P(SPACE, None, None),
            P(SPACE, None),
            P(None, SPACE, None),
            P(None, SPACE, None),
            P(),
            P(),
            P(),
            P(),
            P(),
            P(),
            state,
        ),
        out_specs=(state, state, P(), P(), P(), P(), P()),
        check_vma=False,
    )
```

```python
import functools
import math

import jax
import jax.numpy as jnp
from jax import lax
from jax.experimental import pallas as pl
from jax.experimental.pallas import tpu as pltpu
from jax.sharding import Mesh
from jax.sharding import PartitionSpec as P

F32 = jnp.float32
BF16 = jnp.bfloat16
SPACE = ("z", "x", "core")
GELU_SCALE = math.sqrt(2.0 / math.pi)
GELU_CUBE = 0.044715
PART_ROWS = 40
TABLE_AT = 16
PREPARE_COST = 10**9
PART_COST = 0
ADJOINT_COST = 10**11
SCATTER_COST = 0
CHOOSE_COST = 2 * 10**9

VMEM = pl.BlockSpec(memory_space=pltpu.VMEM)
ANY = pl.BlockSpec(memory_space=pl.ANY)
SMEM = pl.BlockSpec(memory_space=pltpu.SMEM)


def dot(left, right, left_dim=1, right_dim=0):
    return lax.dot_general(
        left,
        right,
        (((left_dim,), (right_dim,)), ((), ())),
        preferred_element_type=F32,
    )


def call(kernel, outs, ins, scratch=(), flops=0, name=None):
    nbytes = sum(math.prod(o.shape) * o.dtype.itemsize for o in outs)
    return pl.pallas_call(
        kernel,
        out_shape=outs,
        in_specs=ins,
        out_specs=[VMEM] * len(outs),
        scratch_shapes=list(scratch),
        compiler_params=pltpu.CompilerParams(vmem_limit_bytes=32 * 1024 * 1024),
        cost_estimate=pl.CostEstimate(
            flops=flops, bytes_accessed=2 * nbytes, transcendentals=0
        ),
        name=name,
    )


def quad_boxes(index, quads):
    pick = one_hot(
        lax.broadcasted_iota(jnp.int32, (4 * quads, quads), 0)
        == 4 * lax.broadcasted_iota(jnp.int32, (4 * quads, quads), 1)
    )
    high = (index >> 3).astype(F32).astype(BF16)
    low = (index & 7).astype(F32).astype(BF16)
    return (dot(high, pick) * 8.0 + dot(low, pick)).astype(jnp.int32)


def live_quads(count_ref, offset, quads):
    slot_at = 4 * lax.broadcasted_iota(jnp.int32, (quads, 1), 0)
    return slot_at < count_ref[:, offset : offset + 1]


def one_hot(mask):
    return mask.astype(F32).astype(BF16)


def choose_kernel(rows_ref, cells_ref, select_ref, index):
    quads = cells_ref.shape[1]
    offsets = rows_ref.shape[0]
    index[...] = jnp.zeros_like(index)
    for offset in range(offsets):
        index[offset : offset + 1] = rows_ref[offset]
    cells = quad_boxes(index[...], quads)
    cells_ref[...] = cells
    columns = cells.astype(F32).T.astype(jnp.int32)
    box_at = lax.broadcasted_iota(jnp.int32, (quads, select_ref.shape[1]), 1)
    for offset in range(offsets):
        select_ref[offset * quads : (offset + 1) * quads] = one_hot(
            box_at == columns[:, offset : offset + 1]
        )


def pack_kernel(offsets, field_ref, select_ref, count_ref, *refs):
    outs, pair = refs[:offsets], refs[offsets]
    band_rows, lon, ch = field_ref.shape
    quads = outs[0].shape[0]
    boxes = (band_rows - 1) * lon
    for row in range(band_rows):
        line = field_ref[row]
        pair[row * lon : (row + 1) * lon, :ch] = line
        pair[row * lon : (row + 1) * lon, ch:] = pltpu.roll(
            line.astype(F32), lon - 1, 0
        ).astype(BF16)
    for part in range(2):
        picked = dot(select_ref[...], pair[part * lon : part * lon + boxes])
        for offset in range(offsets):
            outs[offset][:, part * 2 * ch : (part + 1) * 2 * ch] = jnp.where(
                live_quads(count_ref, offset, quads),
                picked[offset * quads : (offset + 1) * quads],
                0.0,
            ).astype(BF16)


def prepare_kernel(slot_ref, weight_ref, helm_ref, b1_ref, b2_ref, table_ref):
    taps, band_rows, lon = weight_ref.shape
    ch = helm_ref.shape[1]
    hid = b1_ref.shape[1]
    table_ref[...] = jnp.zeros_like(table_ref)
    for tap in range(taps):
        table_ref[tap * band_rows : (tap + 1) * band_rows] = weight_ref[tap]
    at = taps * band_rows
    table_ref[at : at + band_rows] = (slot_ref[0] >> 2).astype(F32)
    helm = helm_ref[...]
    table_ref[at + 8 : at + 9, :ch] = helm
    table_ref[at + 8 : at + 9, ch : 2 * ch] = 1.0 / (1.0 + 4.0 * helm)
    table_ref[at + 9 : at + 10, :hid] = b1_ref[...]
    table_ref[at + 10 : at + 11, :hid] = b2_ref[...]


def coefficients(table_ref, at, ch):
    return table_ref[at + 8 : at + 9, :ch], table_ref[at + 8 : at + 9, ch : 2 * ch]


def interp_kernel(offsets, order, *refs):
    blocks = dict(zip(order, refs[:offsets]))
    table_ref, dep_ref, up_ref, down_ref, table = refs[offsets:]
    band_rows, lon, ch = dep_ref.shape
    quads, wide = refs[0].shape
    taps = wide // ch
    weights = table_ref[: taps * band_rows + 8].T
    columns = weights[:, taps * band_rows :].astype(jnp.int32)
    quad_at = lax.broadcasted_iota(jnp.int32, (lon, offsets * quads), 1)
    for offset in range(offsets):
        table[offset * quads : (offset + 1) * quads] = blocks[offset][...]
    for row in range(band_rows):
        tapped = dot(one_hot(quad_at == columns[:, row : row + 1]), table[...])
        line = jnp.zeros((lon, ch), F32)
        for tap in range(taps):
            at = tap * band_rows + row
            line = line + weights[:, at : at + 1] * tapped[:, tap * ch : (tap + 1) * ch]
        dep_ref[row] = line
        if row < 2:
            up_ref[row] = line.astype(BF16)
        if row >= band_rows - 2:
            down_ref[row - band_rows + 2] = line.astype(BF16)


def lon_sum(line):
    lon = line.shape[0]
    return pltpu.roll(line, 1, 0) + pltpu.roll(line, lon - 1, 0)


def gelu_parts(pre):
    square = pre * pre
    curve = jnp.tanh(pre * (GELU_SCALE + (GELU_SCALE * GELU_CUBE) * square))
    share = 0.5 + 0.5 * curve
    act = pre * share
    slope = share + (act - act * share) * (
        2.0 * GELU_SCALE + (6.0 * GELU_SCALE * GELU_CUBE) * square
    )
    return act, slope


def mlp_kernel(
    dep_ref,
    after_ref,
    before_ref,
    cot_ref,
    place_ref,
    table_ref,
    w1_ref,
    w2_ref,
    w3_ref,
    next_ref,
    scaled_ref,
    grads_ref,
    gb1,
    gb2,
    once,
    smooth,
    a1,
    a2,
    p1,
    p2,
):
    band_rows, lon, ch = dep_ref.shape
    hid = w1_ref.shape[1]
    helm, inverse = coefficients(table_ref, TABLE_AT, ch)
    b1 = table_ref[TABLE_AT + 9 : TABLE_AT + 10, :hid]
    b2 = table_ref[TABLE_AT + 10 : TABLE_AT + 11, :hid]

    def departure(row):
        if row < 0:
            return before_ref[row + 2].astype(F32)
        if row >= band_rows:
            return after_ref[row - band_rows].astype(F32)
        return dep_ref[row]

    first = jnp.where(place_ref[0] == 0, 0.0, 1.0)
    last = jnp.where(place_ref[0] == place_ref[1] - 1, 0.0, 1.0)
    ahead = departure(-2) * first, departure(-1) * first
    behind = departure(band_rows) * last, departure(band_rows + 1) * last
    lines = {-2: ahead[0], -1: ahead[1], band_rows: behind[0], band_rows + 1: behind[1]}
    for row in range(-1, band_rows + 1):
        mid, above, below = (
            lines[r] if r in lines else departure(r) for r in (row, row - 1, row + 1)
        )
        value = (mid + helm * (above + below + lon_sum(mid))) * inverse
        if row < 0:
            value = value * first
        if row >= band_rows:
            value = value * last
        once[row + 1] = value
    for row in range(band_rows):
        value = (
            dep_ref[row] + helm * (once[row] + once[row + 2] + lon_sum(once[row + 1]))
        ) * inverse
        smooth[row] = value.astype(BF16)
    gb1[...] = jnp.zeros_like(gb1)
    gb2[...] = jnp.zeros_like(gb2)

    for row in range(band_rows):
        rows = smooth[row]
        cot = cot_ref[row]
        act, slope_first = gelu_parts(dot(rows, w1_ref[...]) + b1)
        act_first = act.astype(BF16)
        act, slope_second = gelu_parts(dot(act_first, w2_ref[...]) + b2)
        act_second = act.astype(BF16)
        next_ref[row] = (rows.astype(F32) + dot(act_second, w3_ref[...])).astype(BF16)
        gpre = dot(cot, w3_ref[...], 1, 1) * slope_second
        gpre_second = gpre.astype(BF16)
        gb2[...] += jnp.sum(gpre_second.astype(F32), axis=0, keepdims=True)
        gpre = dot(gpre_second, w2_ref[...], 1, 1) * slope_first
        gpre_first = gpre.astype(BF16)
        gb1[...] += jnp.sum(gpre_first.astype(F32), axis=0, keepdims=True)
        a1[row], a2[row], p1[row], p2[row] = act_first, act_second, gpre_first, gpre_second
        gsmooth = cot.astype(F32) + dot(gpre_first, w1_ref[...], 1, 1)
        scaled_ref[row] = gsmooth * inverse
    flat = band_rows * lon

    def whole(ref):
        return ref[...].reshape(flat, ref.shape[2])

    g3 = dot(whole(a2), whole(cot_ref), 0, 0).astype(BF16)
    g2 = dot(whole(a1), whole(p2), 0, 0).astype(BF16)
    g1 = dot(whole(smooth), whole(p1), 0, 0).astype(BF16)
    grads_ref[:ch] = g1[:, :ch]
    grads_ref[ch : 2 * ch] = g1[:, ch:]
    grads_ref[2 * ch : 4 * ch] = g2[:, :ch]
    grads_ref[4 * ch : 6 * ch] = g2[:, ch:]
    grads_ref[6 * ch : 8 * ch] = g3
    rest = grads_ref.shape[0] - 8 * ch
    row_at = lax.broadcasted_iota(jnp.int32, (rest, ch), 0)
    tail = jnp.zeros((rest, ch), F32)
    for index, line in enumerate((gb1[:, :ch], gb1[:, ch:], gb2[:, :ch], gb2[:, ch:])):
        tail = jnp.where(row_at == index, line, tail)
    grads_ref[8 * ch :] = tail.astype(BF16)


def edges_kernel(scaled_ref, up_ref, down_ref):
    up_ref[...] = scaled_ref[:2].astype(BF16)
    down_ref[...] = scaled_ref[scaled_ref.shape[0] - 2 :].astype(BF16)


def adjoint_kernel(
    offsets,
    scaled_ref,
    before_ref,
    after_ref,
    place_ref,
    table_ref,
    *refs,
):
    outs, (once, spread, hit) = refs[:offsets], refs[offsets:]
    band_rows, lon, ch = scaled_ref.shape
    quads, wide = outs[0].shape
    taps = wide // ch
    helm, inverse = coefficients(table_ref, TABLE_AT, ch)
    first = jnp.where(place_ref[0] == 0, 0.0, 1.0)
    last = jnp.where(place_ref[0] == place_ref[1] - 1, 0.0, 1.0)
    weights = table_ref[:TABLE_AT].T
    quad_lanes = table_ref[TABLE_AT : TABLE_AT + 8].astype(jnp.int32)
    quad_at = lax.broadcasted_iota(jnp.int32, (offsets * quads, lon), 0)
    for row in range(band_rows):
        hit[:, row * lon : (row + 1) * lon] = one_hot(quad_at == quad_lanes[row : row + 1])

    def scaled(row):
        if row < 0:
            return before_ref[row + 2].astype(F32) * first
        if row >= band_rows:
            return after_ref[row - band_rows].astype(F32) * last
        return scaled_ref[row]

    for row in range(-1, band_rows + 1):
        value = (helm * inverse) * (scaled(row - 1) + scaled(row + 1) + lon_sum(scaled(row)))
        if row < 0:
            value = value * first
        if row >= band_rows:
            value = value * last
        once[row + 1] = value
    for row in range(band_rows):
        value = (
            scaled_ref[row]
            + once[row + 1]
            + helm * (once[row] + once[row + 2] + lon_sum(once[row + 1]))
        )
        for tap in range(taps):
            at = tap * band_rows + row
            spread[row * lon : (row + 1) * lon, tap * ch : (tap + 1) * ch] = (
                weights[:, at : at + 1] * value
            ).astype(BF16)
    slot_grads = dot(hit[...], spread[...]).astype(BF16)
    for offset in range(offsets):
        outs[offset][...] = slot_grads[offset * quads : (offset + 1) * quads]


def scatter_kernel(offsets, cells_ref, count_ref, *refs):
    blocks = refs[:offsets]
    out_ref, done_ref, table, hit = refs[offsets:]
    done_ref[...] = jnp.zeros_like(done_ref)
    band_rows, lon, ch = out_ref.shape
    quads = blocks[0].shape[0]
    box_at = lax.broadcasted_iota(jnp.int32, ((band_rows - 1) * lon, quads), 0)
    for offset in range(offsets):
        table[offset * quads : (offset + 1) * quads] = jnp.where(
            live_quads(count_ref, offset, quads), blocks[offset][...].astype(F32), 0.0
        ).astype(BF16)
        hit[:, offset * quads : (offset + 1) * quads] = one_hot(
            box_at == cells_ref[offset : offset + 1]
        )
    for row in range(band_rows):
        here = jnp.zeros((lon, ch), F32)
        right = jnp.zeros((lon, ch), F32)
        if row < band_rows - 1:
            both = dot(hit[row * lon : (row + 1) * lon], table[:, : 2 * ch])
            here = here + both[:, :ch]
            right = right + both[:, ch:]
        if row > 0:
            both = dot(hit[(row - 1) * lon : row * lon], table[:, 2 * ch :])
            here = here + both[:, :ch]
            right = right + both[:, ch:]
        out_ref[row] = here + pltpu.roll(right, 1, 0)


def sum_kernel(copies, parts_ref, *refs):
    out_ref = refs[-1]
    total = parts_ref[0].astype(F32)
    for part in range(1, parts_ref.shape[0]):
        total = total + parts_ref[part].astype(F32)
    total = total.astype(BF16)
    for copy in range(copies):
        out_ref[copy] = total


def unpack_kernel(sums_ref, ahead_ref, g1, gb1, g2, gb2, g3):
    ch, hid = g1.shape
    g1[:, :ch] = sums_ref[:ch].astype(F32)
    g1[:, ch:] = sums_ref[ch : 2 * ch].astype(F32)
    g2[:, :ch] = sums_ref[2 * ch : 4 * ch].astype(F32)
    g2[:, ch:] = sums_ref[4 * ch : 6 * ch].astype(F32)
    g3[...] = sums_ref[6 * ch : 8 * ch].astype(F32)
    tail = sums_ref[8 * ch : 8 * ch + 8].astype(F32)
    gb1[:, :ch], gb1[:, ch:] = tail[0:1], tail[1:2]
    gb2[:, :ch], gb2[:, ch:] = tail[2:3], tail[3:4]


def shifted(block, by, count):
    return lax.ppermute(block, SPACE, [(i, (i + by) % count) for i in range(count)])


def body(
    field,
    send_rows,
    send_count,
    dep_slot,
    dep_weight,
    helm_coef,
    w_first,
    b_first,
    w_second,
    b_second,
    w_third,
    cotangent,
):
    _, band_rows, lon, ch = field.shape
    hid = w_first.shape[1]
    offsets, slots = send_rows.shape[1:]
    taps = dep_slot.shape[0]
    reach = (offsets - 1) // 2
    quads = slots // 4
    bands = lax.axis_size(SPACE)
    shape = jax.ShapeDtypeStruct
    place = jnp.stack([lax.axis_index(SPACE).astype(jnp.int32), jnp.int32(bands)])
    block = shape((quads, taps * ch), BF16)
    edge = shape((2, lon, ch), BF16)

    cells, select = call(
        choose_kernel,
        [
            shape((8, quads), jnp.int32),
            shape((offsets * quads, (band_rows - 1) * lon), BF16),
        ],
        [VMEM],
        [pltpu.VMEM((8, slots), jnp.int32)],
        flops=CHOOSE_COST,
        name="choose",
    )(jnp.transpose(send_rows, (1, 0, 2)))
    packed = call(
        functools.partial(pack_kernel, offsets),
        [block] * offsets,
        [VMEM] * 3,
        [pltpu.VMEM((band_rows * lon, 2 * ch), BF16)],
        name="pack",
    )(field[0], select, send_count)
    received = [
        packed[e] if e == reach else shifted(packed[e], e - reach, bands)
        for e in range(offsets)
    ]
    order = sorted(range(offsets), key=lambda e: -abs(e - reach))
    (table,) = call(
        prepare_kernel,
        [shape((TABLE_AT + 16, lon), F32)],
        [VMEM] * 5,
        flops=PREPARE_COST,
        name="prepare",
    )(
        dep_slot,
        dep_weight,
        helm_coef.reshape(1, ch),
        b_first.reshape(1, hid),
        b_second.reshape(1, hid),
    )
    departure, up, down = call(
        functools.partial(interp_kernel, offsets, order),
        [shape((band_rows, lon, ch), F32), edge, edge],
        [VMEM] * (offsets + 1),
        [pltpu.VMEM((offsets * quads, taps * ch), BF16)],
        name="interp",
    )(*(received[e] for e in order), table)
    after = shifted(up, -1, bands)
    before = shifted(down, 1, bands)
    groups = ("y", "x", "core")
    group = lax.axis_size(groups)
    depth = lax.axis_size("z")
    next_state, scaled, grads = call(
        mlp_kernel,
        [
            shape((band_rows, lon, ch), BF16),
            shape((band_rows, lon, ch), F32),
            shape((group * PART_ROWS, ch), BF16),
        ],
        [VMEM] * 4 + [SMEM] + [VMEM] * 4,
        [
            pltpu.VMEM((1, hid), F32),
            pltpu.VMEM((1, hid), F32),
            pltpu.VMEM((band_rows + 2, lon, ch), F32),
            pltpu.VMEM((band_rows, lon, ch), BF16),
        ]
        + [pltpu.VMEM((band_rows, lon, hid), BF16)] * 4,
        name="smooth_mlp",
    )(departure, after, before, cotangent[0], place, table, w_first, w_second, w_third)
    up, down = call(edges_kernel, [edge, edge], [VMEM], name="edges")(scaled)
    after = shifted(up, -1, bands)
    before = shifted(down, 1, bands)

    parts = lax.all_to_all(grads.reshape(group, PART_ROWS, ch), groups, 0, 0)
    slot_grads = call(
        functools.partial(adjoint_kernel, offsets),
        [block] * offsets,
        [VMEM] * 3 + [SMEM, VMEM],
        [
            pltpu.VMEM((band_rows + 2, lon, ch), F32),
            pltpu.VMEM((band_rows * lon, taps * ch), BF16),
            pltpu.VMEM((offsets * quads, band_rows * lon), BF16),
        ],
        flops=ADJOINT_COST,
        name="adjoint",
    )(scaled, before, after, place, table)
    (part_sum,) = call(
        functools.partial(sum_kernel, depth),
        [shape((depth, PART_ROWS, ch), BF16)],
        [VMEM],
        flops=PART_COST,
        name="part_sum",
    )(parts)
    parts = lax.all_to_all(part_sum, "z", 0, 0)
    back = [
        slot_grads[e] if e == reach else shifted(slot_grads[e], reach - e, bands)
        for e in range(offsets)
    ]
    field_grad, done = call(
        functools.partial(scatter_kernel, offsets),
        [shape((band_rows, lon, ch), F32), shape((8, ch), F32)],
        [VMEM] * (offsets + 2),
        [
            pltpu.VMEM((offsets * quads, taps * ch), BF16),
            pltpu.VMEM(((band_rows - 1) * lon, offsets * quads), BF16),
        ],
        flops=SCATTER_COST,
        name="scatter",
    )(cells, send_count, *back)
    (whole_sum,) = call(
        functools.partial(sum_kernel, group),
        [shape((group, PART_ROWS, ch), BF16)],
        [VMEM, ANY],
        name="whole_sum",
    )(parts, slot_grads[reach])
    sums = lax.all_to_all(whole_sum, groups, 0, 0).reshape(group * PART_ROWS, ch)
    grad_shapes = [
        shape((ch, hid), F32),
        shape((1, hid), F32),
        shape((hid, hid), F32),
        shape((1, hid), F32),
        shape((hid, ch), F32),
    ]
    grads = call(
        unpack_kernel,
        grad_shapes,
        [VMEM, ANY],
        name="unpack",
    )(sums, done)
    return (
        next_state[None],
        field_grad[None],
        grads[0],
        grads[1].reshape(hid),
        grads[2],
        grads[3].reshape(hid),
        grads[4],
    )


def solution(mesh):
    fine = Mesh(mesh.devices.reshape(4, 8, 4, 2), ("y",) + SPACE)
    state = P("y", SPACE, None, None)
    return jax.shard_map(
        body,
        mesh=fine,
        in_specs=(
            state,
            P(SPACE, None, None),
            P(SPACE, None),
            P(None, SPACE, None),
            P(None, SPACE, None),
            P(),
            P(),
            P(),
            P(),
            P(),
            P(),
            state,
        ),
        out_specs=(state, state, P(), P(), P(), P(), P()),
        check_vma=False,
    )
```

```python
import functools
import math

import jax
import jax.numpy as jnp
from jax import lax
from jax.experimental import pallas as pl
from jax.experimental.pallas import tpu as pltpu
from jax.sharding import Mesh
from jax.sharding import PartitionSpec as P

F32 = jnp.float32
BF16 = jnp.bfloat16
SPACE = ("z", "x", "core")
GELU_SCALE = math.sqrt(2.0 / math.pi)
GELU_CUBE = 0.044715
PART_ROWS = 40
TABLE_AT = 16
PREPARE_COST = 10**9
PART_COST = 0
ADJOINT_COST = 10**11
SCATTER_COST = 10**11
CHOOSE_COST = 2 * 10**9

VMEM = pl.BlockSpec(memory_space=pltpu.VMEM)
ANY = pl.BlockSpec(memory_space=pl.ANY)
SMEM = pl.BlockSpec(memory_space=pltpu.SMEM)


def dot(left, right, left_dim=1, right_dim=0):
    return lax.dot_general(
        left,
        right,
        (((left_dim,), (right_dim,)), ((), ())),
        preferred_element_type=F32,
    )


def call(kernel, outs, ins, scratch=(), flops=0, name=None):
    nbytes = sum(math.prod(o.shape) * o.dtype.itemsize for o in outs)
    return pl.pallas_call(
        kernel,
        out_shape=outs,
        in_specs=ins,
        out_specs=[VMEM] * len(outs),
        scratch_shapes=list(scratch),
        compiler_params=pltpu.CompilerParams(vmem_limit_bytes=32 * 1024 * 1024),
        cost_estimate=pl.CostEstimate(
            flops=flops, bytes_accessed=2 * nbytes, transcendentals=0
        ),
        name=name,
    )


def quad_boxes(index, quads):
    pick = one_hot(
        lax.broadcasted_iota(jnp.int32, (4 * quads, quads), 0)
        == 4 * lax.broadcasted_iota(jnp.int32, (4 * quads, quads), 1)
    )
    high = (index >> 3).astype(F32).astype(BF16)
    low = (index & 7).astype(F32).astype(BF16)
    return (dot(high, pick) * 8.0 + dot(low, pick)).astype(jnp.int32)


def live_quads(count_ref, offset, quads):
    slot_at = 4 * lax.broadcasted_iota(jnp.int32, (quads, 1), 0)
    return slot_at < count_ref[:, offset : offset + 1]


def one_hot(mask):
    return mask.astype(F32).astype(BF16)


def choose_kernel(rows_ref, cells_ref, select_ref, index):
    quads = cells_ref.shape[1]
    offsets = rows_ref.shape[0]
    index[...] = jnp.zeros_like(index)
    for offset in range(offsets):
        index[offset : offset + 1] = rows_ref[offset]
    cells = quad_boxes(index[...], quads)
    cells_ref[...] = cells
    columns = cells.astype(F32).T.astype(jnp.int32)
    box_at = lax.broadcasted_iota(jnp.int32, (quads, select_ref.shape[1]), 1)
    for offset in range(offsets):
        select_ref[offset * quads : (offset + 1) * quads] = one_hot(
            box_at == columns[:, offset : offset + 1]
        )


def pack_kernel(offsets, field_ref, select_ref, count_ref, *refs):
    outs, pair = refs[:offsets], refs[offsets]
    band_rows, lon, ch = field_ref.shape
    quads = outs[0].shape[0]
    boxes = (band_rows - 1) * lon
    for row in range(band_rows):
        line = field_ref[row]
        pair[row * lon : (row + 1) * lon, :ch] = line
        pair[row * lon : (row + 1) * lon, ch:] = pltpu.roll(
            line.astype(F32), lon - 1, 0
        ).astype(BF16)
    for part in range(2):
        picked = dot(select_ref[...], pair[part * lon : part * lon + boxes])
        for offset in range(offsets):
            outs[offset][:, part * 2 * ch : (part + 1) * 2 * ch] = jnp.where(
                live_quads(count_ref, offset, quads),
                picked[offset * quads : (offset + 1) * quads],
                0.0,
            ).astype(BF16)


def prepare_kernel(slot_ref, weight_ref, helm_ref, b1_ref, b2_ref, table_ref):
    taps, band_rows, lon = weight_ref.shape
    ch = helm_ref.shape[1]
    hid = b1_ref.shape[1]
    table_ref[...] = jnp.zeros_like(table_ref)
    for tap in range(taps):
        table_ref[tap * band_rows : (tap + 1) * band_rows] = weight_ref[tap]
    at = taps * band_rows
    table_ref[at : at + band_rows] = (slot_ref[0] >> 2).astype(F32)
    helm = helm_ref[...]
    table_ref[at + 8 : at + 9, :ch] = helm
    table_ref[at + 8 : at + 9, ch : 2 * ch] = 1.0 / (1.0 + 4.0 * helm)
    table_ref[at + 9 : at + 10, :hid] = b1_ref[...]
    table_ref[at + 10 : at + 11, :hid] = b2_ref[...]


def coefficients(table_ref, at, ch):
    return table_ref[at + 8 : at + 9, :ch], table_ref[at + 8 : at + 9, ch : 2 * ch]


def interp_kernel(offsets, order, *refs):
    blocks = dict(zip(order, refs[:offsets]))
    table_ref, dep_ref, up_ref, down_ref, table = refs[offsets:]
    band_rows, lon, ch = dep_ref.shape
    quads, wide = refs[0].shape
    taps = wide // ch
    weights = table_ref[: taps * band_rows + 8].T
    columns = weights[:, taps * band_rows :].astype(jnp.int32)
    quad_at = lax.broadcasted_iota(jnp.int32, (lon, offsets * quads), 1)
    for offset in range(offsets):
        table[offset * quads : (offset + 1) * quads] = blocks[offset][...]
    for row in range(band_rows):
        tapped = dot(one_hot(quad_at == columns[:, row : row + 1]), table[...])
        line = jnp.zeros((lon, ch), F32)
        for tap in range(taps):
            at = tap * band_rows + row
            line = line + weights[:, at : at + 1] * tapped[:, tap * ch : (tap + 1) * ch]
        dep_ref[row] = line
        if row < 2:
            up_ref[row] = line.astype(BF16)
        if row >= band_rows - 2:
            down_ref[row - band_rows + 2] = line.astype(BF16)


def lon_sum(line):
    lon = line.shape[0]
    return pltpu.roll(line, 1, 0) + pltpu.roll(line, lon - 1, 0)


def gelu_parts(pre):
    square = pre * pre
    curve = jnp.tanh(pre * (GELU_SCALE + (GELU_SCALE * GELU_CUBE) * square))
    share = 0.5 + 0.5 * curve
    act = pre * share
    slope = share + (act - act * share) * (
        2.0 * GELU_SCALE + (6.0 * GELU_SCALE * GELU_CUBE) * square
    )
    return act, slope


def mlp_kernel(
    dep_ref,
    after_ref,
    before_ref,
    cot_ref,
    place_ref,
    table_ref,
    w1_ref,
    w2_ref,
    w3_ref,
    next_ref,
    scaled_ref,
    up_ref,
    down_ref,
    grads_ref,
    gb1,
    gb2,
    once,
    smooth,
    a1,
    a2,
    p1,
    p2,
):
    band_rows, lon, ch = dep_ref.shape
    hid = w1_ref.shape[1]
    helm, inverse = coefficients(table_ref, TABLE_AT, ch)
    b1 = table_ref[TABLE_AT + 9 : TABLE_AT + 10, :hid]
    b2 = table_ref[TABLE_AT + 10 : TABLE_AT + 11, :hid]

    def departure(row):
        if row < 0:
            return before_ref[row + 2].astype(F32)
        if row >= band_rows:
            return after_ref[row - band_rows].astype(F32)
        return dep_ref[row]

    first = jnp.where(place_ref[0] == 0, 0.0, 1.0)
    last = jnp.where(place_ref[0] == place_ref[1] - 1, 0.0, 1.0)
    ahead = departure(-2) * first, departure(-1) * first
    behind = departure(band_rows) * last, departure(band_rows + 1) * last
    lines = {-2: ahead[0], -1: ahead[1], band_rows: behind[0], band_rows + 1: behind[1]}
    for row in range(-1, band_rows + 1):
        mid, above, below = (
            lines[r] if r in lines else departure(r) for r in (row, row - 1, row + 1)
        )
        value = (mid + helm * (above + below + lon_sum(mid))) * inverse
        if row < 0:
            value = value * first
        if row >= band_rows:
            value = value * last
        once[row + 1] = value
    for row in range(band_rows):
        value = (
            dep_ref[row] + helm * (once[row] + once[row + 2] + lon_sum(once[row + 1]))
        ) * inverse
        smooth[row] = value.astype(BF16)
    gb1[...] = jnp.zeros_like(gb1)
    gb2[...] = jnp.zeros_like(gb2)

    for row in range(band_rows):
        rows = smooth[row]
        cot = cot_ref[row]
        act, slope_first = gelu_parts(dot(rows, w1_ref[...]) + b1)
        act_first = act.astype(BF16)
        act, slope_second = gelu_parts(dot(act_first, w2_ref[...]) + b2)
        act_second = act.astype(BF16)
        next_ref[row] = (rows.astype(F32) + dot(act_second, w3_ref[...])).astype(BF16)
        gpre = dot(cot, w3_ref[...], 1, 1) * slope_second
        gpre_second = gpre.astype(BF16)
        gb2[...] += jnp.sum(gpre_second.astype(F32), axis=0, keepdims=True)
        gpre = dot(gpre_second, w2_ref[...], 1, 1) * slope_first
        gpre_first = gpre.astype(BF16)
        gb1[...] += jnp.sum(gpre_first.astype(F32), axis=0, keepdims=True)
        a1[row], a2[row], p1[row], p2[row] = act_first, act_second, gpre_first, gpre_second
        gsmooth = cot.astype(F32) + dot(gpre_first, w1_ref[...], 1, 1)
        scaled_ref[row] = gsmooth * inverse
    flat = band_rows * lon

    def whole(ref):
        return ref[...].reshape(flat, ref.shape[2])

    g3 = dot(whole(a2), whole(cot_ref), 0, 0).astype(BF16)
    g2 = dot(whole(a1), whole(p2), 0, 0).astype(BF16)
    g1 = dot(whole(smooth), whole(p1), 0, 0).astype(BF16)
    for row in range(2):
        up_ref[row] = scaled_ref[row].astype(BF16)
        down_ref[row] = scaled_ref[band_rows - 2 + row].astype(BF16)
    grads_ref[:ch] = g1[:, :ch]
    grads_ref[ch : 2 * ch] = g1[:, ch:]
    grads_ref[2 * ch : 4 * ch] = g2[:, :ch]
    grads_ref[4 * ch : 6 * ch] = g2[:, ch:]
    grads_ref[6 * ch : 8 * ch] = g3
    rest = grads_ref.shape[0] - 8 * ch
    row_at = lax.broadcasted_iota(jnp.int32, (rest, ch), 0)
    tail = jnp.zeros((rest, ch), F32)
    for index, line in enumerate((gb1[:, :ch], gb1[:, ch:], gb2[:, :ch], gb2[:, ch:])):
        tail = jnp.where(row_at == index, line, tail)
    grads_ref[8 * ch :] = tail.astype(BF16)


def adjoint_kernel(
    offsets,
    scaled_ref,
    after_ref,
    before_ref,
    place_ref,
    table_ref,
    *refs,
):
    outs, (once, spread, hit) = refs[:offsets], refs[offsets:]
    band_rows, lon, ch = scaled_ref.shape
    quads, wide = outs[0].shape
    taps = wide // ch
    helm, inverse = coefficients(table_ref, TABLE_AT, ch)
    first = jnp.where(place_ref[0] == 0, 0.0, 1.0)
    last = jnp.where(place_ref[0] == place_ref[1] - 1, 0.0, 1.0)
    weights = table_ref[:TABLE_AT].T
    quad_lanes = table_ref[TABLE_AT : TABLE_AT + 8].astype(jnp.int32)
    quad_at = lax.broadcasted_iota(jnp.int32, (offsets * quads, lon), 0)
    for row in range(band_rows):
        hit[:, row * lon : (row + 1) * lon] = one_hot(quad_at == quad_lanes[row : row + 1])

    def scaled(row):
        if row < 0:
            return before_ref[row + 2].astype(F32) * first
        if row >= band_rows:
            return after_ref[row - band_rows].astype(F32) * last
        return scaled_ref[row]

    for row in range(-1, band_rows + 1):
        value = (helm * inverse) * (scaled(row - 1) + scaled(row + 1) + lon_sum(scaled(row)))
        if row < 0:
            value = value * first
        if row >= band_rows:
            value = value * last
        once[row + 1] = value
    for row in range(band_rows):
        value = (
            scaled_ref[row]
            + once[row + 1]
            + helm * (once[row] + once[row + 2] + lon_sum(once[row + 1]))
        )
        for tap in range(taps):
            at = tap * band_rows + row
            spread[row * lon : (row + 1) * lon, tap * ch : (tap + 1) * ch] = (
                weights[:, at : at + 1] * value
            ).astype(BF16)
    slot_grads = dot(hit[...], spread[...]).astype(BF16)
    for offset in range(offsets):
        outs[offset][...] = slot_grads[offset * quads : (offset + 1) * quads]


def scatter_kernel(offsets, order, cells_ref, count_ref, *refs):
    blocks = dict(zip(order, refs[:offsets]))
    out_ref, done_ref, table, hit = refs[offsets:]
    done_ref[...] = jnp.zeros_like(done_ref)
    band_rows, lon, ch = out_ref.shape
    quads = refs[0].shape[0]
    box_at = lax.broadcasted_iota(jnp.int32, ((band_rows - 1) * lon, quads), 0)
    for offset in range(offsets):
        table[offset * quads : (offset + 1) * quads] = jnp.where(
            live_quads(count_ref, offset, quads), blocks[offset][...].astype(F32), 0.0
        ).astype(BF16)
        hit[:, offset * quads : (offset + 1) * quads] = one_hot(
            box_at == cells_ref[offset : offset + 1]
        )
    for row in range(band_rows):
        here = jnp.zeros((lon, ch), F32)
        right = jnp.zeros((lon, ch), F32)
        if row < band_rows - 1:
            both = dot(hit[row * lon : (row + 1) * lon], table[:, : 2 * ch])
            here = here + both[:, :ch]
            right = right + both[:, ch:]
        if row > 0:
            both = dot(hit[(row - 1) * lon : row * lon], table[:, 2 * ch :])
            here = here + both[:, :ch]
            right = right + both[:, ch:]
        out_ref[row] = here + pltpu.roll(right, 1, 0)


def sum_kernel(copies, parts_ref, ahead_ref, out_ref):
    total = parts_ref[0].astype(F32)
    for part in range(1, parts_ref.shape[0]):
        total = total + parts_ref[part].astype(F32)
    total = total.astype(BF16)
    for copy in range(copies):
        out_ref[copy] = total


def unpack_kernel(sums_ref, ahead_ref, g1, gb1, g2, gb2, g3):
    ch, hid = g1.shape
    g1[:, :ch] = sums_ref[:ch].astype(F32)
    g1[:, ch:] = sums_ref[ch : 2 * ch].astype(F32)
    g2[:, :ch] = sums_ref[2 * ch : 4 * ch].astype(F32)
    g2[:, ch:] = sums_ref[4 * ch : 6 * ch].astype(F32)
    g3[...] = sums_ref[6 * ch : 8 * ch].astype(F32)
    tail = sums_ref[8 * ch : 8 * ch + 8].astype(F32)
    gb1[:, :ch], gb1[:, ch:] = tail[0:1], tail[1:2]
    gb2[:, :ch], gb2[:, ch:] = tail[2:3], tail[3:4]


def shifted(block, by, count):
    return lax.ppermute(block, SPACE, [(i, (i + by) % count) for i in range(count)])


def body(
    field,
    send_rows,
    send_count,
    dep_slot,
    dep_weight,
    helm_coef,
    w_first,
    b_first,
    w_second,
    b_second,
    w_third,
    cotangent,
):
    _, band_rows, lon, ch = field.shape
    hid = w_first.shape[1]
    offsets, slots = send_rows.shape[1:]
    taps = dep_slot.shape[0]
    reach = (offsets - 1) // 2
    quads = slots // 4
    bands = lax.axis_size(SPACE)
    shape = jax.ShapeDtypeStruct
    place = jnp.stack([lax.axis_index(SPACE).astype(jnp.int32), jnp.int32(bands)])
    block = shape((quads, taps * ch), BF16)
    edge = shape((2, lon, ch), BF16)

    cells, select = call(
        choose_kernel,
        [
            shape((8, quads), jnp.int32),
            shape((offsets * quads, (band_rows - 1) * lon), BF16),
        ],
        [VMEM],
        [pltpu.VMEM((8, slots), jnp.int32)],
        flops=CHOOSE_COST,
        name="choose",
    )(jnp.transpose(send_rows, (1, 0, 2)))
    packed = call(
        functools.partial(pack_kernel, offsets),
        [block] * offsets,
        [VMEM] * 3,
        [pltpu.VMEM((band_rows * lon, 2 * ch), BF16)],
        name="pack",
    )(field[0], select, send_count)
    received = [
        packed[e] if e == reach else shifted(packed[e], e - reach, bands)
        for e in range(offsets)
    ]
    order = sorted(range(offsets), key=lambda e: -abs(e - reach))
    (table,) = call(
        prepare_kernel,
        [shape((TABLE_AT + 16, lon), F32)],
        [VMEM] * 5,
        flops=PREPARE_COST,
        name="prepare",
    )(
        dep_slot,
        dep_weight,
        helm_coef.reshape(1, ch),
        b_first.reshape(1, hid),
        b_second.reshape(1, hid),
    )
    departure, up, down = call(
        functools.partial(interp_kernel, offsets, order),
        [shape((band_rows, lon, ch), F32), edge, edge],
        [VMEM] * (offsets + 1),
        [pltpu.VMEM((offsets * quads, taps * ch), BF16)],
        name="interp",
    )(*(received[e] for e in order), table)
    after = shifted(up, -1, bands)
    before = shifted(down, 1, bands)
    groups = ("y", "x", "core")
    group = lax.axis_size(groups)
    depth = lax.axis_size("z")
    next_state, scaled, up, down, grads = call(
        mlp_kernel,
        [
            shape((band_rows, lon, ch), BF16),
            shape((band_rows, lon, ch), F32),
            edge,
            edge,
            shape((group * PART_ROWS, ch), BF16),
        ],
        [VMEM] * 4 + [SMEM] + [VMEM] * 4,
        [
            pltpu.VMEM((1, hid), F32),
            pltpu.VMEM((1, hid), F32),
            pltpu.VMEM((band_rows + 2, lon, ch), F32),
            pltpu.VMEM((band_rows, lon, ch), BF16),
        ]
        + [pltpu.VMEM((band_rows, lon, hid), BF16)] * 4,
        name="smooth_mlp",
    )(departure, after, before, cotangent[0], place, table, w_first, w_second, w_third)
    after = shifted(up, -1, bands)
    before = shifted(down, 1, bands)

    parts = lax.all_to_all(grads.reshape(group, PART_ROWS, ch), groups, 0, 0)
    slot_grads = call(
        functools.partial(adjoint_kernel, offsets),
        [block] * offsets,
        [VMEM] * 3 + [SMEM, VMEM],
        [
            pltpu.VMEM((band_rows + 2, lon, ch), F32),
            pltpu.VMEM((band_rows * lon, taps * ch), BF16),
            pltpu.VMEM((offsets * quads, band_rows * lon), BF16),
        ],
        flops=ADJOINT_COST,
        name="adjoint",
    )(scaled, after, before, place, table)
    (part_sum,) = call(
        functools.partial(sum_kernel, depth),
        [shape((depth, PART_ROWS, ch), BF16)],
        [VMEM, ANY],
        flops=PART_COST,
        name="part_sum",
    )(parts, slot_grads[reach])
    parts = lax.all_to_all(part_sum, "z", 0, 0)
    back = [
        slot_grads[e] if e == reach else shifted(slot_grads[e], reach - e, bands)
        for e in range(offsets)
    ]
    field_grad, done = call(
        functools.partial(scatter_kernel, offsets, order),
        [shape((band_rows, lon, ch), F32), shape((8, ch), F32)],
        [VMEM] * (offsets + 2),
        [
            pltpu.VMEM((offsets * quads, taps * ch), BF16),
            pltpu.VMEM(((band_rows - 1) * lon, offsets * quads), BF16),
        ],
        flops=SCATTER_COST,
        name="scatter",
    )(cells, send_count, *(back[e] for e in order))
    (whole_sum,) = call(
        functools.partial(sum_kernel, group),
        [shape((group, PART_ROWS, ch), BF16)],
        [VMEM, ANY],
        name="whole_sum",
    )(parts, slot_grads[reach])
    sums = lax.all_to_all(whole_sum, groups, 0, 0).reshape(group * PART_ROWS, ch)
    grad_shapes = [
        shape((ch, hid), F32),
        shape((1, hid), F32),
        shape((hid, hid), F32),
        shape((1, hid), F32),
        shape((hid, ch), F32),
    ]
    grads = call(
        unpack_kernel,
        grad_shapes,
        [VMEM, ANY],
        name="unpack",
    )(sums, done)
    return (
        next_state[None],
        field_grad[None],
        grads[0],
        grads[1].reshape(hid),
        grads[2],
        grads[3].reshape(hid),
        grads[4],
    )


def solution(mesh):
    fine = Mesh(mesh.devices.reshape(4, 8, 4, 2), ("y",) + SPACE)
    state = P("y", SPACE, None, None)
    return jax.shard_map(
        body,
        mesh=fine,
        in_specs=(
            state,
            P(SPACE, None, None),
            P(SPACE, None),
            P(None, SPACE, None),
            P(None, SPACE, None),
            P(),
            P(),
            P(),
            P(),
            P(),
            P(),
            state,
        ),
        out_specs=(state, state, P(), P(), P(), P(), P()),
        check_vma=False,
    )
```

```python
import functools
import math

import jax
import jax.numpy as jnp
from jax import lax
from jax.experimental import pallas as pl
from jax.experimental.pallas import tpu as pltpu
from jax.sharding import Mesh
from jax.sharding import PartitionSpec as P

F32 = jnp.float32
BF16 = jnp.bfloat16
SPACE = ("z", "x", "core")
GELU_SCALE = math.sqrt(2.0 / math.pi)
GELU_CUBE = 0.044715
PART_ROWS = 40
TABLE_AT = 16
PREPARE_COST = 10**9
PART_COST = 0
ADJOINT_COST = 10**11
SCATTER_COST = 10**11
CHOOSE_COST = 2 * 10**9

VMEM = pl.BlockSpec(memory_space=pltpu.VMEM)
ANY = pl.BlockSpec(memory_space=pl.ANY)
SMEM = pl.BlockSpec(memory_space=pltpu.SMEM)


def dot(left, right, left_dim=1, right_dim=0):
    return lax.dot_general(
        left,
        right,
        (((left_dim,), (right_dim,)), ((), ())),
        preferred_element_type=F32,
    )


def call(kernel, outs, ins, scratch=(), flops=0, name=None):
    nbytes = sum(math.prod(o.shape) * o.dtype.itemsize for o in outs)
    return pl.pallas_call(
        kernel,
        out_shape=outs,
        in_specs=ins,
        out_specs=[VMEM] * len(outs),
        scratch_shapes=list(scratch),
        compiler_params=pltpu.CompilerParams(vmem_limit_bytes=32 * 1024 * 1024),
        cost_estimate=pl.CostEstimate(
            flops=flops, bytes_accessed=2 * nbytes, transcendentals=0
        ),
        name=name,
    )


def quad_boxes(index, quads):
    pick = one_hot(
        lax.broadcasted_iota(jnp.int32, (4 * quads, quads), 0)
        == 4 * lax.broadcasted_iota(jnp.int32, (4 * quads, quads), 1)
    )
    high = (index >> 3).astype(F32).astype(BF16)
    low = (index & 7).astype(F32).astype(BF16)
    return (dot(high, pick) * 8.0 + dot(low, pick)).astype(jnp.int32)


def live_quads(count_ref, offset, quads):
    slot_at = 4 * lax.broadcasted_iota(jnp.int32, (quads, 1), 0)
    return slot_at < count_ref[:, offset : offset + 1]


def one_hot(mask):
    return mask.astype(F32).astype(BF16)


def choose_kernel(rows_ref, cells_ref, select_ref, index):
    quads = cells_ref.shape[1]
    offsets = rows_ref.shape[0]
    index[...] = jnp.zeros_like(index)
    for offset in range(offsets):
        index[offset : offset + 1] = rows_ref[offset]
    cells = quad_boxes(index[...], quads)
    cells_ref[...] = cells
    columns = cells.astype(F32).T.astype(jnp.int32)
    box_at = lax.broadcasted_iota(jnp.int32, (quads, select_ref.shape[1]), 1)
    for offset in range(offsets):
        select_ref[offset * quads : (offset + 1) * quads] = one_hot(
            box_at == columns[:, offset : offset + 1]
        )


def pack_kernel(offsets, field_ref, select_ref, count_ref, *refs):
    outs, pair = refs[:offsets], refs[offsets]
    band_rows, lon, ch = field_ref.shape
    quads = outs[0].shape[0]
    boxes = (band_rows - 1) * lon
    for row in range(band_rows):
        line = field_ref[row]
        pair[row * lon : (row + 1) * lon, :ch] = line
        pair[row * lon : (row + 1) * lon, ch:] = pltpu.roll(
            line.astype(F32), lon - 1, 0
        ).astype(BF16)
    for part in range(2):
        picked = dot(select_ref[...], pair[part * lon : part * lon + boxes])
        for offset in range(offsets):
            outs[offset][:, part * 2 * ch : (part + 1) * 2 * ch] = jnp.where(
                live_quads(count_ref, offset, quads),
                picked[offset * quads : (offset + 1) * quads],
                0.0,
            ).astype(BF16)


def prepare_kernel(slot_ref, weight_ref, helm_ref, b1_ref, b2_ref, table_ref):
    taps, band_rows, lon = weight_ref.shape
    ch = helm_ref.shape[1]
    hid = b1_ref.shape[1]
    table_ref[...] = jnp.zeros_like(table_ref)
    for tap in range(taps):
        table_ref[tap * band_rows : (tap + 1) * band_rows] = weight_ref[tap]
    at = taps * band_rows
    table_ref[at : at + band_rows] = (slot_ref[0] >> 2).astype(F32)
    helm = helm_ref[...]
    table_ref[at + 8 : at + 9, :ch] = helm
    table_ref[at + 8 : at + 9, ch : 2 * ch] = 1.0 / (1.0 + 4.0 * helm)
    table_ref[at + 9 : at + 10, :hid] = b1_ref[...]
    table_ref[at + 10 : at + 11, :hid] = b2_ref[...]


def coefficients(table_ref, at, ch):
    return table_ref[at + 8 : at + 9, :ch], table_ref[at + 8 : at + 9, ch : 2 * ch]


def interp_kernel(offsets, order, *refs):
    blocks = dict(zip(order, refs[:offsets]))
    table_ref, dep_ref, up_ref, down_ref, table = refs[offsets:]
    band_rows, lon, ch = dep_ref.shape
    quads, wide = refs[0].shape
    taps = wide // ch
    weights = table_ref[: taps * band_rows + 8].T
    columns = weights[:, taps * band_rows :].astype(jnp.int32)
    quad_at = lax.broadcasted_iota(jnp.int32, (lon, offsets * quads), 1)
    for offset in range(offsets):
        table[offset * quads : (offset + 1) * quads] = blocks[offset][...]
    for row in range(band_rows):
        tapped = dot(one_hot(quad_at == columns[:, row : row + 1]), table[...])
        line = jnp.zeros((lon, ch), F32)
        for tap in range(taps):
            at = tap * band_rows + row
            line = line + weights[:, at : at + 1] * tapped[:, tap * ch : (tap + 1) * ch]
        dep_ref[row] = line
        if row < 2:
            up_ref[row] = line.astype(BF16)
        if row >= band_rows - 2:
            down_ref[row - band_rows + 2] = line.astype(BF16)


def lon_sum(line):
    lon = line.shape[0]
    return pltpu.roll(line, 1, 0) + pltpu.roll(line, lon - 1, 0)


def gelu_parts(pre):
    square = pre * pre
    curve = jnp.tanh(pre * (GELU_SCALE + (GELU_SCALE * GELU_CUBE) * square))
    share = 0.5 + 0.5 * curve
    act = pre * share
    slope = share + (act - act * share) * (
        2.0 * GELU_SCALE + (6.0 * GELU_SCALE * GELU_CUBE) * square
    )
    return act, slope


def mlp_kernel(
    dep_ref,
    after_ref,
    before_ref,
    cot_ref,
    place_ref,
    table_ref,
    w1_ref,
    w2_ref,
    w3_ref,
    next_ref,
    scaled_ref,
    up_ref,
    down_ref,
    grads_ref,
    gb1,
    gb2,
    once,
    smooth,
    a1,
    a2,
    p1,
    p2,
):
    band_rows, lon, ch = dep_ref.shape
    hid = w1_ref.shape[1]
    helm, inverse = coefficients(table_ref, TABLE_AT, ch)
    b1 = table_ref[TABLE_AT + 9 : TABLE_AT + 10, :hid]
    b2 = table_ref[TABLE_AT + 10 : TABLE_AT + 11, :hid]

    def departure(row):
        if row < 0:
            return before_ref[row + 2].astype(F32)
        if row >= band_rows:
            return after_ref[row - band_rows].astype(F32)
        return dep_ref[row]

    first = jnp.where(place_ref[0] == 0, 0.0, 1.0)
    last = jnp.where(place_ref[0] == place_ref[1] - 1, 0.0, 1.0)
    ahead = departure(-2) * first, departure(-1) * first
    behind = departure(band_rows) * last, departure(band_rows + 1) * last
    lines = {-2: ahead[0], -1: ahead[1], band_rows: behind[0], band_rows + 1: behind[1]}
    for row in range(-1, band_rows + 1):
        mid, above, below = (
            lines[r] if r in lines else departure(r) for r in (row, row - 1, row + 1)
        )
        value = (mid + helm * (above + below + lon_sum(mid))) * inverse
        if row < 0:
            value = value * first
        if row >= band_rows:
            value = value * last
        once[row + 1] = value
    for row in range(band_rows):
        value = (
            dep_ref[row] + helm * (once[row] + once[row + 2] + lon_sum(once[row + 1]))
        ) * inverse
        smooth[row] = value.astype(BF16)
    gb1[...] = jnp.zeros_like(gb1)
    gb2[...] = jnp.zeros_like(gb2)

    for row in range(band_rows):
        rows = smooth[row]
        cot = cot_ref[row]
        act, slope_first = gelu_parts(dot(rows, w1_ref[...]) + b1)
        act_first = act.astype(BF16)
        act, slope_second = gelu_parts(dot(act_first, w2_ref[...]) + b2)
        act_second = act.astype(BF16)
        next_ref[row] = (rows.astype(F32) + dot(act_second, w3_ref[...])).astype(BF16)
        gpre = dot(cot, w3_ref[...], 1, 1) * slope_second
        gpre_second = gpre.astype(BF16)
        gb2[...] += jnp.sum(gpre_second.astype(F32), axis=0, keepdims=True)
        gpre = dot(gpre_second, w2_ref[...], 1, 1) * slope_first
        gpre_first = gpre.astype(BF16)
        gb1[...] += jnp.sum(gpre_first.astype(F32), axis=0, keepdims=True)
        a1[row], a2[row], p1[row], p2[row] = act_first, act_second, gpre_first, gpre_second
        gsmooth = cot.astype(F32) + dot(gpre_first, w1_ref[...], 1, 1)
        scaled_ref[row] = gsmooth * inverse
    flat = band_rows * lon

    def whole(ref):
        return ref[...].reshape(flat, ref.shape[2])

    g3 = dot(whole(a2), whole(cot_ref), 0, 0).astype(BF16)
    g2 = dot(whole(a1), whole(p2), 0, 0).astype(BF16)
    g1 = dot(whole(smooth), whole(p1), 0, 0).astype(BF16)
    for row in range(2):
        up_ref[row] = scaled_ref[row].astype(BF16)
        down_ref[row] = scaled_ref[band_rows - 2 + row].astype(BF16)
    grads_ref[:ch] = g1[:, :ch]
    grads_ref[ch : 2 * ch] = g1[:, ch:]
    grads_ref[2 * ch : 4 * ch] = g2[:, :ch]
    grads_ref[4 * ch : 6 * ch] = g2[:, ch:]
    grads_ref[6 * ch : 8 * ch] = g3
    rest = grads_ref.shape[0] - 8 * ch
    row_at = lax.broadcasted_iota(jnp.int32, (rest, ch), 0)
    tail = jnp.zeros((rest, ch), F32)
    for index, line in enumerate((gb1[:, :ch], gb1[:, ch:], gb2[:, :ch], gb2[:, ch:])):
        tail = jnp.where(row_at == index, line, tail)
    grads_ref[8 * ch :] = tail.astype(BF16)


def adjoint_kernel(
    offsets,
    scaled_ref,
    after_ref,
    before_ref,
    place_ref,
    table_ref,
    *refs,
):
    outs, (once, spread, hit) = refs[:offsets], refs[offsets:]
    band_rows, lon, ch = scaled_ref.shape
    quads, wide = outs[0].shape
    taps = wide // ch
    helm, inverse = coefficients(table_ref, TABLE_AT, ch)
    first = jnp.where(place_ref[0] == 0, 0.0, 1.0)
    last = jnp.where(place_ref[0] == place_ref[1] - 1, 0.0, 1.0)
    weights = table_ref[:TABLE_AT].T
    quad_lanes = table_ref[TABLE_AT : TABLE_AT + 8].astype(jnp.int32)
    quad_at = lax.broadcasted_iota(jnp.int32, (offsets * quads, lon), 0)
    for row in range(band_rows):
        hit[:, row * lon : (row + 1) * lon] = one_hot(quad_at == quad_lanes[row : row + 1])

    def scaled(row):
        if row < 0:
            return before_ref[row + 2].astype(F32) * first
        if row >= band_rows:
            return after_ref[row - band_rows].astype(F32) * last
        return scaled_ref[row]

    for row in range(-1, band_rows + 1):
        value = (helm * inverse) * (scaled(row - 1) + scaled(row + 1) + lon_sum(scaled(row)))
        if row < 0:
            value = value * first
        if row >= band_rows:
            value = value * last
        once[row + 1] = value
    for row in range(band_rows):
        value = (
            scaled_ref[row]
            + once[row + 1]
            + helm * (once[row] + once[row + 2] + lon_sum(once[row + 1]))
        )
        for tap in range(taps):
            at = tap * band_rows + row
            spread[row * lon : (row + 1) * lon, tap * ch : (tap + 1) * ch] = (
                weights[:, at : at + 1] * value
            ).astype(BF16)
    slot_grads = dot(hit[...], spread[...]).astype(BF16)
    for offset in range(offsets):
        outs[offset][...] = slot_grads[offset * quads : (offset + 1) * quads]


def scatter_kernel(offsets, order, cells_ref, count_ref, *refs):
    blocks = dict(zip(order, refs[:offsets]))
    out_ref, done_ref, table, hit = refs[offsets:]
    done_ref[...] = jnp.zeros_like(done_ref)
    band_rows, lon, ch = out_ref.shape
    quads = refs[0].shape[0]
    box_at = lax.broadcasted_iota(jnp.int32, ((band_rows - 1) * lon, quads), 0)
    for offset in range(offsets):
        table[offset * quads : (offset + 1) * quads] = jnp.where(
            live_quads(count_ref, offset, quads), blocks[offset][...].astype(F32), 0.0
        ).astype(BF16)
        hit[:, offset * quads : (offset + 1) * quads] = one_hot(
            box_at == cells_ref[offset : offset + 1]
        )
    for row in range(band_rows):
        here = jnp.zeros((lon, ch), F32)
        right = jnp.zeros((lon, ch), F32)
        if row < band_rows - 1:
            both = dot(hit[row * lon : (row + 1) * lon], table[:, : 2 * ch])
            here = here + both[:, :ch]
            right = right + both[:, ch:]
        if row > 0:
            both = dot(hit[(row - 1) * lon : row * lon], table[:, 2 * ch :])
            here = here + both[:, :ch]
            right = right + both[:, ch:]
        out_ref[row] = here + pltpu.roll(right, 1, 0)


def sum_kernel(copies, parts_ref, ahead_ref, out_ref):
    total = parts_ref[0].astype(F32)
    for part in range(1, parts_ref.shape[0]):
        total = total + parts_ref[part].astype(F32)
    total = total.astype(BF16)
    for copy in range(copies):
        out_ref[copy] = total


def unpack_kernel(sums_ref, ahead_ref, g1, gb1, g2, gb2, g3):
    ch, hid = g1.shape
    g1[:, :ch] = sums_ref[:ch].astype(F32)
    g1[:, ch:] = sums_ref[ch : 2 * ch].astype(F32)
    g2[:, :ch] = sums_ref[2 * ch : 4 * ch].astype(F32)
    g2[:, ch:] = sums_ref[4 * ch : 6 * ch].astype(F32)
    g3[...] = sums_ref[6 * ch : 8 * ch].astype(F32)
    tail = sums_ref[8 * ch : 8 * ch + 8].astype(F32)
    gb1[:, :ch], gb1[:, ch:] = tail[0:1], tail[1:2]
    gb2[:, :ch], gb2[:, ch:] = tail[2:3], tail[3:4]


def shifted(block, by, count):
    return lax.ppermute(block, SPACE, [(i, (i + by) % count) for i in range(count)])


def body(
    field,
    send_rows,
    send_count,
    dep_slot,
    dep_weight,
    helm_coef,
    w_first,
    b_first,
    w_second,
    b_second,
    w_third,
    cotangent,
):
    _, band_rows, lon, ch = field.shape
    hid = w_first.shape[1]
    offsets, slots = send_rows.shape[1:]
    taps = dep_slot.shape[0]
    reach = (offsets - 1) // 2
    quads = slots // 4
    bands = lax.axis_size(SPACE)
    shape = jax.ShapeDtypeStruct
    place = jnp.stack([lax.axis_index(SPACE).astype(jnp.int32), jnp.int32(bands)])
    block = shape((quads, taps * ch), BF16)
    edge = shape((2, lon, ch), BF16)

    cells, select = call(
        choose_kernel,
        [
            shape((8, quads), jnp.int32),
            shape((offsets * quads, (band_rows - 1) * lon), BF16),
        ],
        [VMEM],
        [pltpu.VMEM((8, slots), jnp.int32)],
        flops=CHOOSE_COST,
        name="choose",
    )(jnp.transpose(send_rows, (1, 0, 2)))
    packed = call(
        functools.partial(pack_kernel, offsets),
        [block] * offsets,
        [VMEM] * 3,
        [pltpu.VMEM((band_rows * lon, 2 * ch), BF16)],
        name="pack",
    )(field[0], select, send_count)
    received = [
        packed[e] if e == reach else shifted(packed[e], e - reach, bands)
        for e in range(offsets)
    ]
    order = sorted(range(offsets), key=lambda e: -abs(e - reach))
    (table,) = call(
        prepare_kernel,
        [shape((TABLE_AT + 16, lon), F32)],
        [VMEM] * 5,
        flops=PREPARE_COST,
        name="prepare",
    )(
        dep_slot,
        dep_weight,
        helm_coef.reshape(1, ch),
        b_first.reshape(1, hid),
        b_second.reshape(1, hid),
    )
    departure, up, down = call(
        functools.partial(interp_kernel, offsets, order),
        [shape((band_rows, lon, ch), F32), edge, edge],
        [VMEM] * (offsets + 1),
        [pltpu.VMEM((offsets * quads, taps * ch), BF16)],
        name="interp",
    )(*(received[e] for e in order), table)
    after = shifted(up, -1, bands)
    before = shifted(down, 1, bands)
    groups = ("y", "x", "core")
    group = lax.axis_size(groups)
    depth = lax.axis_size("z")
    next_state, scaled, up, down, grads = call(
        mlp_kernel,
        [
            shape((band_rows, lon, ch), BF16),
            shape((band_rows, lon, ch), F32),
            edge,
            edge,
            shape((group * PART_ROWS, ch), BF16),
        ],
        [VMEM] * 4 + [SMEM] + [VMEM] * 4,
        [
            pltpu.VMEM((1, hid), F32),
            pltpu.VMEM((1, hid), F32),
            pltpu.VMEM((band_rows + 2, lon, ch), F32),
            pltpu.VMEM((band_rows, lon, ch), BF16),
        ]
        + [pltpu.VMEM((band_rows, lon, hid), BF16)] * 4,
        name="smooth_mlp",
    )(departure, after, before, cotangent[0], place, table, w_first, w_second, w_third)
    after = shifted(up, -1, bands)
    before = shifted(down, 1, bands)

    parts = lax.all_to_all(grads.reshape(group, PART_ROWS, ch), groups, 0, 0)
    slot_grads = call(
        functools.partial(adjoint_kernel, offsets),
        [block] * offsets,
        [VMEM] * 3 + [SMEM, VMEM],
        [
            pltpu.VMEM((band_rows + 2, lon, ch), F32),
            pltpu.VMEM((band_rows * lon, taps * ch), BF16),
            pltpu.VMEM((offsets * quads, band_rows * lon), BF16),
        ],
        flops=ADJOINT_COST,
        name="adjoint",
    )(scaled, after, before, place, table)
    (part_sum,) = call(
        functools.partial(sum_kernel, depth),
        [shape((depth, PART_ROWS, ch), BF16)],
        [VMEM, ANY],
        flops=PART_COST,
        name="part_sum",
    )(parts, slot_grads[reach])
    parts = lax.all_to_all(part_sum, "z", 0, 0)
    back = [
        slot_grads[e] if e == reach else shifted(slot_grads[e], reach - e, bands)
        for e in range(offsets)
    ]
    field_grad, done = call(
        functools.partial(scatter_kernel, offsets, range(offsets)),
        [shape((band_rows, lon, ch), F32), shape((8, ch), F32)],
        [VMEM] * (offsets + 2),
        [
            pltpu.VMEM((offsets * quads, taps * ch), BF16),
            pltpu.VMEM(((band_rows - 1) * lon, offsets * quads), BF16),
        ],
        flops=SCATTER_COST,
        name="scatter",
    )(cells, send_count, *back)
    (whole_sum,) = call(
        functools.partial(sum_kernel, group),
        [shape((group, PART_ROWS, ch), BF16)],
        [VMEM, ANY],
        name="whole_sum",
    )(parts, slot_grads[reach])
    sums = lax.all_to_all(whole_sum, groups, 0, 0).reshape(group * PART_ROWS, ch)
    grad_shapes = [
        shape((ch, hid), F32),
        shape((1, hid), F32),
        shape((hid, hid), F32),
        shape((1, hid), F32),
        shape((hid, ch), F32),
    ]
    grads = call(
        unpack_kernel,
        grad_shapes,
        [VMEM, ANY],
        name="unpack",
    )(sums, done)
    return (
        next_state[None],
        field_grad[None],
        grads[0],
        grads[1].reshape(hid),
        grads[2],
        grads[3].reshape(hid),
        grads[4],
    )


def solution(mesh):
    fine = Mesh(mesh.devices.reshape(4, 8, 4, 2), ("y",) + SPACE)
    state = P("y", SPACE, None, None)
    return jax.shard_map(
        body,
        mesh=fine,
        in_specs=(
            state,
            P(SPACE, None, None),
            P(SPACE, None),
            P(None, SPACE, None),
            P(None, SPACE, None),
            P(),
            P(),
            P(),
            P(),
            P(),
            P(),
            state,
        ),
        out_specs=(state, state, P(), P(), P(), P(), P()),
        check_vma=False,
    )
```

```python
import functools
import math

import jax
import jax.numpy as jnp
from jax import lax
from jax.experimental import pallas as pl
from jax.experimental.pallas import tpu as pltpu
from jax.sharding import Mesh
from jax.sharding import PartitionSpec as P

F32 = jnp.float32
BF16 = jnp.bfloat16
SPACE = ("z", "x", "core")
GELU_SCALE = math.sqrt(2.0 / math.pi)
GELU_CUBE = 0.044715
PART_ROWS = 40
TABLE_AT = 16
PREPARE_COST = 10**9
PART_COST = 0
ADJOINT_COST = 10**11
SCATTER_COST = 10**11
CHOOSE_COST = 2 * 10**9

VMEM = pl.BlockSpec(memory_space=pltpu.VMEM)
ANY = pl.BlockSpec(memory_space=pl.ANY)
SMEM = pl.BlockSpec(memory_space=pltpu.SMEM)


def dot(left, right, left_dim=1, right_dim=0):
    return lax.dot_general(
        left,
        right,
        (((left_dim,), (right_dim,)), ((), ())),
        preferred_element_type=F32,
    )


def call(kernel, outs, ins, scratch=(), flops=0, name=None):
    nbytes = sum(math.prod(o.shape) * o.dtype.itemsize for o in outs)
    return pl.pallas_call(
        kernel,
        out_shape=outs,
        in_specs=ins,
        out_specs=[VMEM] * len(outs),
        scratch_shapes=list(scratch),
        compiler_params=pltpu.CompilerParams(vmem_limit_bytes=32 * 1024 * 1024),
        cost_estimate=pl.CostEstimate(
            flops=flops, bytes_accessed=2 * nbytes, transcendentals=0
        ),
        name=name,
    )


def quad_boxes(index, quads):
    pick = one_hot(
        lax.broadcasted_iota(jnp.int32, (4 * quads, quads), 0)
        == 4 * lax.broadcasted_iota(jnp.int32, (4 * quads, quads), 1)
    )
    high = (index >> 3).astype(F32).astype(BF16)
    low = (index & 7).astype(F32).astype(BF16)
    return (dot(high, pick) * 8.0 + dot(low, pick)).astype(jnp.int32)


def live_quads(count_ref, offset, quads):
    slot_at = 4 * lax.broadcasted_iota(jnp.int32, (quads, 1), 0)
    return slot_at < count_ref[:, offset : offset + 1]


def one_hot(mask):
    return mask.astype(F32).astype(BF16)


def choose_kernel(rows_ref, cells_ref, select_ref, index):
    quads = cells_ref.shape[1]
    offsets = rows_ref.shape[0]
    index[...] = jnp.zeros_like(index)
    for offset in range(offsets):
        index[offset : offset + 1] = rows_ref[offset]
    cells = quad_boxes(index[...], quads)
    cells_ref[...] = cells
    columns = cells.astype(F32).T.astype(jnp.int32)
    box_at = lax.broadcasted_iota(jnp.int32, (quads, select_ref.shape[1]), 1)
    for offset in range(offsets):
        select_ref[offset * quads : (offset + 1) * quads] = one_hot(
            box_at == columns[:, offset : offset + 1]
        )


def pack_kernel(offsets, field_ref, select_ref, count_ref, *refs):
    outs, pair = refs[:offsets], refs[offsets]
    band_rows, lon, ch = field_ref.shape
    quads = outs[0].shape[0]
    boxes = (band_rows - 1) * lon
    for row in range(band_rows):
        line = field_ref[row]
        pair[row * lon : (row + 1) * lon, :ch] = line
        pair[row * lon : (row + 1) * lon, ch:] = pltpu.roll(
            line.astype(F32), lon - 1, 0
        ).astype(BF16)
    for part in range(2):
        picked = dot(select_ref[...], pair[part * lon : part * lon + boxes])
        for offset in range(offsets):
            outs[offset][:, part * 2 * ch : (part + 1) * 2 * ch] = jnp.where(
                live_quads(count_ref, offset, quads),
                picked[offset * quads : (offset + 1) * quads],
                0.0,
            ).astype(BF16)


def prepare_kernel(slot_ref, weight_ref, helm_ref, b1_ref, b2_ref, table_ref):
    taps, band_rows, lon = weight_ref.shape
    ch = helm_ref.shape[1]
    hid = b1_ref.shape[1]
    table_ref[...] = jnp.zeros_like(table_ref)
    for tap in range(taps):
        table_ref[tap * band_rows : (tap + 1) * band_rows] = weight_ref[tap]
    at = taps * band_rows
    table_ref[at : at + band_rows] = (slot_ref[0] >> 2).astype(F32)
    helm = helm_ref[...]
    table_ref[at + 8 : at + 9, :ch] = helm
    table_ref[at + 8 : at + 9, ch : 2 * ch] = 1.0 / (1.0 + 4.0 * helm)
    table_ref[at + 9 : at + 10, :hid] = b1_ref[...]
    table_ref[at + 10 : at + 11, :hid] = b2_ref[...]


def coefficients(table_ref, at, ch):
    return table_ref[at + 8 : at + 9, :ch], table_ref[at + 8 : at + 9, ch : 2 * ch]


def interp_kernel(offsets, order, *refs):
    blocks = dict(zip(order, refs[:offsets]))
    table_ref, dep_ref, up_ref, down_ref, table = refs[offsets:]
    band_rows, lon, ch = dep_ref.shape
    quads, wide = refs[0].shape
    taps = wide // ch
    weights = table_ref[: taps * band_rows + 8].T
    columns = weights[:, taps * band_rows :].astype(jnp.int32)
    quad_at = lax.broadcasted_iota(jnp.int32, (lon, offsets * quads), 1)
    for offset in range(offsets):
        table[offset * quads : (offset + 1) * quads] = blocks[offset][...]
    for row in range(band_rows):
        tapped = dot(one_hot(quad_at == columns[:, row : row + 1]), table[...])
        line = jnp.zeros((lon, ch), F32)
        for tap in range(taps):
            at = tap * band_rows + row
            line = line + weights[:, at : at + 1] * tapped[:, tap * ch : (tap + 1) * ch]
        dep_ref[row] = line
        if row < 2:
            up_ref[row] = line.astype(BF16)
        if row >= band_rows - 2:
            down_ref[row - band_rows + 2] = line.astype(BF16)


def lon_sum(line):
    lon = line.shape[0]
    return pltpu.roll(line, 1, 0) + pltpu.roll(line, lon - 1, 0)


def gelu_parts(pre):
    square = pre * pre
    curve = jnp.tanh(pre * (GELU_SCALE + (GELU_SCALE * GELU_CUBE) * square))
    share = 0.5 + 0.5 * curve
    act = pre * share
    slope = share + (act - act * share) * (
        2.0 * GELU_SCALE + (6.0 * GELU_SCALE * GELU_CUBE) * square
    )
    return act, slope


def mlp_kernel(
    dep_ref,
    after_ref,
    before_ref,
    cot_ref,
    place_ref,
    table_ref,
    w1_ref,
    w2_ref,
    w3_ref,
    next_ref,
    scaled_ref,
    up_ref,
    down_ref,
    grads_ref,
    gb1,
    gb2,
    once,
    smooth,
    a1,
    a2,
    p1,
    p2,
):
    band_rows, lon, ch = dep_ref.shape
    hid = w1_ref.shape[1]
    helm, inverse = coefficients(table_ref, TABLE_AT, ch)
    b1 = table_ref[TABLE_AT + 9 : TABLE_AT + 10, :hid]
    b2 = table_ref[TABLE_AT + 10 : TABLE_AT + 11, :hid]

    def departure(row):
        if row < 0:
            return before_ref[row + 2].astype(F32)
        if row >= band_rows:
            return after_ref[row - band_rows].astype(F32)
        return dep_ref[row]

    first = jnp.where(place_ref[0] == 0, 0.0, 1.0)
    last = jnp.where(place_ref[0] == place_ref[1] - 1, 0.0, 1.0)
    ahead = departure(-2) * first, departure(-1) * first
    behind = departure(band_rows) * last, departure(band_rows + 1) * last
    lines = {-2: ahead[0], -1: ahead[1], band_rows: behind[0], band_rows + 1: behind[1]}
    for row in range(-1, band_rows + 1):
        mid, above, below = (
            lines[r] if r in lines else departure(r) for r in (row, row - 1, row + 1)
        )
        value = (mid + helm * (above + below + lon_sum(mid))) * inverse
        if row < 0:
            value = value * first
        if row >= band_rows:
            value = value * last
        once[row + 1] = value
    for row in range(band_rows):
        value = (
            dep_ref[row] + helm * (once[row] + once[row + 2] + lon_sum(once[row + 1]))
        ) * inverse
        smooth[row] = value.astype(BF16)
    gb1[...] = jnp.zeros_like(gb1)
    gb2[...] = jnp.zeros_like(gb2)

    for row in range(band_rows):
        rows = smooth[row]
        cot = cot_ref[row]
        act, slope_first = gelu_parts(dot(rows, w1_ref[...]) + b1)
        act_first = act.astype(BF16)
        act, slope_second = gelu_parts(dot(act_first, w2_ref[...]) + b2)
        act_second = act.astype(BF16)
        next_ref[row] = (rows.astype(F32) + dot(act_second, w3_ref[...])).astype(BF16)
        gpre = dot(cot, w3_ref[...], 1, 1) * slope_second
        gpre_second = gpre.astype(BF16)
        gb2[...] += jnp.sum(gpre_second.astype(F32), axis=0, keepdims=True)
        gpre = dot(gpre_second, w2_ref[...], 1, 1) * slope_first
        gpre_first = gpre.astype(BF16)
        gb1[...] += jnp.sum(gpre_first.astype(F32), axis=0, keepdims=True)
        a1[row], a2[row], p1[row], p2[row] = act_first, act_second, gpre_first, gpre_second
        gsmooth = cot.astype(F32) + dot(gpre_first, w1_ref[...], 1, 1)
        scaled_ref[row] = gsmooth * inverse
    flat = band_rows * lon

    def whole(ref):
        return ref[...].reshape(flat, ref.shape[2])

    g3 = dot(whole(a2), whole(cot_ref), 0, 0).astype(BF16)
    g2 = dot(whole(a1), whole(p2), 0, 0).astype(BF16)
    g1 = dot(whole(smooth), whole(p1), 0, 0).astype(BF16)
    for row in range(2):
        up_ref[row] = scaled_ref[row].astype(BF16)
        down_ref[row] = scaled_ref[band_rows - 2 + row].astype(BF16)
    grads_ref[:ch] = g1[:, :ch]
    grads_ref[ch : 2 * ch] = g1[:, ch:]
    grads_ref[2 * ch : 4 * ch] = g2[:, :ch]
    grads_ref[4 * ch : 6 * ch] = g2[:, ch:]
    grads_ref[6 * ch : 8 * ch] = g3
    rest = grads_ref.shape[0] - 8 * ch
    row_at = lax.broadcasted_iota(jnp.int32, (rest, ch), 0)
    tail = jnp.zeros((rest, ch), F32)
    for index, line in enumerate((gb1[:, :ch], gb1[:, ch:], gb2[:, :ch], gb2[:, ch:])):
        tail = jnp.where(row_at == index, line, tail)
    grads_ref[8 * ch :] = tail.astype(BF16)


def adjoint_kernel(
    offsets,
    scaled_ref,
    after_ref,
    before_ref,
    place_ref,
    table_ref,
    *refs,
):
    outs, (once, spread, hit) = refs[:offsets], refs[offsets:]
    band_rows, lon, ch = scaled_ref.shape
    quads, wide = outs[0].shape
    taps = wide // ch
    helm, inverse = coefficients(table_ref, TABLE_AT, ch)
    first = jnp.where(place_ref[0] == 0, 0.0, 1.0)
    last = jnp.where(place_ref[0] == place_ref[1] - 1, 0.0, 1.0)
    weights = table_ref[:TABLE_AT].T
    quad_lanes = table_ref[TABLE_AT : TABLE_AT + 8].astype(jnp.int32)
    quad_at = lax.broadcasted_iota(jnp.int32, (offsets * quads, lon), 0)
    for row in range(band_rows):
        hit[:, row * lon : (row + 1) * lon] = one_hot(quad_at == quad_lanes[row : row + 1])

    def scaled(row):
        if row < 0:
            return before_ref[row + 2].astype(F32) * first
        if row >= band_rows:
            return after_ref[row - band_rows].astype(F32) * last
        return scaled_ref[row]

    for row in range(-1, band_rows + 1):
        value = (helm * inverse) * (scaled(row - 1) + scaled(row + 1) + lon_sum(scaled(row)))
        if row < 0:
            value = value * first
        if row >= band_rows:
            value = value * last
        once[row + 1] = value
    for row in range(band_rows):
        value = (
            scaled_ref[row]
            + once[row + 1]
            + helm * (once[row] + once[row + 2] + lon_sum(once[row + 1]))
        )
        for tap in range(taps):
            at = tap * band_rows + row
            spread[row * lon : (row + 1) * lon, tap * ch : (tap + 1) * ch] = (
                weights[:, at : at + 1] * value
            ).astype(BF16)
    slot_grads = dot(hit[...], spread[...]).astype(BF16)
    for offset in range(offsets):
        outs[offset][...] = slot_grads[offset * quads : (offset + 1) * quads]


def scatter_kernel(offsets, order, cells_ref, count_ref, *refs):
    blocks = dict(zip(order, refs[:offsets]))
    out_ref, done_ref, table, hit = refs[offsets:]
    done_ref[...] = jnp.zeros_like(done_ref)
    band_rows, lon, ch = out_ref.shape
    quads = refs[0].shape[0]
    box_at = lax.broadcasted_iota(jnp.int32, ((band_rows - 1) * lon, quads), 0)
    for offset in range(offsets):
        table[offset * quads : (offset + 1) * quads] = jnp.where(
            live_quads(count_ref, offset, quads), blocks[offset][...].astype(F32), 0.0
        ).astype(BF16)
        hit[:, offset * quads : (offset + 1) * quads] = one_hot(
            box_at == cells_ref[offset : offset + 1]
        )
    for row in range(band_rows):
        here = jnp.zeros((lon, ch), F32)
        right = jnp.zeros((lon, ch), F32)
        if row < band_rows - 1:
            both = dot(hit[row * lon : (row + 1) * lon], table[:, : 2 * ch])
            here = here + both[:, :ch]
            right = right + both[:, ch:]
        if row > 0:
            both = dot(hit[(row - 1) * lon : row * lon], table[:, 2 * ch :])
            here = here + both[:, :ch]
            right = right + both[:, ch:]
        out_ref[row] = here + pltpu.roll(right, 1, 0)


def sum_kernel(copies, parts_ref, ahead_ref, out_ref):
    total = parts_ref[0].astype(F32)
    for part in range(1, parts_ref.shape[0]):
        total = total + parts_ref[part].astype(F32)
    total = total.astype(BF16)
    for copy in range(copies):
        out_ref[copy] = total


def unpack_kernel(sums_ref, ahead_ref, g1, gb1, g2, gb2, g3):
    ch, hid = g1.shape
    g1[:, :ch] = sums_ref[:ch].astype(F32)
    g1[:, ch:] = sums_ref[ch : 2 * ch].astype(F32)
    g2[:, :ch] = sums_ref[2 * ch : 4 * ch].astype(F32)
    g2[:, ch:] = sums_ref[4 * ch : 6 * ch].astype(F32)
    g3[...] = sums_ref[6 * ch : 8 * ch].astype(F32)
    tail = sums_ref[8 * ch : 8 * ch + 8].astype(F32)
    gb1[:, :ch], gb1[:, ch:] = tail[0:1], tail[1:2]
    gb2[:, :ch], gb2[:, ch:] = tail[2:3], tail[3:4]


def shifted(block, by, count):
    return lax.ppermute(block, SPACE, [(i, (i + by) % count) for i in range(count)])


def body(
    field,
    send_rows,
    send_count,
    dep_slot,
    dep_weight,
    helm_coef,
    w_first,
    b_first,
    w_second,
    b_second,
    w_third,
    cotangent,
):
    _, band_rows, lon, ch = field.shape
    hid = w_first.shape[1]
    offsets, slots = send_rows.shape[1:]
    taps = dep_slot.shape[0]
    reach = (offsets - 1) // 2
    quads = slots // 4
    bands = lax.axis_size(SPACE)
    shape = jax.ShapeDtypeStruct
    place = jnp.stack([lax.axis_index(SPACE).astype(jnp.int32), jnp.int32(bands)])
    block = shape((quads, taps * ch), BF16)
    edge = shape((2, lon, ch), BF16)

    cells, select = call(
        choose_kernel,
        [
            shape((8, quads), jnp.int32),
            shape((offsets * quads, (band_rows - 1) * lon), BF16),
        ],
        [VMEM],
        [pltpu.VMEM((8, slots), jnp.int32)],
        flops=CHOOSE_COST,
        name="choose",
    )(jnp.transpose(send_rows, (1, 0, 2)))
    packed = call(
        functools.partial(pack_kernel, offsets),
        [block] * offsets,
        [VMEM] * 3,
        [pltpu.VMEM((band_rows * lon, 2 * ch), BF16)],
        name="pack",
    )(field[0], select, send_count)
    received = [
        packed[e] if e == reach else shifted(packed[e], e - reach, bands)
        for e in range(offsets)
    ]
    order = sorted(range(offsets), key=lambda e: (-abs(e - reach), -e))
    (table,) = call(
        prepare_kernel,
        [shape((TABLE_AT + 16, lon), F32)],
        [VMEM] * 5,
        flops=PREPARE_COST,
        name="prepare",
    )(
        dep_slot,
        dep_weight,
        helm_coef.reshape(1, ch),
        b_first.reshape(1, hid),
        b_second.reshape(1, hid),
    )
    departure, up, down = call(
        functools.partial(interp_kernel, offsets, order),
        [shape((band_rows, lon, ch), F32), edge, edge],
        [VMEM] * (offsets + 1),
        [pltpu.VMEM((offsets * quads, taps * ch), BF16)],
        name="interp",
    )(*(received[e] for e in order), table)
    after = shifted(up, -1, bands)
    before = shifted(down, 1, bands)
    groups = ("y", "x", "core")
    group = lax.axis_size(groups)
    depth = lax.axis_size("z")
    next_state, scaled, up, down, grads = call(
        mlp_kernel,
        [
            shape((band_rows, lon, ch), BF16),
            shape((band_rows, lon, ch), F32),
            edge,
            edge,
            shape((group * PART_ROWS, ch), BF16),
        ],
        [VMEM] * 4 + [SMEM] + [VMEM] * 4,
        [
            pltpu.VMEM((1, hid), F32),
            pltpu.VMEM((1, hid), F32),
            pltpu.VMEM((band_rows + 2, lon, ch), F32),
            pltpu.VMEM((band_rows, lon, ch), BF16),
        ]
        + [pltpu.VMEM((band_rows, lon, hid), BF16)] * 4,
        name="smooth_mlp",
    )(departure, after, before, cotangent[0], place, table, w_first, w_second, w_third)
    after = shifted(up, -1, bands)
    before = shifted(down, 1, bands)

    parts = lax.all_to_all(grads.reshape(group, PART_ROWS, ch), groups, 0, 0)
    slot_grads = call(
        functools.partial(adjoint_kernel, offsets),
        [block] * offsets,
        [VMEM] * 3 + [SMEM, VMEM],
        [
            pltpu.VMEM((band_rows + 2, lon, ch), F32),
            pltpu.VMEM((band_rows * lon, taps * ch), BF16),
            pltpu.VMEM((offsets * quads, band_rows * lon), BF16),
        ],
        flops=ADJOINT_COST,
        name="adjoint",
    )(scaled, after, before, place, table)
    (part_sum,) = call(
        functools.partial(sum_kernel, depth),
        [shape((depth, PART_ROWS, ch), BF16)],
        [VMEM, ANY],
        flops=PART_COST,
        name="part_sum",
    )(parts, slot_grads[reach])
    parts = lax.all_to_all(part_sum, "z", 0, 0)
    back = [
        slot_grads[e] if e == reach else shifted(slot_grads[e], reach - e, bands)
        for e in range(offsets)
    ]
    field_grad, done = call(
        functools.partial(scatter_kernel, offsets, range(offsets)),
        [shape((band_rows, lon, ch), F32), shape((8, ch), F32)],
        [VMEM] * (offsets + 2),
        [
            pltpu.VMEM((offsets * quads, taps * ch), BF16),
            pltpu.VMEM(((band_rows - 1) * lon, offsets * quads), BF16),
        ],
        flops=SCATTER_COST,
        name="scatter",
    )(cells, send_count, *back)
    (whole_sum,) = call(
        functools.partial(sum_kernel, group),
        [shape((group, PART_ROWS, ch), BF16)],
        [VMEM, ANY],
        name="whole_sum",
    )(parts, slot_grads[reach])
    sums = lax.all_to_all(whole_sum, groups, 0, 0).reshape(group * PART_ROWS, ch)
    grad_shapes = [
        shape((ch, hid), F32),
        shape((1, hid), F32),
        shape((hid, hid), F32),
        shape((1, hid), F32),
        shape((hid, ch), F32),
    ]
    grads = call(
        unpack_kernel,
        grad_shapes,
        [VMEM, ANY],
        name="unpack",
    )(sums, done)
    return (
        next_state[None],
        field_grad[None],
        grads[0],
        grads[1].reshape(hid),
        grads[2],
        grads[3].reshape(hid),
        grads[4],
    )


def solution(mesh):
    fine = Mesh(mesh.devices.reshape(4, 8, 4, 2), ("y",) + SPACE)
    state = P("y", SPACE, None, None)
    return jax.shard_map(
        body,
        mesh=fine,
        in_specs=(
            state,
            P(SPACE, None, None),
            P(SPACE, None),
            P(None, SPACE, None),
            P(None, SPACE, None),
            P(),
            P(),
            P(),
            P(),
            P(),
            P(),
            state,
        ),
        out_specs=(state, state, P(), P(), P(), P(), P()),
        check_vma=False,
    )
```

```python
import functools
import math

import jax
import jax.numpy as jnp
from jax import lax
from jax.experimental import pallas as pl
from jax.experimental.pallas import tpu as pltpu
from jax.sharding import Mesh
from jax.sharding import PartitionSpec as P

F32 = jnp.float32
BF16 = jnp.bfloat16
SPACE = ("z", "x", "core")
GELU_SCALE = math.sqrt(2.0 / math.pi)
GELU_CUBE = 0.044715
PART_ROWS = 40
TABLE_AT = 16
PREPARE_COST = 10**9
PART_COST = 0
ADJOINT_COST = 10**11
SCATTER_COST = 10**11
CHOOSE_COST = 2 * 10**9

VMEM = pl.BlockSpec(memory_space=pltpu.VMEM)
ANY = pl.BlockSpec(memory_space=pl.ANY)
SMEM = pl.BlockSpec(memory_space=pltpu.SMEM)


def dot(left, right, left_dim=1, right_dim=0):
    return lax.dot_general(
        left,
        right,
        (((left_dim,), (right_dim,)), ((), ())),
        preferred_element_type=F32,
    )


def call(kernel, outs, ins, scratch=(), flops=0, name=None):
    nbytes = sum(math.prod(o.shape) * o.dtype.itemsize for o in outs)
    return pl.pallas_call(
        kernel,
        out_shape=outs,
        in_specs=ins,
        out_specs=[VMEM] * len(outs),
        scratch_shapes=list(scratch),
        compiler_params=pltpu.CompilerParams(vmem_limit_bytes=32 * 1024 * 1024),
        cost_estimate=pl.CostEstimate(
            flops=flops, bytes_accessed=2 * nbytes, transcendentals=0
        ),
        name=name,
    )


def quad_boxes(index, quads):
    pick = one_hot(
        lax.broadcasted_iota(jnp.int32, (4 * quads, quads), 0)
        == 4 * lax.broadcasted_iota(jnp.int32, (4 * quads, quads), 1)
    )
    high = (index >> 3).astype(F32).astype(BF16)
    low = (index & 7).astype(F32).astype(BF16)
    return (dot(high, pick) * 8.0 + dot(low, pick)).astype(jnp.int32)


def live_quads(count_ref, offset, quads):
    slot_at = 4 * lax.broadcasted_iota(jnp.int32, (quads, 1), 0)
    return slot_at < count_ref[:, offset : offset + 1]


def one_hot(mask):
    return mask.astype(F32).astype(BF16)


def choose_kernel(rows_ref, cells_ref, select_ref, index):
    quads = cells_ref.shape[1]
    offsets = rows_ref.shape[0]
    index[...] = jnp.zeros_like(index)
    for offset in range(offsets):
        index[offset : offset + 1] = rows_ref[offset]
    cells = quad_boxes(index[...], quads)
    cells_ref[...] = cells
    columns = cells.astype(F32).T.astype(jnp.int32)
    box_at = lax.broadcasted_iota(jnp.int32, (quads, select_ref.shape[1]), 1)
    for offset in range(offsets):
        select_ref[offset * quads : (offset + 1) * quads] = one_hot(
            box_at == columns[:, offset : offset + 1]
        )


def pack_kernel(offsets, field_ref, select_ref, count_ref, *refs):
    outs, pair = refs[:offsets], refs[offsets]
    band_rows, lon, ch = field_ref.shape
    quads = outs[0].shape[0]
    boxes = (band_rows - 1) * lon
    for row in range(band_rows):
        line = field_ref[row]
        pair[row * lon : (row + 1) * lon, :ch] = line
        pair[row * lon : (row + 1) * lon, ch:] = pltpu.roll(
            line.astype(F32), lon - 1, 0
        ).astype(BF16)
    for part in range(2):
        picked = dot(select_ref[...], pair[part * lon : part * lon + boxes])
        for offset in range(offsets):
            outs[offset][:, part * 2 * ch : (part + 1) * 2 * ch] = jnp.where(
                live_quads(count_ref, offset, quads),
                picked[offset * quads : (offset + 1) * quads],
                0.0,
            ).astype(BF16)


def prepare_kernel(slot_ref, weight_ref, helm_ref, b1_ref, b2_ref, table_ref):
    taps, band_rows, lon = weight_ref.shape
    ch = helm_ref.shape[1]
    hid = b1_ref.shape[1]
    table_ref[...] = jnp.zeros_like(table_ref)
    for tap in range(taps):
        table_ref[tap * band_rows : (tap + 1) * band_rows] = weight_ref[tap]
    at = taps * band_rows
    table_ref[at : at + band_rows] = (slot_ref[0] >> 2).astype(F32)
    helm = helm_ref[...]
    table_ref[at + 8 : at + 9, :ch] = helm
    table_ref[at + 8 : at + 9, ch : 2 * ch] = 1.0 / (1.0 + 4.0 * helm)
    table_ref[at + 9 : at + 10, :hid] = b1_ref[...]
    table_ref[at + 10 : at + 11, :hid] = b2_ref[...]


def coefficients(table_ref, at, ch):
    return table_ref[at + 8 : at + 9, :ch], table_ref[at + 8 : at + 9, ch : 2 * ch]


def interp_kernel(offsets, order, *refs):
    blocks = dict(zip(order, refs[:offsets]))
    table_ref, dep_ref, up_ref, down_ref, table = refs[offsets:]
    band_rows, lon, ch = dep_ref.shape
    quads, wide = refs[0].shape
    taps = wide // ch
    weights = table_ref[: taps * band_rows + 8].T
    columns = weights[:, taps * band_rows :].astype(jnp.int32)
    quad_at = lax.broadcasted_iota(jnp.int32, (lon, offsets * quads), 1)
    for offset in range(offsets):
        table[offset * quads : (offset + 1) * quads] = blocks[offset][...]
    for row in range(band_rows):
        tapped = dot(one_hot(quad_at == columns[:, row : row + 1]), table[...])
        line = jnp.zeros((lon, ch), F32)
        for tap in range(taps):
            at = tap * band_rows + row
            line = line + weights[:, at : at + 1] * tapped[:, tap * ch : (tap + 1) * ch]
        dep_ref[row] = line
        if row < 2:
            up_ref[row] = line.astype(BF16)
        if row >= band_rows - 2:
            down_ref[row - band_rows + 2] = line.astype(BF16)


def lon_sum(line):
    lon = line.shape[0]
    return pltpu.roll(line, 1, 0) + pltpu.roll(line, lon - 1, 0)


def gelu_parts(pre):
    square = pre * pre
    curve = jnp.tanh(pre * (GELU_SCALE + (GELU_SCALE * GELU_CUBE) * square))
    share = 0.5 + 0.5 * curve
    act = pre * share
    slope = share + (act - act * share) * (
        2.0 * GELU_SCALE + (6.0 * GELU_SCALE * GELU_CUBE) * square
    )
    return act, slope


def mlp_kernel(
    dep_ref,
    after_ref,
    before_ref,
    cot_ref,
    place_ref,
    table_ref,
    w1_ref,
    w2_ref,
    w3_ref,
    next_ref,
    scaled_ref,
    up_ref,
    down_ref,
    grads_ref,
    gb1,
    gb2,
    once,
    smooth,
    a1,
    a2,
    p1,
    p2,
):
    band_rows, lon, ch = dep_ref.shape
    hid = w1_ref.shape[1]
    helm, inverse = coefficients(table_ref, TABLE_AT, ch)
    b1 = table_ref[TABLE_AT + 9 : TABLE_AT + 10, :hid]
    b2 = table_ref[TABLE_AT + 10 : TABLE_AT + 11, :hid]

    def departure(row):
        if row < 0:
            return before_ref[row + 2].astype(F32)
        if row >= band_rows:
            return after_ref[row - band_rows].astype(F32)
        return dep_ref[row]

    first = jnp.where(place_ref[0] == 0, 0.0, 1.0)
    last = jnp.where(place_ref[0] == place_ref[1] - 1, 0.0, 1.0)
    ahead = departure(-2) * first, departure(-1) * first
    behind = departure(band_rows) * last, departure(band_rows + 1) * last
    lines = {-2: ahead[0], -1: ahead[1], band_rows: behind[0], band_rows + 1: behind[1]}
    for row in range(-1, band_rows + 1):
        mid, above, below = (
            lines[r] if r in lines else departure(r) for r in (row, row - 1, row + 1)
        )
        value = (mid + helm * (above + below + lon_sum(mid))) * inverse
        if row < 0:
            value = value * first
        if row >= band_rows:
            value = value * last
        once[row + 1] = value
    for row in range(band_rows):
        value = (
            dep_ref[row] + helm * (once[row] + once[row + 2] + lon_sum(once[row + 1]))
        ) * inverse
        smooth[row] = value.astype(BF16)
    gb1[...] = jnp.zeros_like(gb1)
    gb2[...] = jnp.zeros_like(gb2)

    for row in range(band_rows):
        rows = smooth[row]
        cot = cot_ref[row]
        act, slope_first = gelu_parts(dot(rows, w1_ref[...]) + b1)
        act_first = act.astype(BF16)
        act, slope_second = gelu_parts(dot(act_first, w2_ref[...]) + b2)
        act_second = act.astype(BF16)
        next_ref[row] = (rows.astype(F32) + dot(act_second, w3_ref[...])).astype(BF16)
        gpre = dot(cot, w3_ref[...], 1, 1) * slope_second
        gpre_second = gpre.astype(BF16)
        gb2[...] += jnp.sum(gpre_second.astype(F32), axis=0, keepdims=True)
        gpre = dot(gpre_second, w2_ref[...], 1, 1) * slope_first
        gpre_first = gpre.astype(BF16)
        gb1[...] += jnp.sum(gpre_first.astype(F32), axis=0, keepdims=True)
        a1[row], a2[row], p1[row], p2[row] = act_first, act_second, gpre_first, gpre_second
        gsmooth = cot.astype(F32) + dot(gpre_first, w1_ref[...], 1, 1)
        scaled_ref[row] = gsmooth * inverse
    flat = band_rows * lon

    def whole(ref):
        return ref[...].reshape(flat, ref.shape[2])

    g3 = dot(whole(a2), whole(cot_ref), 0, 0).astype(BF16)
    g2 = dot(whole(a1), whole(p2), 0, 0).astype(BF16)
    g1 = dot(whole(smooth), whole(p1), 0, 0).astype(BF16)
    for row in range(2):
        up_ref[row] = scaled_ref[row].astype(BF16)
        down_ref[row] = scaled_ref[band_rows - 2 + row].astype(BF16)
    grads_ref[:ch] = g1[:, :ch]
    grads_ref[ch : 2 * ch] = g1[:, ch:]
    grads_ref[2 * ch : 4 * ch] = g2[:, :ch]
    grads_ref[4 * ch : 6 * ch] = g2[:, ch:]
    grads_ref[6 * ch : 8 * ch] = g3
    rest = grads_ref.shape[0] - 8 * ch
    row_at = lax.broadcasted_iota(jnp.int32, (rest, ch), 0)
    tail = jnp.zeros((rest, ch), F32)
    for index, line in enumerate((gb1[:, :ch], gb1[:, ch:], gb2[:, :ch], gb2[:, ch:])):
        tail = jnp.where(row_at == index, line, tail)
    grads_ref[8 * ch :] = tail.astype(BF16)


def adjoint_kernel(
    offsets,
    scaled_ref,
    after_ref,
    before_ref,
    place_ref,
    table_ref,
    *refs,
):
    outs, (once, spread, hit) = refs[:offsets], refs[offsets:]
    band_rows, lon, ch = scaled_ref.shape
    quads, wide = outs[0].shape
    taps = wide // ch
    helm, inverse = coefficients(table_ref, TABLE_AT, ch)
    first = jnp.where(place_ref[0] == 0, 0.0, 1.0)
    last = jnp.where(place_ref[0] == place_ref[1] - 1, 0.0, 1.0)
    weights = table_ref[:TABLE_AT].T
    quad_lanes = table_ref[TABLE_AT : TABLE_AT + 8].astype(jnp.int32)
    quad_at = lax.broadcasted_iota(jnp.int32, (offsets * quads, lon), 0)
    for row in range(band_rows):
        hit[:, row * lon : (row + 1) * lon] = one_hot(quad_at == quad_lanes[row : row + 1])

    def scaled(row):
        if row < 0:
            return before_ref[row + 2].astype(F32) * first
        if row >= band_rows:
            return after_ref[row - band_rows].astype(F32) * last
        return scaled_ref[row]

    for row in range(-1, band_rows + 1):
        value = (helm * inverse) * (scaled(row - 1) + scaled(row + 1) + lon_sum(scaled(row)))
        if row < 0:
            value = value * first
        if row >= band_rows:
            value = value * last
        once[row + 1] = value
    for row in range(band_rows):
        value = (
            scaled_ref[row]
            + once[row + 1]
            + helm * (once[row] + once[row + 2] + lon_sum(once[row + 1]))
        )
        for tap in range(taps):
            at = tap * band_rows + row
            spread[row * lon : (row + 1) * lon, tap * ch : (tap + 1) * ch] = (
                weights[:, at : at + 1] * value
            ).astype(BF16)
    slot_grads = dot(hit[...], spread[...]).astype(BF16)
    for offset in range(offsets):
        outs[offset][...] = slot_grads[offset * quads : (offset + 1) * quads]


def scatter_kernel(offsets, order, cells_ref, count_ref, *refs):
    blocks = dict(zip(order, refs[:offsets]))
    out_ref, done_ref, table, hit = refs[offsets:]
    done_ref[...] = jnp.zeros_like(done_ref)
    band_rows, lon, ch = out_ref.shape
    quads = refs[0].shape[0]
    box_at = lax.broadcasted_iota(jnp.int32, ((band_rows - 1) * lon, quads), 0)
    for offset in range(offsets):
        table[offset * quads : (offset + 1) * quads] = jnp.where(
            live_quads(count_ref, offset, quads), blocks[offset][...].astype(F32), 0.0
        ).astype(BF16)
        hit[:, offset * quads : (offset + 1) * quads] = one_hot(
            box_at == cells_ref[offset : offset + 1]
        )
    for row in range(band_rows):
        here = jnp.zeros((lon, ch), F32)
        right = jnp.zeros((lon, ch), F32)
        if row < band_rows - 1:
            both = dot(hit[row * lon : (row + 1) * lon], table[:, : 2 * ch])
            here = here + both[:, :ch]
            right = right + both[:, ch:]
        if row > 0:
            both = dot(hit[(row - 1) * lon : row * lon], table[:, 2 * ch :])
            here = here + both[:, :ch]
            right = right + both[:, ch:]
        out_ref[row] = here + pltpu.roll(right, 1, 0)


def sum_kernel(copies, parts_ref, ahead_ref, out_ref):
    total = parts_ref[0].astype(F32)
    for part in range(1, parts_ref.shape[0]):
        total = total + parts_ref[part].astype(F32)
    total = total.astype(BF16)
    for copy in range(copies):
        out_ref[copy] = total


def unpack_kernel(sums_ref, ahead_ref, g1, gb1, g2, gb2, g3):
    ch, hid = g1.shape
    g1[:, :ch] = sums_ref[:ch].astype(F32)
    g1[:, ch:] = sums_ref[ch : 2 * ch].astype(F32)
    g2[:, :ch] = sums_ref[2 * ch : 4 * ch].astype(F32)
    g2[:, ch:] = sums_ref[4 * ch : 6 * ch].astype(F32)
    g3[...] = sums_ref[6 * ch : 8 * ch].astype(F32)
    tail = sums_ref[8 * ch : 8 * ch + 8].astype(F32)
    gb1[:, :ch], gb1[:, ch:] = tail[0:1], tail[1:2]
    gb2[:, :ch], gb2[:, ch:] = tail[2:3], tail[3:4]


def shifted(block, by, count):
    return lax.ppermute(block, SPACE, [(i, (i + by) % count) for i in range(count)])


def body(
    field,
    send_rows,
    send_count,
    dep_slot,
    dep_weight,
    helm_coef,
    w_first,
    b_first,
    w_second,
    b_second,
    w_third,
    cotangent,
):
    _, band_rows, lon, ch = field.shape
    hid = w_first.shape[1]
    offsets, slots = send_rows.shape[1:]
    taps = dep_slot.shape[0]
    reach = (offsets - 1) // 2
    quads = slots // 4
    bands = lax.axis_size(SPACE)
    shape = jax.ShapeDtypeStruct
    place = jnp.stack([lax.axis_index(SPACE).astype(jnp.int32), jnp.int32(bands)])
    block = shape((quads, taps * ch), BF16)
    edge = shape((2, lon, ch), BF16)

    cells, select = call(
        choose_kernel,
        [
            shape((8, quads), jnp.int32),
            shape((offsets * quads, (band_rows - 1) * lon), BF16),
        ],
        [VMEM],
        [pltpu.VMEM((8, slots), jnp.int32)],
        flops=CHOOSE_COST,
        name="choose",
    )(jnp.transpose(send_rows, (1, 0, 2)))
    packed = call(
        functools.partial(pack_kernel, offsets),
        [block] * offsets,
        [VMEM] * 3,
        [pltpu.VMEM((band_rows * lon, 2 * ch), BF16)],
        name="pack",
    )(field[0], select, send_count)
    received = [
        packed[e] if e == reach else shifted(packed[e], e - reach, bands)
        for e in range(offsets)
    ]
    order = sorted(range(offsets), key=lambda e: (-abs(e - reach), abs(e - reach) * (e - reach) * (2 * abs(e - reach) - 3)))
    (table,) = call(
        prepare_kernel,
        [shape((TABLE_AT + 16, lon), F32)],
        [VMEM] * 5,
        flops=PREPARE_COST,
        name="prepare",
    )(
        dep_slot,
        dep_weight,
        helm_coef.reshape(1, ch),
        b_first.reshape(1, hid),
        b_second.reshape(1, hid),
    )
    departure, up, down = call(
        functools.partial(interp_kernel, offsets, order),
        [shape((band_rows, lon, ch), F32), edge, edge],
        [VMEM] * (offsets + 1),
        [pltpu.VMEM((offsets * quads, taps * ch), BF16)],
        name="interp",
    )(*(received[e] for e in order), table)
    after = shifted(up, -1, bands)
    before = shifted(down, 1, bands)
    groups = ("y", "x", "core")
    group = lax.axis_size(groups)
    depth = lax.axis_size("z")
    next_state, scaled, up, down, grads = call(
        mlp_kernel,
        [
            shape((band_rows, lon, ch), BF16),
            shape((band_rows, lon, ch), F32),
            edge,
            edge,
            shape((group * PART_ROWS, ch), BF16),
        ],
        [VMEM] * 4 + [SMEM] + [VMEM] * 4,
        [
            pltpu.VMEM((1, hid), F32),
            pltpu.VMEM((1, hid), F32),
            pltpu.VMEM((band_rows + 2, lon, ch), F32),
            pltpu.VMEM((band_rows, lon, ch), BF16),
        ]
        + [pltpu.VMEM((band_rows, lon, hid), BF16)] * 4,
        name="smooth_mlp",
    )(departure, after, before, cotangent[0], place, table, w_first, w_second, w_third)
    after = shifted(up, -1, bands)
    before = shifted(down, 1, bands)

    parts = lax.all_to_all(grads.reshape(group, PART_ROWS, ch), groups, 0, 0)
    slot_grads = call(
        functools.partial(adjoint_kernel, offsets),
        [block] * offsets,
        [VMEM] * 3 + [SMEM, VMEM],
        [
            pltpu.VMEM((band_rows + 2, lon, ch), F32),
            pltpu.VMEM((band_rows * lon, taps * ch), BF16),
            pltpu.VMEM((offsets * quads, band_rows * lon), BF16),
        ],
        flops=ADJOINT_COST,
        name="adjoint",
    )(scaled, after, before, place, table)
    (part_sum,) = call(
        functools.partial(sum_kernel, depth),
        [shape((depth, PART_ROWS, ch), BF16)],
        [VMEM, ANY],
        flops=PART_COST,
        name="part_sum",
    )(parts, slot_grads[reach])
    parts = lax.all_to_all(part_sum, "z", 0, 0)
    back = [
        slot_grads[e] if e == reach else shifted(slot_grads[e], reach - e, bands)
        for e in range(offsets)
    ]
    field_grad, done = call(
        functools.partial(scatter_kernel, offsets, range(offsets)),
        [shape((band_rows, lon, ch), F32), shape((8, ch), F32)],
        [VMEM] * (offsets + 2),
        [
            pltpu.VMEM((offsets * quads, taps * ch), BF16),
            pltpu.VMEM(((band_rows - 1) * lon, offsets * quads), BF16),
        ],
        flops=SCATTER_COST,
        name="scatter",
    )(cells, send_count, *back)
    (whole_sum,) = call(
        functools.partial(sum_kernel, group),
        [shape((group, PART_ROWS, ch), BF16)],
        [VMEM, ANY],
        name="whole_sum",
    )(parts, slot_grads[reach])
    sums = lax.all_to_all(whole_sum, groups, 0, 0).reshape(group * PART_ROWS, ch)
    grad_shapes = [
        shape((ch, hid), F32),
        shape((1, hid), F32),
        shape((hid, hid), F32),
        shape((1, hid), F32),
        shape((hid, ch), F32),
    ]
    grads = call(
        unpack_kernel,
        grad_shapes,
        [VMEM, ANY],
        name="unpack",
    )(sums, done)
    return (
        next_state[None],
        field_grad[None],
        grads[0],
        grads[1].reshape(hid),
        grads[2],
        grads[3].reshape(hid),
        grads[4],
    )


def solution(mesh):
    fine = Mesh(mesh.devices.reshape(4, 8, 4, 2), ("y",) + SPACE)
    state = P("y", SPACE, None, None)
    return jax.shard_map(
        body,
        mesh=fine,
        in_specs=(
            state,
            P(SPACE, None, None),
            P(SPACE, None),
            P(None, SPACE, None),
            P(None, SPACE, None),
            P(),
            P(),
            P(),
            P(),
            P(),
            P(),
            state,
        ),
        out_specs=(state, state, P(), P(), P(), P(), P()),
        check_vma=False,
    )
```
